32 devices in a mesh: dp: 16 (over z, x, core), seq: 2 (over y).
Axes of the slice: x: 2, y: 2, z: 4, core: 2. Of those that a mesh axis runs over, the one named last changes fastest.
Arguments:
- tokens: bfloat16 [32, 1024, 768], P('dp', 'seq'), may hold values from -6 to 6
- first_values: bfloat16 [32, 1024, 384], P('dp', 'seq'), may hold values from -6 to 6
- cotangent: bfloat16 [32, 1024, 768], P('dp', 'seq'), may hold values from -6 to 6
- lengths: int32 [32], P('dp'), may hold values from 256 to 1024, as said below
- qkv_master: float32 [768, 1920], P(('dp', 'seq')), may hold values from -0.21875 to 0.21875
- qkv_moment: float32 [768, 1920], P(('dp', 'seq')), may hold values from -112 to 112
- qkv_average: float32 [768, 1920], P(('dp', 'seq')), may hold values from -0.21875 to 0.21875
- out_master: float32 [768, 768], P(('dp', 'seq')), may hold values from -1.75 to 1.75
- out_moment: float32 [768, 768], P(('dp', 'seq')), may hold values from -224 to 224
- out_average: float32 [768, 768], P(('dp', 'seq')), may hold values from -1.75 to 1.75
- up_master: float32 [768, 3072], P(('dp', 'seq')), may hold values from -0.21875 to 0.21875
- up_moment: float32 [768, 3072], P(('dp', 'seq')), may hold values from -448 to 448
- up_average: float32 [768, 3072], P(('dp', 'seq')), may hold values from -0.21875 to 0.21875
- down_master: float32 [3072, 768], P(('dp', 'seq')), may hold values from -0.109375 to 0.109375
- down_moment: float32 [3072, 768], P(('dp', 'seq')), may hold values from -448 to 448
- down_average: float32 [3072, 768], P(('dp', 'seq')), may hold values from -0.109375 to 0.109375
- norm_master: float32 [768, 4], P(('dp', 'seq')), may hold values from -0.5 to 1.4, as said below
- norm_moment: float32 [768, 4], P(('dp', 'seq')), may hold values from -512 to 512
- norm_average: float32 [768, 4], P(('dp', 'seq')), may hold values from -6 to 6
Outputs:
- mixed: bfloat16 [32, 1024, 768], P('dp', 'seq')
- tokens_grad: bfloat16 [32, 1024, 768], P('dp', 'seq')
- first_values_grad: bfloat16 [32, 1024, 384], P('dp', 'seq')
- qkv_moment_new: float32 [768, 1920], P(('dp', 'seq'))
- qkv_master_new: float32 [768, 1920], P(('dp', 'seq'))
- qkv_average_new: float32 [768, 1920], P(('dp', 'seq'))
- out_moment_new: float32 [768, 768], P(('dp', 'seq'))
- out_master_new: float32 [768, 768], P(('dp', 'seq'))
- out_average_new: float32 [768, 768], P(('dp', 'seq'))
- up_moment_new: float32 [768, 3072], P(('dp', 'seq'))
- up_master_new: float32 [768, 3072], P(('dp', 'seq'))
- up_average_new: float32 [768, 3072], P(('dp', 'seq'))
- down_moment_new: float32 [3072, 768], P(('dp', 'seq'))
- down_master_new: float32 [3072, 768], P(('dp', 'seq'))
- down_average_new: float32 [3072, 768], P(('dp', 'seq'))
- norm_moment_new: float32 [768, 4], P(('dp', 'seq'))
- norm_master_new: float32 [768, 4], P(('dp', 'seq'))
- norm_average_new: float32 [768, 4], P(('dp', 'seq'))
The draws below stay inside these ranges and needn't reach their ends.
Inputs may be any that keep to these rules, and one draw needn't show every extreme that they name: `lengths`: in every draw some sequence has all 1024 positions. `norm_master`: columns 0 and 2 are gains, columns 1 and 3 shifts.
All inputs are finite; a program needn't handle non-finite values.
Results may differ from the reference program's by a relative error of at most 0.012.
Values may be sent and summed in bfloat16 or wider, within the bound.
No kernel may reach another device: no remote copies, remote signals or barrier semaphores. Data moves between devices by JAX's collectives and lax.ppermute only.
A program may use at most 192 MiB of HBM per device.

```python
import jax
import jax.numpy as jnp
from jax import lax

D = 768
HEAD_DIM = 64
FF = 3072
SEQ_LEN = 1024
SEQS = 32


def draw_lengths(key, part):
    key = jax.random.fold_in(key, 11)
    draw_key, pick_key = jax.random.split(key)
    lengths_drawn = jax.random.randint(draw_key, (SEQS,), SEQ_LEN // 4, SEQ_LEN + 1)
    chosen = jax.random.randint(pick_key, (), 0, SEQS)
    return jnp.where(jnp.arange(SEQS) == chosen, SEQ_LEN, lengths_drawn).astype(jnp.int32)


def draw_norm_master(key, part):
    key = jax.random.fold_in(key, 12)
    gain_key, shift_key = jax.random.split(key)
    gain_values = jax.random.uniform(gain_key, (D, 4), jnp.float32, 0.6, 1.4)
    shift_values = jax.random.uniform(shift_key, (D, 4), jnp.float32, -0.5, 0.5)
    column_index = jnp.arange(4)[None, :] % 2
    return jnp.where(column_index == 0, gain_values, shift_values)


def levels(own_key, extent, pieces, low, high):
    def one(dim, shards_of):
        draws = jax.random.uniform(jax.random.fold_in(jax.random.fold_in(own_key, 6), dim), (shards_of,), jnp.float32, low / len(pieces), high / len(pieces))
        return jnp.repeat(jnp.exp(draws), extent[dim] // shards_of).reshape((-1,) + (1,) * (len(extent) - dim - 1))

    loudness = one(*pieces[0])
    for cut in pieces[1:]:
        loudness = loudness * one(*cut)
    return loudness


def normal_values(key, dims, width, bound, cuts=(), dtype=jnp.bfloat16):
    result = width * jax.random.normal(key, dims, jnp.float32)
    if cuts:
        result = result * levels(key, dims, cuts, -0.22, 0.18)
    return jnp.clip(result, -bound, bound).astype(dtype)


def setup_inputs(seed: int = 0) -> dict:
    key_list = jax.random.split(jax.random.key(seed), 20)
    tokens = normal_values(key_list[0], (SEQS, SEQ_LEN, D), 1.0, 6.0, ((0, 16), (1, 2)))
    first_values = normal_values(key_list[1], (SEQS, SEQ_LEN, D // 2), 1.0, 6.0, ((0, 16), (1, 2)))
    cotangent = normal_values(key_list[2], (SEQS, SEQ_LEN, D), 1.0, 6.0, ((0, 16), (1, 2)))
    lengths = draw_lengths(jax.random.fold_in(key_list[19], 71), 0)
    qkv_master = normal_values(key_list[4], (D, 5 * D // 2), D ** -0.5, 0.21875, ((0, 32),), jnp.float32)
    qkv_moment = normal_values(key_list[5], (D, 5 * D // 2), (0.1 * (SEQS * SEQ_LEN) ** 0.5), 112.0, ((0, 32),), jnp.float32)
    qkv_average = normal_values(key_list[6], (D, 5 * D // 2), D ** -0.5, 0.21875, ((0, 32),), jnp.float32)
    out_master = normal_values(key_list[7], (D, D), (D // 64) ** -0.5, 1.75, ((0, 32),), jnp.float32)
    out_moment = normal_values(key_list[8], (D, D), (0.2 * (SEQS * SEQ_LEN) ** 0.5), 224.0, ((0, 32),), jnp.float32)
    out_average = normal_values(key_list[9], (D, D), (D // 64) ** -0.5, 1.75, ((0, 32),), jnp.float32)
    up_master = normal_values(key_list[10], (D, FF), D ** -0.5, 0.21875, ((0, 32),), jnp.float32)
    up_moment = normal_values(key_list[11], (D, FF), (0.4 * (SEQS * SEQ_LEN) ** 0.5), 448.0, ((0, 32),), jnp.float32)
    up_average = normal_values(key_list[12], (D, FF), D ** -0.5, 0.21875, ((0, 32),), jnp.float32)
    down_master = normal_values(key_list[13], (FF, D), FF ** -0.5, 0.109375, ((0, 32),), jnp.float32)
    down_moment = normal_values(key_list[14], (FF, D), (0.4 * (SEQS * SEQ_LEN) ** 0.5), 448.0, ((0, 32),), jnp.float32)
    down_average = normal_values(key_list[15], (FF, D), FF ** -0.5, 0.109375, ((0, 32),), jnp.float32)
    norm_master = draw_norm_master(jax.random.fold_in(key_list[19], 71), 0)
    norm_moment = normal_values(key_list[17], (D, 4), (0.5 * (SEQS * SEQ_LEN) ** 0.5), 512.0, ((0, 32),), jnp.float32)
    norm_average = normal_values(key_list[18], (D, 4), 0.5, 6.0, ((0, 32),), jnp.float32)
    return {"tokens": tokens, "first_values": first_values, "cotangent": cotangent, "lengths": lengths, "qkv_master": qkv_master, "qkv_moment": qkv_moment, "qkv_average": qkv_average, "out_master": out_master, "out_moment": out_moment, "out_average": out_average, "up_master": up_master, "up_moment": up_moment, "up_average": up_average, "down_master": down_master, "down_moment": down_moment, "down_average": down_average, "norm_master": norm_master, "norm_moment": norm_moment, "norm_average": norm_average}


EPSILON = 1e-05
MOMENTUM = 0.5
AVERAGING = 0.5
RATE = 0.0006
HIGHEST = lax.Precision.HIGHEST

@jax.custom_vjp
def low(v):
    return lax.optimization_barrier(v.astype(jnp.bfloat16)).astype(jnp.float32)

@jax.custom_vjp
def low_back(v):
    return v

def low_keep(v):
    return (low(v), None)

def low_pass(kept, grad):
    return (grad,)

def back_keep(v):
    return (v, None)

def back_low(kept, grad):
    return (low(grad),)
low.defvjp(low_keep, low_pass)
low_back.defvjp(back_keep, back_low)

def rounded(value):
    return low(low_back(value))

def layer_norm(values, gain, shift):
    center = values - lax.optimization_barrier(jnp.mean(values, -1, keepdims=True))
    spread = lax.optimization_barrier(jnp.mean(center * center, -1, keepdims=True))
    return center * lax.rsqrt(spread + EPSILON) * gain + shift

def attention(queries, keys, values):
    length = queries.shape[0]
    head_count = queries.shape[1] // HEAD_DIM
    query_heads = queries.reshape(length, head_count, HEAD_DIM)
    key_heads = keys.reshape(length, head_count, HEAD_DIM)
    value_heads = values.reshape(length, head_count, HEAD_DIM)
    block_rows = min(512, length)
    columns = jnp.arange(length).astype(jnp.int32)
    score_scale = HEAD_DIM ** (-0.5)

    def one_block(start):
        query_block = lax.dynamic_slice_in_dim(query_heads, start, block_rows, 0)
        scores = jnp.einsum('qhd,khd->hqk', query_block, key_heads, precision=HIGHEST) * score_scale
        scores = low_back(scores)
        row_index = start + jnp.arange(block_rows).astype(jnp.int32)
        visible = row_index[:, None] >= columns[None, :]
        scores = jnp.where(visible[None], scores, -1e+30)
        maximum = lax.optimization_barrier(jnp.max(scores, -1, keepdims=True))
        weights = jnp.exp(scores - maximum)
        probs = low(weights / lax.optimization_barrier(jnp.sum(weights, -1, keepdims=True)))
        return jnp.einsum('hqk,khd->qhd', probs, value_heads, precision=HIGHEST)
    starts = (jnp.arange(length // block_rows) * block_rows).astype(jnp.int32)
    outputs = lax.map(jax.checkpoint(one_block), starts)
    return outputs.reshape(length, head_count * HEAD_DIM)

def layer(rows, firsts, w_qkv, w_out, w_up, w_down, norms):
    normed_one = low(layer_norm(rows, norms[:, 0], norms[:, 1]))
    projected = jnp.dot(normed_one, w_qkv, precision=HIGHEST)
    queries = rounded(projected[:, :D])
    keys = rounded(projected[:, D:2 * D])
    values = rounded(jnp.concatenate([projected[:, 2 * D:], firsts], 1))
    attended = rounded(attention(queries, keys, values))
    mid_rows = rows + low_back(jnp.dot(attended, w_out, precision=HIGHEST))
    normed_two = low(layer_norm(mid_rows, norms[:, 2], norms[:, 3]))
    hidden_pre = low_back(jnp.dot(normed_two, w_up, precision=HIGHEST))
    hidden = low(jax.nn.gelu(hidden_pre, approximate=True))
    return mid_rows + jnp.dot(hidden, w_down, precision=HIGHEST)

def update(gradient, moment, master, average):
    moment_new = MOMENTUM * moment + gradient
    master_new = master - RATE * (gradient + MOMENTUM * moment_new)
    average_new = AVERAGING * average + (1.0 - AVERAGING) * master_new
    return (moment_new, master_new, average_new)

def reference(tokens, first_values, cotangent, lengths, qkv_master, qkv_moment, qkv_average, out_master, out_moment, out_average, up_master, up_moment, up_average, down_master, down_moment, down_average, norm_master, norm_moment, norm_average):
    masters = (qkv_master, out_master, up_master, down_master, norm_master)
    working = tuple((low(master) for master in masters))
    positions = jnp.arange(SEQ_LEN).astype(jnp.int32)

    def seq_step(totals, items):
        rows, firsts, cot_rows, length_now = items
        keep_mask = (positions < length_now).astype(jnp.float32)[:, None]
        output, pull = jax.vjp(layer, rows.astype(jnp.float32), firsts.astype(jnp.float32), working[0], working[1], working[2], working[3], working[4])
        gradients = pull(cot_rows.astype(jnp.float32) * keep_mask)
        totals = tuple((total + grad for total, grad in zip(totals, gradients[2:])))
        return (totals, (output.astype(jnp.bfloat16), gradients[0].astype(jnp.bfloat16), gradients[1].astype(jnp.bfloat16)))
    zeros = tuple((jnp.zeros(w.shape, jnp.float32) for w in working))
    totals, (mixed, tokens_grad, firsts_grad) = lax.scan(seq_step, zeros, (tokens, first_values, cotangent, lengths))
    qkv_new = update(totals[0], qkv_moment, qkv_master, qkv_average)
    out_new = update(totals[1], out_moment, out_master, out_average)
    up_new = update(totals[2], up_moment, up_master, up_average)
    down_new = update(totals[3], down_moment, down_master, down_average)
    norm_new = update(totals[4], norm_moment, norm_master, norm_average)
    return (mixed, tokens_grad, firsts_grad, qkv_new[0], qkv_new[1], qkv_new[2], out_new[0], out_new[1], out_new[2], up_new[0], up_new[1], up_new[2], down_new[0], down_new[1], down_new[2], norm_new[0], norm_new[1], norm_new[2])
```

```python
import functools

import jax
import jax.numpy as jnp
from jax import lax
from jax.experimental import pallas as pl
from jax.experimental.pallas import tpu as pltpu
from jax.sharding import PartitionSpec as P

HEAD_DIM = 64
LANES = 128
EPSILON = 1e-05
MOMENTUM = 0.5
AVERAGING = 0.5
RATE = 0.0006
SCALE = HEAD_DIM ** (-0.5)
VMEM_BYTES = 48 << 20

BF16 = jnp.bfloat16
F32 = jnp.float32


def times_transposed(left, right):
    return lax.dot_general(left, right, (((1,), (1,)), ((), ())), preferred_element_type=F32)


def times(left, right):
    return lax.dot_general(left, right, (((1,), (0,)), ((), ())), preferred_element_type=F32)


def contract_rows(left, right):
    return lax.dot_general(left, right, (((0,), (0,)), ((), ())), preferred_element_type=F32)


def attend_forward_kernel(
    tile, fresh_pairs, q_ref, k_ref, fresh_ref, reused_ref, out_ref, totals_ref
):
    length = q_ref.shape[0]
    first = lax.broadcasted_iota(jnp.int32, (1, LANES), 1) < HEAD_DIM
    values = jnp.where(pl.program_id(1) < fresh_pairs, fresh_ref[...], reused_ref[...])
    row = lax.broadcasted_iota(jnp.int32, (tile, tile), 0)
    column = lax.broadcasted_iota(jnp.int32, (tile, tile), 1)
    for block in range(length // tile):
        start, stop = block * tile, (block + 1) * tile
        queries = q_ref[start:stop, :] * jnp.asarray(SCALE, BF16)
        outputs, totals = [], []
        for own in (first, ~first):
            scores = times_transposed(
                jnp.where(own, queries, jnp.zeros((), BF16)), k_ref[:stop, :]
            )
            diagonal = jnp.where(row >= column, scores[:, start:], -1e30)
            scores = (
                diagonal if block == 0 else jnp.concatenate([scores[:, :start], diagonal], 1)
            )
            maximum = jnp.max(scores, 1, keepdims=True)
            weights = jnp.exp(scores - maximum)
            summed = jnp.sum(weights, 1, keepdims=True)
            outputs.append(times(weights.astype(BF16), values[:stop, :]) * (1.0 / summed))
            totals.append(maximum + jnp.log(summed))
        out_ref[start:stop, :] = jnp.where(first, outputs[0], outputs[1]).astype(BF16)
        turned = jnp.where(first, totals[0], totals[1]).T
        totals_ref[0:1, start:stop] = turned[0:1, :]
        totals_ref[1:2, start:stop] = turned[HEAD_DIM : HEAD_DIM + 1, :]


def attend_backward_kernel(
    tile,
    fresh_pairs,
    q_ref,
    k_ref,
    fresh_ref,
    reused_ref,
    out_ref,
    grad_ref,
    totals_ref,
    grad_q_ref,
    grad_k_ref,
    grad_v_ref,
    sum_q_ref,
):
    length = q_ref.shape[0]
    first = lax.broadcasted_iota(jnp.int32, (1, LANES), 1) < HEAD_DIM
    values = jnp.where(pl.program_id(1) < fresh_pairs, fresh_ref[...], reused_ref[...])
    head_of_lane = lax.broadcasted_iota(jnp.int32, (8, LANES), 1) // HEAD_DIM
    pick = jnp.where(
        head_of_lane == lax.broadcasted_iota(jnp.int32, (8, LANES), 0), 1.0, 0.0
    ).astype(BF16)
    product = out_ref[...].astype(F32) * grad_ref[...].astype(F32)
    coarse = product.astype(BF16)
    fine = (product - coarse.astype(F32)).astype(BF16)
    inner = times_transposed(pick, coarse) + times_transposed(pick, fine)
    row = lax.broadcasted_iota(jnp.int32, (tile, tile), 0)
    column = lax.broadcasted_iota(jnp.int32, (tile, tile), 1)
    for start in range(0, length, tile):
        stop = start + tile
        keys = k_ref[start:stop, :] * jnp.asarray(SCALE, BF16)
        own_values = values[start:stop, :]
        queries, grads = q_ref[start:, :], grad_ref[start:, :]
        grad_keys, grad_values = [], []
        for head, own in enumerate((first, ~first)):
            own_keys = jnp.where(own, keys, jnp.zeros((), BF16))
            scores = times_transposed(own_keys, queries)
            probs = jnp.exp(scores - totals_ref[head : head + 1, start:])
            diagonal = jnp.where(column >= row, probs[:, :tile], 0.0)
            probs = (
                diagonal if stop == length else jnp.concatenate([diagonal, probs[:, tile:]], 1)
            )
            grad_probs = times_transposed(
                jnp.where(own, own_values, jnp.zeros((), BF16)), grads
            )
            grad_scores = (probs * (grad_probs - inner[head : head + 1, start:])).astype(BF16)
            grad_values.append(times(probs.astype(BF16), grads))
            grad_keys.append(times(grad_scores, queries))
            part = contract_rows(grad_scores, own_keys)
            if start == 0 and head == 0:
                sum_q_ref[...] = part
            else:
                sum_q_ref[start:, :] += part
        grad_k_ref[start:stop, :] = (
            jnp.where(first, grad_keys[0], grad_keys[1]) * SCALE
        ).astype(BF16)
        grad_v_ref[start:stop, :] = jnp.where(first, grad_values[0], grad_values[1]).astype(BF16)
    grad_q_ref[...] = sum_q_ref[...].astype(BF16)


def head_specs(length, pairs):
    fresh_pairs = pairs // 2
    return [
        pl.BlockSpec((length, LANES), lambda s, p: (s, p)),
        pl.BlockSpec((length, LANES), lambda s, p: (s, pairs + p)),
        pl.BlockSpec(
            (length, LANES), lambda s, p: (s, 2 * pairs + jnp.minimum(p, fresh_pairs - 1))
        ),
        pl.BlockSpec((length, LANES), lambda s, p: (s, jnp.maximum(p - fresh_pairs, 0))),
    ]


def attend_forward(projected, reused, length, width):
    count, pairs = projected.shape[0] // length, width // LANES
    area = count * length * length * width
    return pl.pallas_call(
        functools.partial(attend_forward_kernel, min(512, length), pairs // 2),
        grid=(count, pairs),
        in_specs=head_specs(length, pairs),
        out_specs=[
            pl.BlockSpec((length, LANES), lambda s, p: (s, p)),
            pl.BlockSpec((None, None, 2, length), lambda s, p: (s, p, 0, 0)),
        ],
        out_shape=[
            jax.ShapeDtypeStruct((count * length, width), BF16),
            jax.ShapeDtypeStruct((count, pairs, 2, length), F32),
        ],
        compiler_params=pltpu.CompilerParams(vmem_limit_bytes=VMEM_BYTES),
        cost_estimate=pl.CostEstimate(
            flops=12 * area,
            bytes_accessed=8 * count * length * width,
            transcendentals=area // HEAD_DIM,
        ),
        name="attend_forward",
    )(projected, projected, projected, reused)


def attend_backward(projected, reused, attended, grads, totals, length, width):
    count, pairs = projected.shape[0] // length, width // LANES
    area = count * length * length * width
    columns = pl.BlockSpec((length, LANES), lambda s, p: (s, p))
    return pl.pallas_call(
        functools.partial(attend_backward_kernel, min(256, length), pairs // 2),
        grid=(count, pairs),
        in_specs=head_specs(length, pairs)
        + [
            columns,
            columns,
            pl.BlockSpec((None, None, 2, length), lambda s, p: (s, p, 0, 0)),
        ],
        out_specs=[columns] * 3,
        out_shape=[jax.ShapeDtypeStruct((count * length, width), BF16)] * 3,
        scratch_shapes=[pltpu.VMEM((length, LANES), F32)],
        compiler_params=pltpu.CompilerParams(vmem_limit_bytes=VMEM_BYTES),
        cost_estimate=pl.CostEstimate(
            flops=24 * area,
            bytes_accessed=16 * count * length * width,
            transcendentals=area // HEAD_DIM,
        ),
        name="attend_backward",
    )(projected, projected, projected, reused, attended, grads, totals)


class Grid:
    def __init__(self, mesh):
        dp, self.halves = mesh.shape["dp"], mesh.shape["seq"]
        assert self.halves == 2 and dp & (dp - 1) == 0
        self.dp = dp
        self.dp_bits = dp.bit_length() - 1
        self.bits = self.dp_bits + 1
        core, near = self.dp_bits - 1, self.dp_bits - 2
        seq = self.dp_bits
        far = list(range(self.dp_bits - 2))
        self.orders = (far + [near, seq, core], far + [seq, near, core])

    def bit(self, which):
        if which == self.dp_bits:
            return lax.axis_index("seq")
        return (lax.axis_index("dp") >> (self.dp_bits - 1 - which)) & 1

    def swap(self, array, which):
        if which == self.dp_bits:
            return lax.ppermute(array, "seq", [(0, 1), (1, 0)])
        mask = 1 << (self.dp_bits - 1 - which)
        return lax.ppermute(array, "dp", [(i, i ^ mask) for i in range(self.dp)])

    def gather(self, shard, order):
        done, whole = [], shard
        for which in order:
            other = self.swap(whole, which)
            place = sum(1 for d in done if d < which)
            low = self.bit(which) == 0
            whole = jnp.stack(
                [jnp.where(low, whole, other), jnp.where(low, other, whole)], place
            )
            done.append(which)
        return whole.reshape(-1, shard.shape[-1])

    def scatter_sum(self, partial, order):
        rows, columns = partial.shape
        whole = partial.reshape((2,) * self.bits + (rows >> self.bits, columns))
        left = list(range(self.bits))
        for which in reversed(order):
            place = left.index(which)
            bit = self.bit(which)
            away = lax.dynamic_index_in_dim(whole, 1 - bit, place, keepdims=False)
            keep = lax.dynamic_index_in_dim(whole, bit, place, keepdims=False)
            left.remove(which)
            whole = keep.astype(F32) + self.swap(away, which).astype(F32)
            if left:
                whole = whole.astype(BF16)
        return whole

    def to_whole(self, array):
        count, half, width = array.shape
        seq = lax.axis_index("seq")
        split = array.reshape(2, count // 2, half, width)
        keep = lax.dynamic_index_in_dim(split, seq, 0, keepdims=False)
        other = self.swap(
            lax.dynamic_index_in_dim(split, 1 - seq, 0, keepdims=False), self.dp_bits
        )
        low = seq == 0
        return jnp.stack(
            [jnp.where(low, keep, other), jnp.where(low, other, keep)], 1
        ).reshape(count * half, width)

    def to_halves(self, array, half):
        width = array.shape[-1]
        seq = lax.axis_index("seq")
        split = array.reshape(-1, 2, half, width)
        keep = lax.dynamic_index_in_dim(split, seq, 1, keepdims=False)
        other = self.swap(
            lax.dynamic_index_in_dim(split, 1 - seq, 1, keepdims=False), self.dp_bits
        )
        low = seq == 0
        return jnp.concatenate([jnp.where(low, keep, other), jnp.where(low, other, keep)], 0)


def normalize(values):
    center = values - jnp.mean(values, -1, keepdims=True)
    spread = jnp.mean(center * center, -1, keepdims=True)
    inverse = lax.rsqrt(spread + EPSILON)
    return center * inverse, inverse


def normalize_back(grad, unit, inverse, gain):
    scaled = grad * gain
    along = jnp.mean(scaled * unit, -1, keepdims=True)
    level = jnp.mean(scaled, -1, keepdims=True)
    return inverse * (scaled - level - unit * along)


def gelu_tanh(values):
    return jax.nn.gelu(values, approximate=True)


def update(gradient, moment, master, average):
    moment_new = MOMENTUM * moment + gradient
    master_new = master - RATE * (gradient + MOMENTUM * moment_new)
    average_new = AVERAGING * average + (1.0 - AVERAGING) * master_new
    return (moment_new, master_new, average_new)


def body(
    grid,
    tokens,
    first_values,
    cotangent,
    lengths,
    qkv_master,
    qkv_moment,
    qkv_average,
    out_master,
    out_moment,
    out_average,
    up_master,
    up_moment,
    up_average,
    down_master,
    down_moment,
    down_average,
    norm_master,
    norm_moment,
    norm_average,
):
    count, half, width = tokens.shape
    length = 2 * half
    order_x, order_y = grid.orders
    norm_columns = norm_master.shape[1]
    qkv_columns = qkv_master.shape[1]

    rows_in = grid.to_whole(tokens).astype(F32)
    norm_padded = jnp.pad(norm_master, ((0, 0), (0, LANES - norm_columns)))
    work = jnp.concatenate([norm_padded, qkv_master], 1).astype(BF16)
    cut = (work.shape[1] // 2) // LANES * LANES
    work = jnp.concatenate(
        [grid.gather(work[:, :cut], order_x), grid.gather(work[:, cut:], order_y)], 1
    )
    norm_param = work[:, :norm_columns].astype(F32)
    w_qkv = work[:, LANES:]
    gain_one, shift_one = norm_param[:, 0], norm_param[:, 1]
    gain_two, shift_two = norm_param[:, 2], norm_param[:, 3]
    reused = grid.to_whole(first_values)
    w_out = grid.gather(out_master.astype(BF16), order_x)
    w_up = grid.gather(up_master.astype(BF16), order_x)
    w_down = grid.gather(down_master.astype(BF16), order_y)
    whole_cotangent = grid.to_whole(cotangent)

    unit_one, inverse_one = normalize(rows_in)
    normed_one = (unit_one * gain_one + shift_one).astype(BF16)
    projected = times(normed_one, w_qkv).astype(BF16)
    attended, totals = attend_forward(projected, reused, length, width)
    mid_rows = rows_in + times(attended, w_out)
    unit_two, inverse_two = normalize(mid_rows)
    normed_two = (unit_two * gain_two + shift_two).astype(BF16)
    hidden_pre = times(normed_two, w_up)
    hidden, pull_gelu = jax.vjp(gelu_tanh, hidden_pre)
    hidden = hidden.astype(BF16)
    mixed = grid.to_halves((mid_rows + times(hidden, w_down)).astype(BF16), half)

    own_lengths = lax.dynamic_index_in_dim(
        lengths.reshape(2, count // 2), lax.axis_index("seq"), 0, keepdims=False
    )
    position = lax.iota(jnp.int32, length)
    keep_mask = (position[None, :] < own_lengths[:, None]).reshape(-1)
    grad_mixed = jnp.where(keep_mask[:, None], whole_cotangent, jnp.zeros((), BF16))
    grad_down = contract_rows(hidden, grad_mixed).astype(BF16)
    sum_down = grid.scatter_sum(grad_down, order_y)
    grad_hidden = pull_gelu(times_transposed(grad_mixed, w_down))[0].astype(BF16)
    grad_up = contract_rows(normed_two, grad_hidden).astype(BF16)
    sum_up = grid.scatter_sum(grad_up, order_x)
    grad_normed_two = times_transposed(grad_hidden, w_up)
    grad_gain_two = jnp.sum(grad_normed_two * unit_two, 0)
    grad_shift_two = jnp.sum(grad_normed_two, 0)
    grad_mid = grad_mixed.astype(F32) + normalize_back(
        grad_normed_two, unit_two, inverse_two, gain_two
    )
    grad_mid_low = grad_mid.astype(BF16)
    grad_out = contract_rows(attended, grad_mid_low).astype(BF16)
    sum_out = grid.scatter_sum(grad_out, order_x)
    grad_attended = times_transposed(grad_mid_low, w_out).astype(BF16)
    grad_q, grad_k, grad_v = attend_backward(
        projected, reused, attended, grad_attended, totals, length, width
    )
    first_grad = grid.to_halves(grad_v[:, width // 2 :], half)
    grad_columns = jnp.concatenate([grad_q, grad_k, grad_v[:, : width // 2]], 1)
    grad_normed_one = times_transposed(grad_columns, w_qkv)
    tokens_grad = grid.to_halves(
        (grad_mid + normalize_back(grad_normed_one, unit_one, inverse_one, gain_one)).astype(
            BF16
        ),
        half,
    )
    grad_norm = jnp.stack(
        [
            jnp.sum(grad_normed_one * unit_one, 0),
            jnp.sum(grad_normed_one, 0),
            grad_gain_two,
            grad_shift_two,
        ],
        1,
    )
    grad_work = jnp.concatenate(
        [
            jnp.pad(grad_norm, ((0, 0), (0, LANES - norm_columns))),
            contract_rows(normed_one, grad_columns),
        ],
        1,
    ).astype(BF16)
    sum_work = jnp.concatenate(
        [
            grid.scatter_sum(grad_work[:, :cut], order_x),
            grid.scatter_sum(grad_work[:, cut:], order_y),
        ],
        1,
    )
    sum_norm, sum_qkv = sum_work[:, :norm_columns], sum_work[:, LANES:]
    return (
        mixed,
        tokens_grad,
        first_grad,
        *update(sum_qkv, qkv_moment, qkv_master, qkv_average),
        *update(sum_out, out_moment, out_master, out_average),
        *update(sum_up, up_moment, up_master, up_average),
        *update(sum_down, down_moment, down_master, down_average),
        *update(sum_norm, norm_moment, norm_master, norm_average),
    )


def solution(mesh):
    activation = P("dp", "seq", None)
    parameter = P(("dp", "seq"), None)
    return jax.shard_map(
        functools.partial(body, Grid(mesh)),
        mesh=mesh,
        in_specs=(activation,) * 3 + (P("dp"),) + (parameter,) * 15,
        out_specs=(activation,) * 3 + (parameter,) * 15,
        check_vma=False,
    )
```

```python
import functools

import jax
import jax.numpy as jnp
from jax import lax
from jax.experimental import pallas as pl
from jax.experimental.pallas import tpu as pltpu
from jax.sharding import PartitionSpec as P

HEAD_DIM = 64
LANES = 128
EPSILON = 1e-05
MOMENTUM = 0.5
AVERAGING = 0.5
RATE = 0.0006
SCALE = HEAD_DIM ** (-0.5)
VMEM_BYTES = 24 << 20

BF16 = jnp.bfloat16
F32 = jnp.float32


def cost(flops, moved):
    return pl.CostEstimate(
        flops=int(flops) // 8, bytes_accessed=int(moved) // 8, transcendentals=0
    )


def times_transposed(left, right):
    return lax.dot_general(left, right, (((1,), (1,)), ((), ())), preferred_element_type=F32)


def times(left, right):
    return lax.dot_general(left, right, (((1,), (0,)), ((), ())), preferred_element_type=F32)


def contract_rows(left, right):
    return lax.dot_general(left, right, (((0,), (0,)), ((), ())), preferred_element_type=F32)


def attend_forward_kernel(tile, q_ref, k_ref, v_ref, out_ref, totals_ref):
    length = q_ref.shape[0]
    first = lax.broadcasted_iota(jnp.int32, (1, LANES), 1) < HEAD_DIM
    row = lax.broadcasted_iota(jnp.int32, (tile, tile), 0)
    column = lax.broadcasted_iota(jnp.int32, (tile, tile), 1)
    for block in range(length // tile):
        start, stop = block * tile, (block + 1) * tile
        queries = q_ref[start:stop, :] * jnp.asarray(SCALE, BF16)
        outputs, totals = [], []
        for own in (first, ~first):
            scores = times_transposed(
                jnp.where(own, queries, jnp.zeros((), BF16)), k_ref[:stop, :]
            )
            diagonal = jnp.where(row >= column, scores[:, start:], -1e30)
            scores = (
                diagonal if block == 0 else jnp.concatenate([scores[:, :start], diagonal], 1)
            )
            maximum = jnp.max(scores, 1, keepdims=True)
            weights = jnp.exp(scores - maximum)
            summed = jnp.sum(weights, 1, keepdims=True)
            outputs.append(times(weights.astype(BF16), v_ref[:stop, :]) * (1.0 / summed))
            totals.append(maximum + jnp.log(summed))
        out_ref[start:stop, :] = jnp.where(first, outputs[0], outputs[1]).astype(BF16)
        turned = jnp.where(first, totals[0], totals[1]).T
        totals_ref[0:1, start:stop] = turned[0:1, :]
        totals_ref[1:2, start:stop] = turned[HEAD_DIM : HEAD_DIM + 1, :]


def attend_backward_kernel(
    tile, q_ref, k_ref, v_ref, out_ref, grad_ref, totals_ref, grad_refs, sum_q_ref
):
    grad_q_ref, grad_k_ref, grad_v_ref = grad_refs
    length = q_ref.shape[0]
    first = lax.broadcasted_iota(jnp.int32, (1, LANES), 1) < HEAD_DIM
    head_of_lane = lax.broadcasted_iota(jnp.int32, (8, LANES), 1) // HEAD_DIM
    pick = jnp.where(
        head_of_lane == lax.broadcasted_iota(jnp.int32, (8, LANES), 0), 1.0, 0.0
    ).astype(BF16)
    product = out_ref[...].astype(F32) * grad_ref[...].astype(F32)
    coarse = product.astype(BF16)
    fine = (product - coarse.astype(F32)).astype(BF16)
    inner = times_transposed(pick, coarse) + times_transposed(pick, fine)
    row = lax.broadcasted_iota(jnp.int32, (tile, tile), 0)
    column = lax.broadcasted_iota(jnp.int32, (tile, tile), 1)
    for start in range(0, length, tile):
        stop = start + tile
        keys = k_ref[start:stop, :] * jnp.asarray(SCALE, BF16)
        own_values = v_ref[start:stop, :]
        queries, grads = q_ref[start:, :], grad_ref[start:, :]
        grad_keys, grad_values = [], []
        for head, own in enumerate((first, ~first)):
            own_keys = jnp.where(own, keys, jnp.zeros((), BF16))
            scores = times_transposed(own_keys, queries)
            probs = jnp.exp(scores - totals_ref[head : head + 1, start:])
            diagonal = jnp.where(column >= row, probs[:, :tile], 0.0)
            probs = (
                diagonal if stop == length else jnp.concatenate([diagonal, probs[:, tile:]], 1)
            )
            grad_probs = times_transposed(
                jnp.where(own, own_values, jnp.zeros((), BF16)), grads
            )
            grad_scores = (probs * (grad_probs - inner[head : head + 1, start:])).astype(BF16)
            grad_values.append(times(probs.astype(BF16), grads))
            grad_keys.append(times(grad_scores, queries))
            part = contract_rows(grad_scores, own_keys)
            if start == 0 and head == 0:
                sum_q_ref[...] = part
            else:
                sum_q_ref[start:, :] += part
        grad_k_ref[start:stop, :] = (
            jnp.where(first, grad_keys[0], grad_keys[1]) * SCALE
        ).astype(BF16)
        grad_v_ref[start:stop, :] = jnp.where(first, grad_values[0], grad_values[1]).astype(BF16)
    grad_q_ref[...] = sum_q_ref[...].astype(BF16)


def column_spec(length, base, step=1, width=LANES):
    return pl.BlockSpec((length, width), lambda s, p: (s, base + step * p))


def attend_forward(queries, keys, values, places, length, pairs):
    rows = queries.shape[0]
    seqs = rows // length
    return pl.pallas_call(
        functools.partial(attend_forward_kernel, min(512, length)),
        grid=(seqs, pairs),
        in_specs=[column_spec(length, *place) for place in places],
        out_specs=[
            column_spec(length, 0),
            pl.BlockSpec((None, None, 2, length), lambda s, p: (s, p, 0, 0)),
        ],
        out_shape=[
            jax.ShapeDtypeStruct((rows, pairs * LANES), BF16),
            jax.ShapeDtypeStruct((seqs, pairs, 2, length), F32),
        ],
        compiler_params=pltpu.CompilerParams(vmem_limit_bytes=VMEM_BYTES),
        cost_estimate=cost(12 * rows * length * pairs * LANES, 8 * rows * pairs * LANES),
        name="attend_forward",
    )(queries, keys, values)


def attend_backward(queries, keys, values, attended, grads, totals, places, length, at, pairs, together):
    seqs = totals.shape[0]
    rows = seqs * length
    places = [(base + step * at, step) for base, step in places]
    widths = (3 * LANES,) if together else (2 * LANES, LANES)

    def kernel(*refs):
        ins, outs, sum_q_ref = refs[:6], refs[6:-1], refs[-1]
        parts = [outs[0].at[:, :LANES], outs[0].at[:, LANES : 2 * LANES]]
        parts.append(outs[0].at[:, 2 * LANES :] if together else outs[1])
        attend_backward_kernel(min(256, length), *ins, parts, sum_q_ref)

    return pl.pallas_call(
        kernel,
        grid=(seqs, pairs),
        in_specs=[column_spec(length, *place) for place in places]
        + [pl.BlockSpec((None, None, 2, length), lambda s, p: (s, at + p, 0, 0))],
        out_specs=[column_spec(length, 0, 1, w) for w in widths],
        out_shape=[jax.ShapeDtypeStruct((rows, pairs * w), BF16) for w in widths],
        scratch_shapes=[pltpu.VMEM((length, LANES), F32)],
        compiler_params=pltpu.CompilerParams(vmem_limit_bytes=VMEM_BYTES),
        cost_estimate=cost(24 * rows * length * pairs * LANES, 16 * rows * pairs * LANES),
        name="attend_backward",
    )(queries, keys, values, attended, grads, totals)


def after(array, *others):
    others = [o for o in others if o is not None]
    return lax.optimization_barrier((array, *others))[0] if others else array


class Chain:
    def __init__(self, steps):
        self.steps, self.came, self.value, self.left = steps, None, None, True

    def step(self, now):
        try:
            if self.came is None:
                return next(self.steps)
            return self.steps.send([after(c, now) for c in self.came])
        except StopIteration as stop:
            self.value, self.left = stop.value, False
            return []


class Grid:
    def __init__(self, mesh):
        self.dp, halves = mesh.shape["dp"], mesh.shape["seq"]
        assert halves == 2 and self.dp & (self.dp - 1) == 0
        self.bits = self.dp.bit_length()
        self.masks = [1 << b for b in reversed(range(self.bits - 1))]

    def go(self, *chains, now=None, inputs=()):
        moves = [(chain, chain.step(now)) for chain in chains]
        arrays = [after(array, now) for _, some in moves for array, _ in some]
        if inputs and arrays:
            tied = lax.optimization_barrier((*inputs, *arrays))
            inputs, arrays = tied[: len(inputs)], tied[len(inputs) :]
        for chain, some in moves:
            chain.came = [self.swap(arrays[n], mask) for n, (_, mask) in enumerate(some)]
            arrays = arrays[len(some) :]
        return inputs

    def swap(self, array, mask):
        if mask == 0:
            return lax.ppermute(array, "seq", [(0, 1), (1, 0)])
        return lax.ppermute(array, "dp", [(i, i ^ mask) for i in range(self.dp)])

    def end(self, *chains, now=None):
        while any(chain.left for chain in chains):
            self.go(*[chain for chain in chains if chain.left], now=now)
        return [chain.value for chain in chains]

    def bit(self, mask):
        if mask == 0:
            return lax.axis_index("seq")
        return jnp.where(lax.axis_index("dp") & mask, 1, 0)

    def in_pieces(self, rows):
        return (2 * rows) % 16 == 0

    def pair(self, held, came):
        low = self.bit(0) == 0
        return jnp.concatenate([jnp.where(low, held, came), jnp.where(low, came, held)], 1)

    def gather(self, shard, masks):
        if not self.in_pieces(shard.shape[0]):
            return (yield from self.gather_in_order(shard))
        held = shard[None]
        for mask in masks[:-1]:
            (came,) = yield [(held, mask)]
            held = jnp.concatenate([held, came], 0) if mask else self.pair(held, came)
        (came,) = yield [(held, masks[-1])]
        return held, came

    def gather_plane(self, shard, near):
        if not self.in_pieces(shard.shape[0]):
            return (yield from self.gather_in_order(shard))
        held = shard[None]
        for mask in self.masks[:-2]:
            (came,) = yield [(held, mask)]
            held = jnp.concatenate([held, came], 0)
        aside, across = yield [(held, near), (held, 0)]
        cut = held.shape[2] // 2 // LANES * LANES
        left, right = yield [(across[:, :, :cut], near), (aside[:, :, cut:], 0)]
        corner = jnp.concatenate([left, right], 2)
        held = jnp.concatenate([self.pair(held, across), self.pair(aside, corner)], 0)
        (came,) = yield [(held, 1)]
        return held, came

    def flips(self, masks):
        masks = [m for m in masks if m]
        return [
            sum(m for b, m in enumerate(masks) if j >> b & 1) for j in range(1 << len(masks))
        ]

    def gather_in_order(self, shard):
        whole = shard
        for step, mask in enumerate(self.masks + [0]):
            (came,) = yield [(whole, mask)]
            low = self.bit(mask) == 0
            whole = jnp.stack([jnp.where(low, whole, came), jnp.where(low, came, whole)], step)
        return (whole.reshape(-1, shard.shape[-1]),)

    def scatter_sum(self, pieces, masks, direct=False, unsummed=False):
        if len(pieces) == 1:
            return (yield from self.scatter_sum_in_order(pieces[0]))
        keep, away = pieces
        (came,) = yield [(away, 1)]
        for step, mask in enumerate(masks):
            count, rows, columns = keep.shape
            if direct and mask in self.masks[:-2]:
                if mask == self.masks[-3]:
                    far = [m for m in masks if m in self.masks[:-2]][::-1]
                    flips = self.flips(far)
                    moves = [(self.add(keep[j : j + 1], came[j : j + 1]), flips[j]) for j in range(1, count)]
                    keep = self.add(keep[:1], came[:1])
                    several = yield moves
                    came = sum(c.astype(F32) for c in several)
                continue
            if mask:
                parts = [(t[: count // 2], t[count // 2 :]) for t in (keep, came)]
            else:
                parts = [self.part(t) for t in (keep, came)]
            away = self.add(parts[0][1], parts[1][1])
            keep = self.add(parts[0][0], parts[1][0])
            (came,) = yield [(away, mask)]
        return (keep[0], came[0]) if unsummed else self.last_sum(keep[0], came[0])

    def last_sum(self, keep, came):
        def kernel(keep_ref, came_ref, out_ref):
            out_ref[...] = keep_ref[...].astype(F32) + came_ref[...].astype(F32)

        return pl.pallas_call(
            kernel, out_shape=jax.ShapeDtypeStruct(keep.shape, F32), name="last_sum"
        )(keep, came)

    def part(self, array):
        count, rows, columns = array.shape
        split = array.reshape(count, 2, rows // 2, columns)
        seq = self.bit(0)
        return [lax.dynamic_index_in_dim(split, w, 1, keepdims=False) for w in (seq, 1 - seq)]

    def scatter_sum_plane(self, pieces, near):
        if len(pieces) == 1:
            return (yield from self.scatter_sum_in_order(pieces[0]))
        keep, away = pieces
        (came,) = yield [(away, 1)]
        half = keep.shape[0] // 2
        cut = keep.shape[2] // 2 // LANES * LANES
        (own, across), (aside, corner) = (
            [
                self.add(k, c)
                for k, c in zip(self.part(keep[at]), self.part(came[at]), strict=True)
            ]
            for at in (slice(0, half), slice(half, None))
        )
        left, right = yield [(corner[:, :, :cut], near), (corner[:, :, cut:], 0)]
        across = jnp.concatenate([self.add(across[:, :, :cut], left), across[:, :, cut:]], 2)
        aside = jnp.concatenate([aside[:, :, :cut], self.add(aside[:, :, cut:], right)], 2)
        left, right = yield [(aside, near), (across, 0)]
        total = own.astype(F32) + left.astype(F32) + right.astype(F32)
        for mask in self.masks[:-2][::-1]:
            total = total.astype(BF16)
            half = total.shape[0] // 2
            (came,) = yield [(total[half:], mask)]
            total = total[:half].astype(F32) + came.astype(F32)
        return total[0]

    def add(self, left, right):
        return (left.astype(F32) + right.astype(F32)).astype(BF16)

    def scatter_sum_in_order(self, partial):
        rows, columns = partial.shape
        order = self.masks + [0]
        whole = partial.reshape((2,) * self.bits + (rows >> self.bits, columns))
        for step in reversed(range(self.bits)):
            bit = self.bit(order[step])
            away = lax.dynamic_index_in_dim(whole, 1 - bit, step, keepdims=False)
            keep = lax.dynamic_index_in_dim(whole, bit, step, keepdims=False)
            (came,) = yield [(away, order[step])]
            whole = keep.astype(F32) + came.astype(F32)
            if step:
                whole = whole.astype(BF16)
        return whole

    def to_other(self, array):
        count, half, width = array.shape
        seq = self.bit(0)
        split = array.reshape(2, count // 2, half, width)
        keep = lax.dynamic_index_in_dim(split, seq, 0, keepdims=False)
        (came,) = yield [(lax.dynamic_index_in_dim(split, 1 - seq, 0, keepdims=False), 0)]
        return keep.reshape(-1, width), came.reshape(-1, width)

    def to_whole(self, array):
        count, half, width = array.shape
        seq = self.bit(0)
        split = array.reshape(2, count // 2, half, width)
        keep = lax.dynamic_index_in_dim(split, seq, 0, keepdims=False)
        (came,) = yield [(lax.dynamic_index_in_dim(split, 1 - seq, 0, keepdims=False), 0)]
        low = seq == 0
        return jnp.stack(
            [jnp.where(low, keep, came), jnp.where(low, came, keep)], 1
        ).reshape(count * half, width)

    def to_halves(self, array, half):
        width = array.shape[-1]
        seq = self.bit(0)
        split = array.reshape(-1, 2, half, width)
        keep = lax.dynamic_index_in_dim(split, seq, 1, keepdims=False)
        (came,) = yield [(lax.dynamic_index_in_dim(split, 1 - seq, 1, keepdims=False), 0)]
        low = seq == 0
        return jnp.concatenate([jnp.where(low, keep, came), jnp.where(low, came, keep)], 0)


class Weight:
    def __init__(self, grid, rows, *gathered):
        self.arrays, self.groups, self.columns, self.rows = [], [], 0, rows
        for arrays, order in gathered:
            flips = grid.flips(order) if len(arrays) == 2 else None
            self.arrays += arrays
            self.groups.append((flips, self.columns, arrays[0].shape[-1]))
            self.columns += arrays[0].shape[-1]

    @property
    def copies(self):
        return sum(len(flips) if flips else 1 for flips, _, _ in self.groups)

    def specs(self):
        return [pl.BlockSpec(memory_space=pl.ANY)] * len(self.arrays)

    def scratch(self):
        return [
            pltpu.VMEM((self.rows, self.columns), BF16),
            pltpu.SemaphoreType.DMA((self.copies,)),
        ]

    def loads(self, me, refs, whole, sems):
        found, at = [], 0
        for flips, start, columns in self.groups:
            if flips is None:
                found.append((refs[at], whole.at[:, start : start + columns]))
                at += 1
                continue
            half = len(flips) // 2
            rows = self.rows // len(flips)
            for j, flip in enumerate(flips):
                to = pl.multiple_of((me ^ flip) * rows, 16)
                found.append(
                    (
                        refs[at + j // half].at[j % half],
                        whole.at[pl.ds(to, rows), start : start + columns],
                    )
                )
            at += 2
        return [
            pltpu.make_async_copy(source, target, sems.at[n])
            for n, (source, target) in enumerate(found)
        ]


def piece_of(index, me, masks):
    apart = index ^ (me >> 1)
    place = 0
    for mask in masks:
        place = 2 * place + jnp.where(apart & (mask >> 1), 1, 0)
    return place


def normalize(values):
    center = values - jnp.mean(values, -1, keepdims=True)
    spread = jnp.mean(center * center, -1, keepdims=True)
    inverse = lax.rsqrt(spread + EPSILON)
    return center * inverse, inverse


def normalize_back(grad, unit, inverse, gain):
    scaled = grad * gain
    along = jnp.mean(scaled * unit, -1, keepdims=True)
    level = jnp.mean(scaled, -1, keepdims=True)
    return inverse * (scaled - level - unit * along)


GELU_A = (2.0 / 3.141592653589793) ** 0.5
GELU_B = 0.044715


def gelu_both(u):
    square = u * u
    turned = jnp.tanh(u * (GELU_A + (GELU_A * GELU_B) * square))
    half = 0.5 + 0.5 * turned
    slope = half + (0.5 * u) * (1.0 - turned * turned) * (GELU_A + (3 * GELU_A * GELU_B) * square)
    return u * half, slope


def update(gradient, moment, master, average):
    moment_new = MOMENTUM * moment + gradient
    master_new = master - RATE * (gradient + MOMENTUM * moment_new)
    average_new = AVERAGING * average + (1.0 - AVERAGING) * master_new
    return (moment_new, master_new, average_new)


def finish(keep, came, fresh, parameters, norms, layout):
    rows, columns = parameters[0].shape
    many = norms[0].shape[0]

    def kernel(keep_ref, came_ref, fresh_ref, *refs):
        ins, outs = refs[:6], refs[6:]
        for place, is_fresh, block in layout:
            at, to = slice(block * LANES, (block + 1) * LANES), slice(place * LANES, (place + 1) * LANES)
            if is_fresh:
                total = fresh_ref[:, at]
            else:
                total = keep_ref[:, at].astype(F32) + came_ref[:, at].astype(F32)
            for ref, new in zip(outs, update(total, *(r[:, to] for r in ins[:3]))):
                ref[:, to] = new
        last = slice(keep_ref.shape[1] - LANES, keep_ref.shape[1])
        total = (keep_ref[:, last].astype(F32) + came_ref[:, last].astype(F32)).T[:many, :]
        for ref, new in zip(outs[3:], update(total, *(r[...] for r in ins[3:]))):
            ref[...] = new

    return pl.pallas_call(
        kernel,
        out_shape=[jax.ShapeDtypeStruct(a.shape, F32) for a in (*parameters, *norms)],
        name="finish",
    )(keep, came, fresh, *parameters, *norms)


def row_spec(tile, width, again=0):
    return pl.BlockSpec((tile, width), lambda i, me: (i % again if again else i, 0))


def whole_spec(shape):
    return pl.BlockSpec(shape, lambda i, me: (0,) * len(shape))


def row_call(kernel, name, me, tile, rows, ins, weights, outs, flops, scratch=(), give_me=False):
    n_in, n_out = len(ins), len(outs)

    def run(me_ref, *refs):
        at = n_in
        in_refs = refs[:n_in]
        weight_refs = []
        for weight in weights:
            weight_refs.append(refs[at : at + len(weight.arrays)])
            at += len(weight.arrays)
        out_refs = refs[at : at + n_out]
        at += n_out
        held, loads = [], []
        for weight, its in zip(weights, weight_refs, strict=True):
            held.append(refs[at])
            loads.append(weight.loads(me_ref[0], its, refs[at], refs[at + 1]))
            at += 2
        step = pl.program_id(0)

        @pl.when(step == 0)
        def _():
            for some in loads:
                for load in some:
                    load.start()

        def ready(which):
            @pl.when(step == 0)
            def _():
                for load in loads[which]:
                    load.wait()

            return held[which]

        kernel(step, ready, *in_refs, *out_refs, *refs[at:], *([me_ref] if give_me else []))

    moved = sum(a.size * a.dtype.itemsize for a, _ in ins)
    moved += sum(w.rows * w.columns * 2 for w in weights)
    moved += sum(s[0] * s[1] * jnp.dtype(d).itemsize for s, d, _ in outs)
    return pl.pallas_call(
        run,
        grid_spec=pltpu.PrefetchScalarGridSpec(
            num_scalar_prefetch=1,
            grid=(rows // tile,),
            in_specs=[
                whole_spec(a.shape) if whole is True else row_spec(tile, a.shape[1], whole)
                for a, whole in ins
            ]
            + [s for w in weights for s in w.specs()],
            out_specs=[
                whole_spec(shape) if whole else row_spec(tile, shape[1])
                for shape, _, whole in outs
            ],
            scratch_shapes=[s for w in weights for s in w.scratch()] + list(scratch),
        ),
        out_shape=[jax.ShapeDtypeStruct(shape, dtype) for shape, dtype, _ in outs],
        compiler_params=pltpu.CompilerParams(vmem_limit_bytes=VMEM_BYTES),
        cost_estimate=cost(flops, moved),
        name=name,
    )(me, *[a for a, _ in ins], *[x for w in weights for x in w.arrays])


def project(me, own, other, weight):
    rows, width = 2 * own.shape[0], own.shape[1]
    columns = weight.columns - LANES
    tile = 256
    per_half = own.shape[0] // tile

    def kernel(step, ready, own_ref, other_ref, projected_ref, rows_ref, unit_ref, weight_ref, norm_ref, me_ref):
        mine = (step // per_half == me_ref[1]).astype(jnp.int32)
        now = jnp.where(mine == 1, own_ref[...], other_ref[...])
        rows_ref[...] = now
        unit, _ = normalize(now.astype(F32))
        unit_ref[...] = unit.astype(BF16)
        held = ready(0)

        @pl.when(step == 0)
        def _():
            norm_ref[...] = held[:, columns:].astype(F32).T[: norm_ref.shape[0], :]
            weight_ref[...] = held[...]

        normed = (unit * norm_ref[0:1, :] + norm_ref[1:2, :]).astype(BF16)
        projected_ref[...] = times(normed, held[:, :columns]).astype(BF16)

    return row_call(
        kernel,
        "project",
        me,
        tile,
        rows,
        [(own, per_half), (other, per_half)],
        [weight],
        [
            ((rows, columns), BF16, False),
            ((rows, width), BF16, False),
            ((rows, width), BF16, False),
            ((width, weight.columns), BF16, True),
            ((8, width), F32, True),
        ],
        2 * rows * width * columns,
        give_me=True,
    )


def to_hidden(me, attended, rows_in, norm, w_out_up):
    rows, width = rows_in.shape
    hidden = w_out_up.columns - width
    chunk = 768

    part = width // 2

    def kernel(step, ready, one_ref, two_ref, rows_ref, norm_ref, mid_ref, normed_ref, hidden_ref, slope_ref):
        held = ready(0)
        mid = rows_ref[...].astype(F32) + times(one_ref[...], held[:part, :width])
        mid = mid + times(two_ref[...], held[part:, :width])
        mid_ref[...] = mid
        unit, _ = normalize(mid)
        normed = (unit * norm_ref[2:3, :] + norm_ref[3:4, :]).astype(BF16)
        normed_ref[...] = normed
        for at in range(0, hidden, chunk):
            act, slope = gelu_both(times(normed, held[:, width + at : width + at + chunk]))
            hidden_ref[:, at : at + chunk] = act.astype(BF16)
            slope_ref[:, at : at + chunk] = slope.astype(BF16)

    return row_call(
        kernel,
        "to_hidden",
        me,
        256,
        rows,
        [(attended[0], False), (attended[1], False), (rows_in, False), (norm, True)],
        [w_out_up],
        [
            ((rows, width), F32, False),
            ((rows, width), BF16, False),
            ((rows, hidden), BF16, False),
            ((rows, hidden), BF16, False),
        ],
        2 * rows * width * (width + hidden),
    )


def from_hidden(me, hidden, mid_rows, w_down):
    rows, width = mid_rows.shape
    wide = hidden.shape[1]

    def kernel(step, ready, hidden_ref, mid_ref, mixed_ref):
        down = ready(0)
        mixed_ref[...] = (mid_ref[...] + times(hidden_ref[...], down[...])).astype(BF16)

    return row_call(
        kernel,
        "from_hidden",
        me,
        256,
        rows,
        [(hidden, False), (mid_rows, False)],
        [w_down],
        [((rows, width), BF16, False)],
        2 * rows * width * wide,
    )[0]


def hidden_gradient(me, slope, grad_mixed, w_down):
    rows, wide = slope.shape
    width = grad_mixed.shape[1]
    chunk = 768

    def kernel(step, ready, slope_ref, grad_ref, back_ref):
        down = ready(0)
        grad = grad_ref[...]
        for at in range(0, wide, chunk):
            part = times_transposed(grad, down[at : at + chunk, :])
            back_ref[:, at : at + chunk] = (
                part * slope_ref[:, at : at + chunk].astype(F32)
            ).astype(BF16)

    return row_call(
        kernel,
        "hidden_gradient",
        me,
        256,
        rows,
        [(slope, False), (grad_mixed, False)],
        [w_down],
        [((rows, wide), BF16, False)],
        2 * rows * width * wide,
    )[0]


def to_middle(me, grad_hidden, mid_rows, grad_mixed, norm, w_out_up):
    rows, width = mid_rows.shape

    def kernel(step, ready, hidden_ref, mid_ref, grad_ref, norm_ref, dmid_ref, low_ref, do_ref, sums_ref):
        unit, inverse = normalize(mid_ref[...])
        held = ready(0)
        back = times_transposed(hidden_ref[...], held[:, width:])

        @pl.when(step == 0)
        def _():
            sums_ref[...] = jnp.zeros_like(sums_ref)

        sums_ref[0:1, :] += jnp.sum(back * unit, 0, keepdims=True)
        sums_ref[1:2, :] += jnp.sum(back, 0, keepdims=True)
        dmid = grad_ref[...].astype(F32) + normalize_back(back, unit, inverse, norm_ref[2:3, :])
        dmid_ref[...] = dmid
        low = dmid.astype(BF16)
        low_ref[...] = low
        do_ref[...] = times_transposed(low, held[:, :width]).astype(BF16)

    return row_call(
        kernel,
        "to_middle",
        me,
        256,
        rows,
        [(grad_hidden, False), (mid_rows, False), (grad_mixed, False), (norm, True)],
        [w_out_up],
        [
            ((rows, width), F32, False),
            ((rows, width), BF16, False),
            ((rows, width), BF16, False),
            ((8, width), F32, True),
        ],
        2 * rows * width * (width + grad_hidden.shape[1]),
    )


def to_tokens(me, grads, rows_in, grad_mid, norm, w_qkv):
    rows, width = rows_in.shape

    def kernel(step, ready, *refs):
        grad_refs, (rows_ref, dmid_ref, norm_ref, weight_ref, out_ref) = (
            refs[: len(grads)],
            refs[len(grads) :],
        )
        unit, inverse = normalize(rows_ref[...].astype(F32))
        back, at = None, 0
        for ref in grad_refs:
            part = times_transposed(ref[...], weight_ref[:, at : at + ref.shape[1]])
            back = part if back is None else back + part
            at += ref.shape[1]
        out_ref[...] = (
            dmid_ref[...] + normalize_back(back, unit, inverse, norm_ref[0:1, :])
        ).astype(BF16)

    return row_call(
        kernel,
        "to_tokens",
        me,
        256,
        rows,
        [(g, False) for g in grads]
        + [(rows_in, False), (grad_mid, False), (norm, True), (w_qkv, True)],
        [],
        [((rows, width), BF16, False)],
        2 * rows * width * (w_qkv.shape[1] - LANES),
    )[0]


class Norm:
    def __init__(self, weight, column, sums=None, second=None):
        self.weight, self.column, self.sums, self.second = weight, column, sums, second


def rows_gradient(grid, me, lefts, rights, masks, chunk, norm=None):
    lefts = [left if isinstance(left, tuple) else (left,) for left in lefts]
    rows, width = lefts[0][0].shape[0], sum(part.shape[1] for part in lefts[0])
    columns = sum(r.shape[1] for _, r in rights)
    last = len(lefts) - 1
    emit = norm is not None and norm.second is not None
    if not grid.in_pieces(width >> grid.bits):
        parts = []
        if norm:
            column = norm.column
            gain, shift = (norm.weight[:, n - LANES : n - LANES + 1].astype(F32) for n in (0, 1))
            sums = norm.sums if norm.sums is not None else jnp.zeros((width, LANES), F32)
        for n, r in rights:
            product = contract_rows(jnp.concatenate(lefts[n], 1), r)
            if norm and n == last:
                total = jnp.sum(r.astype(F32), 0, keepdims=True)
                own = norm.weight[:, column : column + r.shape[1]].astype(F32)
                column += r.shape[1]
                both = [jnp.sum(own * t, 1, keepdims=True) for t in (product, total)]
                sums = sums + jnp.pad(jnp.concatenate(both, 1), ((0, 0), (0, LANES - 2)))
                product = gain * product + shift * total
            parts.append(product)
        if emit:
            parts.append(sums + jnp.pad(norm.second[:2].T, ((0, 0), (2, LANES - 4))))
        pieces = (jnp.concatenate(parts, 1).astype(BF16),)
        return (pieces, sums) if norm and not emit else pieces
    masks = [m for m in masks if m]
    flat = [part for left in lefts for part in left]
    steps_of = [r.shape[1] // chunk for _, r in rights]
    starts = [sum(steps_of[:n]) for n in range(len(rights))]
    steps = sum(steps_of)
    pairs = grid.dp // 2
    piece = width // grid.dp
    total = columns + (LANES if emit else 0)
    extras, extra_specs = [], []
    if norm:
        first = min(starts[n] for n, (of, _) in enumerate(rights) if of == last)
        extras = [norm.weight]
        extra_specs = [
            whole_spec(norm.weight.shape),
        ]
        for some in (norm.sums, norm.second):
            if some is not None:
                extras.append(some)
                extra_specs.append(whole_spec(some.shape))

    def kernel(me_ref, *refs):
        left_refs, refs = refs[: len(flat)], refs[len(flat) :]
        right_refs, refs = refs[: len(rights)], refs[len(rights) :]
        extra_refs, refs = refs[: len(extras)], refs[len(extras) :]
        keep_ref, away_ref, *refs = refs
        if norm:
            sums_ref, *refs = refs
            weight_ref = extra_refs[0]
        turned_refs = refs
        step = pl.program_id(0)
        device = me_ref[0]
        core = device & 1

        def put(product, at):
            for index in range(pairs):
                place = piece_of(index, device, masks)
                even = product[2 * index * piece : (2 * index + 1) * piece, :]
                odd = product[(2 * index + 1) * piece : (2 * index + 2) * piece, :]
                keep_ref[place, :, at] = jnp.where(core == 0, even, odd).astype(BF16)
                away_ref[place, :, at] = jnp.where(core == 0, odd, even).astype(BF16)

        @pl.when(step == 0)
        def _():
            n = 0
            for left, turned_ref in zip(lefts, turned_refs, strict=True):
                at = 0
                for part in left:
                    turned_ref[at : at + part.shape[1], :] = left_refs[n][...].T
                    at, n = at + part.shape[1], n + 1
            if norm:
                if norm.sums is not None:
                    sums_ref[...] = extra_refs[1][...]
                else:
                    sums_ref[...] = jnp.zeros_like(sums_ref)

        for n, ref in enumerate(right_refs):
            @pl.when((step >= starts[n]) & (step < starts[n] + steps_of[n]))
            def _(n=n, ref=ref):
                product = times(turned_refs[rights[n][0]][...], ref[...])
                if norm and rights[n][0] == last:
                    total = jnp.sum(ref[...].astype(F32), 0, keepdims=True)
                    at = pl.multiple_of(norm.column + (step - first) * chunk, LANES)
                    own = weight_ref[:, pl.ds(at, chunk)].astype(F32)
                    lane = lax.broadcasted_iota(jnp.int32, (1, LANES), 1)
                    sums_ref[...] += jnp.where(
                        lane == 0, jnp.sum(own * product, 1, keepdims=True), 0.0
                    ) + jnp.where(lane == 1, jnp.sum(own * total, 1, keepdims=True), 0.0)
                    param = weight_ref[:, -LANES:].astype(F32)
                    product = param[:, 0:1] * product + param[:, 1:2] * total
                put(product, pl.ds(pl.multiple_of(step * chunk, LANES), chunk))

        if emit:
            @pl.when(step == steps - 1)
            def _():
                second = extra_refs[-1][0:2, :]
                below = jnp.zeros((2, width), F32)
                tail = jnp.zeros((LANES - 4, width), F32)
                put(
                    sums_ref[...] + jnp.concatenate([below, second, tail], 0).T,
                    pl.ds(columns, LANES),
                )

    def right_spec(n):
        return pl.BlockSpec(
            (rows, chunk), lambda i, me: (0, jnp.clip(i - starts[n], 0, steps_of[n] - 1))
        )

    shape = (pairs, piece, total)
    sums_shape = (width, LANES)
    outs = pl.pallas_call(
        kernel,
        grid_spec=pltpu.PrefetchScalarGridSpec(
            num_scalar_prefetch=1,
            grid=(steps,),
            in_specs=[whole_spec(left.shape) for left in flat]
            + [right_spec(n) for n in range(len(rights))]
            + extra_specs,
            out_specs=[whole_spec(shape)] * 2 + [whole_spec(sums_shape)] * bool(norm),
            scratch_shapes=[pltpu.VMEM((width, rows), BF16)] * len(lefts),
        ),
        out_shape=[jax.ShapeDtypeStruct(shape, BF16)] * 2
        + [jax.ShapeDtypeStruct(sums_shape, F32)] * bool(norm),
        compiler_params=pltpu.CompilerParams(vmem_limit_bytes=VMEM_BYTES),
        cost_estimate=cost(2 * rows * width * columns, 2 * (rows * (width + columns) + width * columns)),
        name="rows_gradient",
    )(me, *flat, *[r for _, r in rights], *extras)
    if norm and not emit:
        return outs[:2], outs[2]
    return outs[:2]


def columns_gradient(grid, me, left, right, masks):
    masks = [m for m in masks if m]
    rows, wide = left.shape
    width = right.shape[1]
    piece = wide // grid.dp
    if not grid.in_pieces(wide >> grid.bits) or (2 * piece) % LANES:
        return (contract_rows(left, right).astype(BF16),)
    pairs = grid.dp // 2

    def kernel(me_ref, left_ref, right_ref, keep_ref, away_ref):
        product = contract_rows(left_ref[...], right_ref[...])
        even, odd = product[:piece, :], product[piece:, :]
        core = me_ref[0] & 1
        keep_ref[...] = jnp.where(core == 0, even, odd).astype(BF16)
        away_ref[...] = jnp.where(core == 0, odd, even).astype(BF16)

    out = pl.BlockSpec((None, piece, width), lambda i, me: (piece_of(i, me[0], masks), 0, 0))
    shape = (pairs, piece, width)
    return pl.pallas_call(
        kernel,
        grid_spec=pltpu.PrefetchScalarGridSpec(
            num_scalar_prefetch=1,
            grid=(pairs,),
            in_specs=[
                pl.BlockSpec((rows, 2 * piece), lambda i, me: (0, i)),
                whole_spec(right.shape),
            ],
            out_specs=[out] * 2,
        ),
        out_shape=[jax.ShapeDtypeStruct(shape, BF16)] * 2,
        compiler_params=pltpu.CompilerParams(vmem_limit_bytes=VMEM_BYTES),
        cost_estimate=cost(2 * rows * width * wide, 2 * (rows * (width + wide) + width * wide)),
        name="columns_gradient",
    )(me, left, right)


def body(
    grid,
    tokens,
    first_values,
    cotangent,
    lengths,
    qkv_master,
    qkv_moment,
    qkv_average,
    out_master,
    out_moment,
    out_average,
    up_master,
    up_moment,
    up_average,
    down_master,
    down_moment,
    down_average,
    norm_master,
    norm_moment,
    norm_average,
):
    count, half, width = tokens.shape
    length = 2 * half
    part = width // 2
    norm_columns = norm_master.shape[1]
    assert count == 2
    me = jnp.stack([lax.axis_index("dp"), lax.axis_index("seq")]).astype(jnp.int32)
    far, near = grid.masks[:-2], grid.masks[-2]
    back = far[::-1]
    go, end = grid.go, grid.end
    pairs = width // LANES
    half_pairs = pairs // 2

    fresh_blocks = [n * pairs + p for p in range(half_pairs) for n in range(3)]
    reused_blocks = [n * pairs + p for p in range(half_pairs, pairs) for n in range(2)]

    def blocks(array, which):
        return jnp.concatenate([array[:, n * LANES : (n + 1) * LANES] for n in which], 1)

    fresh_shard = blocks(qkv_master, fresh_blocks).astype(BF16)
    reused_shard = jnp.concatenate(
        [blocks(qkv_master, reused_blocks), jnp.pad(norm_master, ((0, 0), (0, LANES - norm_columns)))], 1
    ).astype(BF16)
    out_up_shard = jnp.concatenate([out_master, up_master], 1).astype(BF16)
    order_fresh, order_reused = [0, *far, near, 1], [0, near, *far, 1]
    order_plane = [*far, near, 1]
    fresh = Chain(grid.gather(fresh_shard, order_fresh))
    reused = Chain(grid.gather(reused_shard, order_reused))
    out_up = Chain(grid.gather_plane(out_up_shard, near))
    down = Chain(grid.gather_plane(down_master.astype(BF16), near))
    tokens_whole = Chain(grid.to_other(tokens))
    values_whole = Chain(grid.to_whole(first_values))
    cotangent_whole = Chain(grid.to_whole(cotangent))
    go(fresh, reused)
    go(tokens_whole)
    go(fresh, reused)
    go(fresh, reused)
    go(out_up)
    go(fresh, reused)
    go(values_whole)
    go(fresh, reused)
    go(out_up)
    fresh_pieces, reused_pieces, (rows_own, rows_other) = end(fresh, reused, tokens_whole)
    w_qkv = Weight(grid, width, (fresh_pieces, order_fresh), (reused_pieces, order_reused))

    projected, rows_in, unit_one, w_qkv, norm = project(me, rows_own, rows_other, w_qkv)
    now = projected
    base = 3 * half_pairs
    one = ((0, 3), (1, 3), (2, 3))
    two = ((base, 2), (base + 1, 2), (0, 1))
    projected, = go(out_up, down, now=now, inputs=(projected,))
    go(cotangent_whole, now=now)
    attended_one, totals_one = attend_forward(projected, projected, projected, one, length, half_pairs)
    now = attended_one
    (values_in,) = end(values_whole, now=now)
    values_in, = go(down, now=now, inputs=(values_in,))
    attended_two, totals_two = attend_forward(projected, projected, values_in, two, length, half_pairs)
    now = attended_two
    attended = (attended_one, attended_two)
    go(out_up, now=after(now, *down.came))
    go(out_up)
    attended_two, = go(down, now=now, inputs=(attended_two,))
    (out_up_pieces,) = end(out_up)
    w_out_up = Weight(grid, width, (out_up_pieces, order_plane))
    mid_rows, normed_two, hidden, slope = to_hidden(
        me, (attended_one, attended_two), rows_in, norm, w_out_up
    )
    now = normed_two
    hidden, = go(down, now=now, inputs=(hidden,))
    (whole_cotangent,) = end(cotangent_whole, now=now)
    own_lengths = lax.dynamic_index_in_dim(
        lengths.reshape(2, count // 2), lax.axis_index("seq"), 0, keepdims=False
    )
    position = lax.iota(jnp.int32, length)
    keep_mask = (position[None, :] < own_lengths[:, None]).reshape(-1)
    grad_mixed = jnp.where(keep_mask[:, None], whole_cotangent, jnp.zeros((), BF16))

    back_down, back_up, back_fresh = [near, *back, 0], [0, near, *back], [0, near, *back]
    back_reused = back_down
    grad_down = columns_gradient(grid, me, hidden, grad_mixed, back_down)
    sum_down = Chain(grid.scatter_sum(grad_down, back_down))
    now = grad_down[0]
    slope, = go(down, sum_down, now=now, inputs=(slope,))
    (down_pieces,) = end(down, now=now)
    w_down = Weight(grid, hidden.shape[1], (down_pieces, order_plane))
    grad_hidden = hidden_gradient(me, slope, grad_mixed, w_down)
    now = grad_hidden
    grad_hidden, = go(sum_down, now=now, inputs=(grad_hidden,))
    grad_up = rows_gradient(grid, me, [normed_two], [(0, grad_hidden)], back_up, 768)
    now = grad_up[0]
    sum_up = Chain(grid.scatter_sum(grad_up, back_up))
    hidden, = go(sum_up, now=now, inputs=(hidden,))
    mixed = from_hidden(me, hidden, mid_rows, w_down)
    now = mixed
    mixed_halves = Chain(grid.to_halves(mixed, half))
    grad_hidden, = go(sum_up, now=now, inputs=(grad_hidden,))
    grad_mid, grad_mid_low, grad_attended, sums_two = to_middle(
        me, grad_hidden, mid_rows, grad_mixed, norm, w_out_up
    )
    now = grad_attended

    def attend_back(which, at, many):
        values = values_in if which else projected
        return attend_backward(
            projected, projected, values, attended[which], grad_attended,
            totals_two if which else totals_one,
            (*(two if which else one), (0, 1), (which * half_pairs, 1)),
            length, at, many, not which,
        )

    grad_attended, = go(sum_down, mixed_halves, now=now, inputs=(grad_attended,))
    (grad_one,) = attend_back(0, 0, 1)
    now = grad_one
    grad_attended, = go(sum_up, now=now, inputs=(grad_attended,))
    (grad_two,) = attend_back(0, 1, 2)
    now = grad_two
    grad_two, = go(sum_down, sum_up, now=now, inputs=(grad_two,))
    grad_fresh, sums_one = rows_gradient(
        grid, me, [attended, unit_one], [(0, grad_mid_low), (1, grad_one), (1, grad_two)],
        back_fresh, 384, Norm(w_qkv, 0),
    )
    now = grad_fresh[0]
    sum_fresh = Chain(grid.scatter_sum(grad_fresh, back_fresh))
    grad_attended, = go(sum_fresh, sum_down, sum_up, now=now, inputs=(grad_attended,))
    grad_three, value_three = attend_back(1, 0, 1)
    now = grad_three
    grad_attended, = go(sum_fresh, now=now, inputs=(grad_attended,))
    (sum_up, sum_down) = end(sum_up, sum_down, now=now)
    grad_four, value_four = attend_back(1, 1, 2)
    now = grad_four
    grad_four, = go(sum_fresh, now=now, inputs=(grad_four,))
    grad_reused = rows_gradient(
        grid, me, [unit_one], [(0, grad_three), (0, grad_four)], back_reused, 256,
        Norm(w_qkv, 3 * part, sums_one, sums_two),
    )
    now = grad_reused[0]
    pieces = len(grad_reused) > 1
    sum_reused = Chain(grid.scatter_sum(grad_reused, back_reused, pieces, pieces))
    first_halves = Chain(grid.to_halves(jnp.concatenate([value_three, value_four], 1), half))
    go(sum_reused, now=now)
    grad_four, = go(sum_reused, inputs=(grad_four,))
    grad_four, = go(first_halves, sum_fresh, inputs=(grad_four,))
    tokens_grad = to_tokens(
        me, [grad_one, grad_two, grad_three, grad_four], rows_in, grad_mid, norm, w_qkv
    )
    now = tokens_grad
    tokens_halves = Chain(grid.to_halves(tokens_grad, half))
    go(sum_reused, now=now)
    go(tokens_halves, sum_fresh, now=now)
    sum_reused, sum_fresh, tokens_grad, first_grad, mixed = end(
        sum_reused, sum_fresh, tokens_halves, first_halves, mixed_halves
    )
    sum_out, sum_fresh = sum_fresh[:, :width], sum_fresh[:, width:]
    qkv = (qkv_moment, qkv_master, qkv_average)
    norms = (norm_moment, norm_master, norm_average)
    layout = [(place, True, n) for n, place in enumerate(fresh_blocks)]
    layout += [(place, False, n) for n, place in enumerate(reused_blocks)]
    if pieces:
        *qkv_new, one, two, three = finish(
            *sum_reused, sum_fresh, qkv, tuple(n.T for n in norms), layout
        )
        norm_new = (one.T, two.T, three.T)
    else:
        both = {
            place: (sum_fresh if is_fresh else sum_reused)[:, n * LANES : (n + 1) * LANES]
            for place, is_fresh, n in layout
        }
        qkv_new = update(jnp.concatenate([both[n] for n in range(len(both))], 1), *qkv)
        norm_new = update(sum_reused[:, 2 * part : 2 * part + norm_columns], *norms)
    return (
        mixed,
        tokens_grad,
        first_grad,
        *qkv_new,
        *update(sum_out, out_moment, out_master, out_average),
        *update(sum_up, up_moment, up_master, up_average),
        *update(sum_down, down_moment, down_master, down_average),
        *norm_new,
    )


def solution(mesh):
    activation = P("dp", "seq", None)
    parameter = P(("dp", "seq"), None)
    return jax.shard_map(
        functools.partial(body, Grid(mesh)),
        mesh=mesh,
        in_specs=(activation,) * 3 + (P("dp"),) + (parameter,) * 15,
        out_specs=(activation,) * 3 + (parameter,) * 15,
        check_vma=False,
    )
```

```python
import functools

import jax
import jax.numpy as jnp
from jax import lax
from jax.experimental import pallas as pl
from jax.experimental.pallas import tpu as pltpu
from jax.sharding import PartitionSpec as P

HEAD_DIM = 64
LANES = 128
EPSILON = 1e-05
MOMENTUM = 0.5
AVERAGING = 0.5
RATE = 0.0006
SCALE = HEAD_DIM ** (-0.5)
VMEM_BYTES = 24 << 20

BF16 = jnp.bfloat16
F32 = jnp.float32


def cost(flops, moved):
    return pl.CostEstimate(
        flops=int(flops) // 8, bytes_accessed=int(moved) // 8, transcendentals=0
    )


def times_transposed(left, right):
    return lax.dot_general(left, right, (((1,), (1,)), ((), ())), preferred_element_type=F32)


def times(left, right):
    return lax.dot_general(left, right, (((1,), (0,)), ((), ())), preferred_element_type=F32)


def contract_rows(left, right):
    return lax.dot_general(left, right, (((0,), (0,)), ((), ())), preferred_element_type=F32)


def attend_forward_kernel(tile, q_ref, k_ref, v_ref, out_ref, totals_ref):
    length = q_ref.shape[0]
    first = lax.broadcasted_iota(jnp.int32, (1, LANES), 1) < HEAD_DIM
    row = lax.broadcasted_iota(jnp.int32, (tile, tile), 0)
    column = lax.broadcasted_iota(jnp.int32, (tile, tile), 1)
    for block in range(length // tile):
        start, stop = block * tile, (block + 1) * tile
        queries = q_ref[start:stop, :] * jnp.asarray(SCALE, BF16)
        outputs, totals = [], []
        for own in (first, ~first):
            scores = times_transposed(
                jnp.where(own, queries, jnp.zeros((), BF16)), k_ref[:stop, :]
            )
            diagonal = jnp.where(row >= column, scores[:, start:], -1e30)
            scores = (
                diagonal if block == 0 else jnp.concatenate([scores[:, :start], diagonal], 1)
            )
            maximum = jnp.max(scores, 1, keepdims=True)
            weights = jnp.exp(scores - maximum)
            summed = jnp.sum(weights, 1, keepdims=True)
            outputs.append(times(weights.astype(BF16), v_ref[:stop, :]) * (1.0 / summed))
            totals.append(maximum + jnp.log(summed))
        out_ref[start:stop, :] = jnp.where(first, outputs[0], outputs[1]).astype(BF16)
        turned = jnp.where(first, totals[0], totals[1]).T
        totals_ref[0:1, start:stop] = turned[0:1, :]
        totals_ref[1:2, start:stop] = turned[HEAD_DIM : HEAD_DIM + 1, :]


def attend_backward_kernel(
    tile, q_ref, k_ref, v_ref, out_ref, grad_ref, totals_ref, grad_refs, sum_q_ref
):
    grad_q_ref, grad_k_ref, grad_v_ref = grad_refs
    length = q_ref.shape[0]
    first = lax.broadcasted_iota(jnp.int32, (1, LANES), 1) < HEAD_DIM
    head_of_lane = lax.broadcasted_iota(jnp.int32, (8, LANES), 1) // HEAD_DIM
    pick = jnp.where(
        head_of_lane == lax.broadcasted_iota(jnp.int32, (8, LANES), 0), 1.0, 0.0
    ).astype(BF16)
    product = out_ref[...].astype(F32) * grad_ref[...].astype(F32)
    coarse = product.astype(BF16)
    fine = (product - coarse.astype(F32)).astype(BF16)
    inner = times_transposed(pick, coarse) + times_transposed(pick, fine)
    row = lax.broadcasted_iota(jnp.int32, (tile, tile), 0)
    column = lax.broadcasted_iota(jnp.int32, (tile, tile), 1)
    for start in range(0, length, tile):
        stop = start + tile
        keys = k_ref[start:stop, :] * jnp.asarray(SCALE, BF16)
        own_values = v_ref[start:stop, :]
        queries, grads = q_ref[start:, :], grad_ref[start:, :]
        grad_keys, grad_values = [], []
        for head, own in enumerate((first, ~first)):
            own_keys = jnp.where(own, keys, jnp.zeros((), BF16))
            scores = times_transposed(own_keys, queries)
            probs = jnp.exp(scores - totals_ref[head : head + 1, start:])
            diagonal = jnp.where(column >= row, probs[:, :tile], 0.0)
            probs = (
                diagonal if stop == length else jnp.concatenate([diagonal, probs[:, tile:]], 1)
            )
            grad_probs = times_transposed(
                jnp.where(own, own_values, jnp.zeros((), BF16)), grads
            )
            grad_scores = (probs * (grad_probs - inner[head : head + 1, start:])).astype(BF16)
            grad_values.append(times(probs.astype(BF16), grads))
            grad_keys.append(times(grad_scores, queries))
            part = contract_rows(grad_scores, own_keys)
            if start == 0 and head == 0:
                sum_q_ref[...] = part
            else:
                sum_q_ref[start:, :] += part
        grad_k_ref[start:stop, :] = (
            jnp.where(first, grad_keys[0], grad_keys[1]) * SCALE
        ).astype(BF16)
        grad_v_ref[start:stop, :] = jnp.where(first, grad_values[0], grad_values[1]).astype(BF16)
    grad_q_ref[...] = sum_q_ref[...].astype(BF16)


def column_spec(length, base, step=1, width=LANES):
    return pl.BlockSpec((length, width), lambda s, p: (s, base + step * p))


def attend_forward(queries, keys, values, places, length, pairs):
    rows = queries.shape[0]
    seqs = rows // length
    return pl.pallas_call(
        functools.partial(attend_forward_kernel, min(512, length)),
        grid=(seqs, pairs),
        in_specs=[column_spec(length, *place) for place in places],
        out_specs=[
            column_spec(length, 0),
            pl.BlockSpec((None, None, 2, length), lambda s, p: (s, p, 0, 0)),
        ],
        out_shape=[
            jax.ShapeDtypeStruct((rows, pairs * LANES), BF16),
            jax.ShapeDtypeStruct((seqs, pairs, 2, length), F32),
        ],
        compiler_params=pltpu.CompilerParams(vmem_limit_bytes=VMEM_BYTES),
        cost_estimate=cost(12 * rows * length * pairs * LANES, 8 * rows * pairs * LANES),
        name="attend_forward",
    )(queries, keys, values)


def attend_backward(queries, keys, values, attended, grads, totals, places, length, at, pairs, together):
    seqs = totals.shape[0]
    rows = seqs * length
    places = [(base + step * at, step) for base, step in places]
    widths = (3 * LANES,) if together else (2 * LANES, LANES)

    def kernel(*refs):
        ins, outs, sum_q_ref = refs[:6], refs[6:-1], refs[-1]
        parts = [outs[0].at[:, :LANES], outs[0].at[:, LANES : 2 * LANES]]
        parts.append(outs[0].at[:, 2 * LANES :] if together else outs[1])
        attend_backward_kernel(min(256, length), *ins, parts, sum_q_ref)

    return pl.pallas_call(
        kernel,
        grid=(seqs, pairs),
        in_specs=[column_spec(length, *place) for place in places]
        + [pl.BlockSpec((None, None, 2, length), lambda s, p: (s, at + p, 0, 0))],
        out_specs=[column_spec(length, 0, 1, w) for w in widths],
        out_shape=[jax.ShapeDtypeStruct((rows, pairs * w), BF16) for w in widths],
        scratch_shapes=[pltpu.VMEM((length, LANES), F32)],
        compiler_params=pltpu.CompilerParams(vmem_limit_bytes=VMEM_BYTES),
        cost_estimate=cost(24 * rows * length * pairs * LANES, 16 * rows * pairs * LANES),
        name="attend_backward",
    )(queries, keys, values, attended, grads, totals)


def after(array, *others):
    others = [o for o in others if o is not None]
    return lax.optimization_barrier((array, *others))[0] if others else array


class Chain:
    def __init__(self, steps):
        self.steps, self.came, self.value, self.left = steps, None, None, True

    def step(self, now):
        try:
            if self.came is None:
                return next(self.steps)
            return self.steps.send([after(c, now) for c in self.came])
        except StopIteration as stop:
            self.value, self.left = stop.value, False
            return []


class Grid:
    def __init__(self, mesh):
        self.dp, halves = mesh.shape["dp"], mesh.shape["seq"]
        assert halves == 2 and self.dp & (self.dp - 1) == 0
        self.bits = self.dp.bit_length()
        self.masks = [1 << b for b in reversed(range(self.bits - 1))]

    def go(self, *chains, now=None, inputs=()):
        moves = [(chain, chain.step(now)) for chain in chains]
        arrays = [after(array, now) for _, some in moves for array, _ in some]
        if inputs and arrays:
            tied = lax.optimization_barrier((*inputs, *arrays))
            inputs, arrays = tied[: len(inputs)], tied[len(inputs) :]
        for chain, some in moves:
            chain.came = [self.swap(arrays[n], mask) for n, (_, mask) in enumerate(some)]
            arrays = arrays[len(some) :]
        return inputs

    def swap(self, array, mask):
        if mask == 0:
            return lax.ppermute(array, "seq", [(0, 1), (1, 0)])
        return lax.ppermute(array, "dp", [(i, i ^ mask) for i in range(self.dp)])

    def end(self, *chains, now=None):
        while any(chain.left for chain in chains):
            self.go(*[chain for chain in chains if chain.left], now=now)
        return [chain.value for chain in chains]

    def bit(self, mask):
        if mask == 0:
            return lax.axis_index("seq")
        return jnp.where(lax.axis_index("dp") & mask, 1, 0)

    def in_pieces(self, rows):
        return (2 * rows) % 16 == 0

    def pair(self, held, came):
        low = self.bit(0) == 0
        return jnp.concatenate([jnp.where(low, held, came), jnp.where(low, came, held)], 1)

    def gather(self, shard, masks):
        if not self.in_pieces(shard.shape[0]):
            return (yield from self.gather_in_order(shard))
        held = shard[None]
        for mask in masks[:-1]:
            (came,) = yield [(held, mask)]
            held = jnp.concatenate([held, came], 0) if mask else self.pair(held, came)
        (came,) = yield [(held, masks[-1])]
        return held, came

    def gather_plane(self, shard, near):
        if not self.in_pieces(shard.shape[0]):
            return (yield from self.gather_in_order(shard))
        held = shard[None]
        for mask in self.masks[:-2]:
            (came,) = yield [(held, mask)]
            held = jnp.concatenate([held, came], 0)
        aside, across = yield [(held, near), (held, 0)]
        cut = held.shape[2] // 2 // LANES * LANES
        left, right = yield [(across[:, :, :cut], near), (aside[:, :, cut:], 0)]
        corner = jnp.concatenate([left, right], 2)
        held = jnp.concatenate([self.pair(held, across), self.pair(aside, corner)], 0)
        (came,) = yield [(held, 1)]
        return held, came

    def flips(self, masks):
        masks = [m for m in masks if m]
        return [
            sum(m for b, m in enumerate(masks) if j >> b & 1) for j in range(1 << len(masks))
        ]

    def gather_in_order(self, shard):
        whole = shard
        for step, mask in enumerate(self.masks + [0]):
            (came,) = yield [(whole, mask)]
            low = self.bit(mask) == 0
            whole = jnp.stack([jnp.where(low, whole, came), jnp.where(low, came, whole)], step)
        return (whole.reshape(-1, shard.shape[-1]),)

    def scatter_sum(self, pieces, masks, direct=False, unsummed=False):
        if len(pieces) == 1:
            return (yield from self.scatter_sum_in_order(pieces[0]))
        keep, away = pieces
        (came,) = yield [(away, 1)]
        for step, mask in enumerate(masks):
            count, rows, columns = keep.shape
            if direct and mask in self.masks[:-2]:
                if mask == self.masks[-3]:
                    far = [m for m in masks if m in self.masks[:-2]][::-1]
                    flips = self.flips(far)
                    moves = [(self.add(keep[j : j + 1], came[j : j + 1]), flips[j]) for j in range(1, count)]
                    keep = self.add(keep[:1], came[:1])
                    several = yield moves
                    came = sum(c.astype(F32) for c in several)
                continue
            if mask:
                parts = [(t[: count // 2], t[count // 2 :]) for t in (keep, came)]
            else:
                parts = [self.part(t) for t in (keep, came)]
            away = self.add(parts[0][1], parts[1][1])
            keep = self.add(parts[0][0], parts[1][0])
            (came,) = yield [(away, mask)]
        return (keep[0], came[0]) if unsummed else self.last_sum(keep[0], came[0])

    def last_sum(self, keep, came):
        def kernel(keep_ref, came_ref, out_ref):
            out_ref[...] = keep_ref[...].astype(F32) + came_ref[...].astype(F32)

        return pl.pallas_call(
            kernel, out_shape=jax.ShapeDtypeStruct(keep.shape, F32), name="last_sum"
        )(keep, came)

    def part(self, array):
        count, rows, columns = array.shape
        split = array.reshape(count, 2, rows // 2, columns)
        seq = self.bit(0)
        return [lax.dynamic_index_in_dim(split, w, 1, keepdims=False) for w in (seq, 1 - seq)]

    def scatter_sum_plane(self, pieces, near):
        if len(pieces) == 1:
            return (yield from self.scatter_sum_in_order(pieces[0]))
        keep, away = pieces
        (came,) = yield [(away, 1)]
        half = keep.shape[0] // 2
        cut = keep.shape[2] // 2 // LANES * LANES
        (own, across), (aside, corner) = (
            [
                self.add(k, c)
                for k, c in zip(self.part(keep[at]), self.part(came[at]), strict=True)
            ]
            for at in (slice(0, half), slice(half, None))
        )
        left, right = yield [(corner[:, :, :cut], near), (corner[:, :, cut:], 0)]
        across = jnp.concatenate([self.add(across[:, :, :cut], left), across[:, :, cut:]], 2)
        aside = jnp.concatenate([aside[:, :, :cut], self.add(aside[:, :, cut:], right)], 2)
        left, right = yield [(aside, near), (across, 0)]
        total = own.astype(F32) + left.astype(F32) + right.astype(F32)
        for mask in self.masks[:-2][::-1]:
            total = total.astype(BF16)
            half = total.shape[0] // 2
            (came,) = yield [(total[half:], mask)]
            total = total[:half].astype(F32) + came.astype(F32)
        return total[0]

    def add(self, left, right):
        return (left.astype(F32) + right.astype(F32)).astype(BF16)

    def scatter_sum_in_order(self, partial):
        rows, columns = partial.shape
        order = self.masks + [0]
        whole = partial.reshape((2,) * self.bits + (rows >> self.bits, columns))
        for step in reversed(range(self.bits)):
            bit = self.bit(order[step])
            away = lax.dynamic_index_in_dim(whole, 1 - bit, step, keepdims=False)
            keep = lax.dynamic_index_in_dim(whole, bit, step, keepdims=False)
            (came,) = yield [(away, order[step])]
            whole = keep.astype(F32) + came.astype(F32)
            if step:
                whole = whole.astype(BF16)
        return whole

    def to_other(self, array):
        count, half, width = array.shape
        seq = self.bit(0)
        split = array.reshape(2, count // 2, half, width)
        keep = lax.dynamic_index_in_dim(split, seq, 0, keepdims=False)
        (came,) = yield [(lax.dynamic_index_in_dim(split, 1 - seq, 0, keepdims=False), 0)]
        return keep.reshape(-1, width), came.reshape(-1, width)

    def to_whole(self, array):
        count, half, width = array.shape
        seq = self.bit(0)
        split = array.reshape(2, count // 2, half, width)
        keep = lax.dynamic_index_in_dim(split, seq, 0, keepdims=False)
        (came,) = yield [(lax.dynamic_index_in_dim(split, 1 - seq, 0, keepdims=False), 0)]
        low = seq == 0
        return jnp.stack(
            [jnp.where(low, keep, came), jnp.where(low, came, keep)], 1
        ).reshape(count * half, width)

    def to_halves(self, array, half):
        width = array.shape[-1]
        seq = self.bit(0)
        split = array.reshape(-1, 2, half, width)
        keep = lax.dynamic_index_in_dim(split, seq, 1, keepdims=False)
        (came,) = yield [(lax.dynamic_index_in_dim(split, 1 - seq, 1, keepdims=False), 0)]
        low = seq == 0
        return jnp.concatenate([jnp.where(low, keep, came), jnp.where(low, came, keep)], 0)


class Weight:
    def __init__(self, grid, rows, *gathered):
        self.arrays, self.groups, self.columns, self.rows = [], [], 0, rows
        for arrays, order in gathered:
            flips = grid.flips(order) if len(arrays) == 2 else None
            self.arrays += arrays
            self.groups.append((flips, self.columns, arrays[0].shape[-1]))
            self.columns += arrays[0].shape[-1]

    @property
    def copies(self):
        return sum(len(flips) if flips else 1 for flips, _, _ in self.groups)

    def specs(self):
        return [pl.BlockSpec(memory_space=pl.ANY)] * len(self.arrays)

    def scratch(self):
        return [
            pltpu.VMEM((self.rows, self.columns), BF16),
            pltpu.SemaphoreType.DMA((self.copies,)),
        ]

    def loads(self, me, refs, whole, sems):
        found, at = [], 0
        for flips, start, columns in self.groups:
            if flips is None:
                found.append((refs[at], whole.at[:, start : start + columns]))
                at += 1
                continue
            half = len(flips) // 2
            rows = self.rows // len(flips)
            for j, flip in enumerate(flips):
                to = pl.multiple_of((me ^ flip) * rows, 16)
                found.append(
                    (
                        refs[at + j // half].at[j % half],
                        whole.at[pl.ds(to, rows), start : start + columns],
                    )
                )
            at += 2
        return [
            pltpu.make_async_copy(source, target, sems.at[n])
            for n, (source, target) in enumerate(found)
        ]


def piece_of(index, me, masks):
    apart = index ^ (me >> 1)
    place = 0
    for mask in masks:
        place = 2 * place + jnp.where(apart & (mask >> 1), 1, 0)
    return place


def normalize(values):
    center = values - jnp.mean(values, -1, keepdims=True)
    spread = jnp.mean(center * center, -1, keepdims=True)
    inverse = lax.rsqrt(spread + EPSILON)
    return center * inverse, inverse


def normalize_back(grad, unit, inverse, gain):
    scaled = grad * gain
    along = jnp.mean(scaled * unit, -1, keepdims=True)
    level = jnp.mean(scaled, -1, keepdims=True)
    return inverse * (scaled - level - unit * along)


GELU_A = (2.0 / 3.141592653589793) ** 0.5
GELU_B = 0.044715


def gelu_both(u):
    square = u * u
    turned = jnp.tanh(u * (GELU_A + (GELU_A * GELU_B) * square))
    half = 0.5 + 0.5 * turned
    slope = half + (0.5 * u) * (1.0 - turned * turned) * (GELU_A + (3 * GELU_A * GELU_B) * square)
    return u * half, slope


def update(gradient, moment, master, average):
    moment_new = MOMENTUM * moment + gradient
    master_new = master - RATE * (gradient + MOMENTUM * moment_new)
    average_new = AVERAGING * average + (1.0 - AVERAGING) * master_new
    return (moment_new, master_new, average_new)


def finish(keep, came, fresh, parameters, norms, layout):
    rows, columns = parameters[0].shape
    many = norms[0].shape[0]

    def kernel(keep_ref, came_ref, fresh_ref, *refs):
        ins, outs = refs[:6], refs[6:]
        for place, is_fresh, block in layout:
            at, to = slice(block * LANES, (block + 1) * LANES), slice(place * LANES, (place + 1) * LANES)
            if is_fresh:
                total = fresh_ref[:, at]
            else:
                total = keep_ref[:, at].astype(F32) + came_ref[:, at].astype(F32)
            for ref, new in zip(outs, update(total, *(r[:, to] for r in ins[:3]))):
                ref[:, to] = new
        last = slice(keep_ref.shape[1] - LANES, keep_ref.shape[1])
        total = (keep_ref[:, last].astype(F32) + came_ref[:, last].astype(F32)).T[:many, :]
        for ref, new in zip(outs[3:], update(total, *(r[...] for r in ins[3:]))):
            ref[...] = new

    return pl.pallas_call(
        kernel,
        out_shape=[jax.ShapeDtypeStruct(a.shape, F32) for a in (*parameters, *norms)],
        name="finish",
    )(keep, came, fresh, *parameters, *norms)


def row_spec(tile, width, again=0):
    return pl.BlockSpec((tile, width), lambda i, me: (i % again if again else i, 0))


def whole_spec(shape):
    return pl.BlockSpec(shape, lambda i, me: (0,) * len(shape))


def row_call(kernel, name, me, tile, rows, ins, weights, outs, flops, scratch=(), give_me=False):
    n_in, n_out = len(ins), len(outs)

    def run(me_ref, *refs):
        at = n_in
        in_refs = refs[:n_in]
        weight_refs = []
        for weight in weights:
            weight_refs.append(refs[at : at + len(weight.arrays)])
            at += len(weight.arrays)
        out_refs = refs[at : at + n_out]
        at += n_out
        held, loads = [], []
        for weight, its in zip(weights, weight_refs, strict=True):
            held.append(refs[at])
            loads.append(weight.loads(me_ref[0], its, refs[at], refs[at + 1]))
            at += 2
        step = pl.program_id(0)

        @pl.when(step == 0)
        def _():
            for some in loads:
                for load in some:
                    load.start()

        def ready(which):
            @pl.when(step == 0)
            def _():
                for load in loads[which]:
                    load.wait()

            return held[which]

        kernel(step, ready, *in_refs, *out_refs, *refs[at:], *([me_ref] if give_me else []))

    moved = sum(a.size * a.dtype.itemsize for a, _ in ins)
    moved += sum(w.rows * w.columns * 2 for w in weights)
    moved += sum(s[0] * s[1] * jnp.dtype(d).itemsize for s, d, _ in outs)
    return pl.pallas_call(
        run,
        grid_spec=pltpu.PrefetchScalarGridSpec(
            num_scalar_prefetch=1,
            grid=(rows // tile,),
            in_specs=[
                whole_spec(a.shape) if whole is True else row_spec(tile, a.shape[1], whole)
                for a, whole in ins
            ]
            + [s for w in weights for s in w.specs()],
            out_specs=[
                whole_spec(shape) if whole else row_spec(tile, shape[1])
                for shape, _, whole in outs
            ],
            scratch_shapes=[s for w in weights for s in w.scratch()] + list(scratch),
        ),
        out_shape=[jax.ShapeDtypeStruct(shape, dtype) for shape, dtype, _ in outs],
        compiler_params=pltpu.CompilerParams(vmem_limit_bytes=VMEM_BYTES),
        cost_estimate=cost(flops, moved),
        name=name,
    )(me, *[a for a, _ in ins], *[x for w in weights for x in w.arrays])


def project(me, own, other, weight):
    rows, width = 2 * own.shape[0], own.shape[1]
    columns = weight.columns - LANES
    tile = 256
    per_half = own.shape[0] // tile

    def kernel(step, ready, own_ref, other_ref, projected_ref, rows_ref, unit_ref, weight_ref, norm_ref, me_ref):
        mine = (step // per_half == me_ref[1]).astype(jnp.int32)
        now = jnp.where(mine == 1, own_ref[...], other_ref[...])
        rows_ref[...] = now
        unit, _ = normalize(now.astype(F32))
        unit_ref[...] = unit.astype(BF16)
        held = ready(0)

        @pl.when(step == 0)
        def _():
            norm_ref[...] = held[:, columns:].astype(F32).T[: norm_ref.shape[0], :]
            weight_ref[...] = held[...]

        normed = (unit * norm_ref[0:1, :] + norm_ref[1:2, :]).astype(BF16)
        projected_ref[...] = times(normed, held[:, :columns]).astype(BF16)

    return row_call(
        kernel,
        "project",
        me,
        tile,
        rows,
        [(own, per_half), (other, per_half)],
        [weight],
        [
            ((rows, columns), BF16, False),
            ((rows, width), BF16, False),
            ((rows, width), BF16, False),
            ((width, weight.columns), BF16, True),
            ((8, width), F32, True),
        ],
        2 * rows * width * columns,
        give_me=True,
    )


def to_hidden(me, attended, rows_in, norm, w_out_up):
    rows, width = rows_in.shape
    hidden = w_out_up.columns - width
    chunk = 768

    part = width // 2

    def kernel(step, ready, one_ref, two_ref, rows_ref, norm_ref, mid_ref, normed_ref, hidden_ref, slope_ref):
        held = ready(0)
        mid = rows_ref[...].astype(F32) + times(one_ref[...], held[:part, :width])
        mid = mid + times(two_ref[...], held[part:, :width])
        mid_ref[...] = mid
        unit, _ = normalize(mid)
        normed = (unit * norm_ref[2:3, :] + norm_ref[3:4, :]).astype(BF16)
        normed_ref[...] = normed
        for at in range(0, hidden, chunk):
            act, slope = gelu_both(times(normed, held[:, width + at : width + at + chunk]))
            hidden_ref[:, at : at + chunk] = act.astype(BF16)
            slope_ref[:, at : at + chunk] = slope.astype(BF16)

    return row_call(
        kernel,
        "to_hidden",
        me,
        256,
        rows,
        [(attended[0], False), (attended[1], False), (rows_in, False), (norm, True)],
        [w_out_up],
        [
            ((rows, width), F32, False),
            ((rows, width), BF16, False),
            ((rows, hidden), BF16, False),
            ((rows, hidden), BF16, False),
        ],
        2 * rows * width * (width + hidden),
    )


def from_hidden(me, hidden, mid_rows, w_down):
    rows, width = mid_rows.shape
    wide = hidden.shape[1]

    def kernel(step, ready, hidden_ref, mid_ref, mixed_ref):
        down = ready(0)
        mixed_ref[...] = (mid_ref[...] + times(hidden_ref[...], down[...])).astype(BF16)

    return row_call(
        kernel,
        "from_hidden",
        me,
        256,
        rows,
        [(hidden, False), (mid_rows, False)],
        [w_down],
        [((rows, width), BF16, False)],
        2 * rows * width * wide,
    )[0]


def hidden_gradient(me, slope, grad_mixed, w_down):
    rows, wide = slope.shape
    width = grad_mixed.shape[1]
    chunk = 768

    def kernel(step, ready, slope_ref, grad_ref, back_ref):
        down = ready(0)
        grad = grad_ref[...]
        for at in range(0, wide, chunk):
            part = times_transposed(grad, down[at : at + chunk, :])
            back_ref[:, at : at + chunk] = (
                part * slope_ref[:, at : at + chunk].astype(F32)
            ).astype(BF16)

    return row_call(
        kernel,
        "hidden_gradient",
        me,
        256,
        rows,
        [(slope, False), (grad_mixed, False)],
        [w_down],
        [((rows, wide), BF16, False)],
        2 * rows * width * wide,
    )[0]


def to_middle(me, grad_hidden, mid_rows, grad_mixed, norm, w_out_up):
    rows, width = mid_rows.shape

    def kernel(step, ready, hidden_ref, mid_ref, grad_ref, norm_ref, dmid_ref, low_ref, do_ref, sums_ref):
        unit, inverse = normalize(mid_ref[...])
        held = ready(0)
        back = times_transposed(hidden_ref[...], held[:, width:])

        @pl.when(step == 0)
        def _():
            sums_ref[...] = jnp.zeros_like(sums_ref)

        sums_ref[0:1, :] += jnp.sum(back * unit, 0, keepdims=True)
        sums_ref[1:2, :] += jnp.sum(back, 0, keepdims=True)
        dmid = grad_ref[...].astype(F32) + normalize_back(back, unit, inverse, norm_ref[2:3, :])
        dmid_ref[...] = dmid
        low = dmid.astype(BF16)
        low_ref[...] = low
        do_ref[...] = times_transposed(low, held[:, :width]).astype(BF16)

    return row_call(
        kernel,
        "to_middle",
        me,
        256,
        rows,
        [(grad_hidden, False), (mid_rows, False), (grad_mixed, False), (norm, True)],
        [w_out_up],
        [
            ((rows, width), F32, False),
            ((rows, width), BF16, False),
            ((rows, width), BF16, False),
            ((8, width), F32, True),
        ],
        2 * rows * width * (width + grad_hidden.shape[1]),
    )


def to_tokens(me, grads, rows_in, grad_mid, norm, w_qkv):
    rows, width = rows_in.shape

    def kernel(step, ready, *refs):
        grad_refs, (rows_ref, dmid_ref, norm_ref, weight_ref, out_ref) = (
            refs[: len(grads)],
            refs[len(grads) :],
        )
        unit, inverse = normalize(rows_ref[...].astype(F32))
        back, at = None, 0
        for ref in grad_refs:
            part = times_transposed(ref[...], weight_ref[:, at : at + ref.shape[1]])
            back = part if back is None else back + part
            at += ref.shape[1]
        out_ref[...] = (
            dmid_ref[...] + normalize_back(back, unit, inverse, norm_ref[0:1, :])
        ).astype(BF16)

    return row_call(
        kernel,
        "to_tokens",
        me,
        256,
        rows,
        [(g, False) for g in grads]
        + [(rows_in, False), (grad_mid, False), (norm, True), (w_qkv, True)],
        [],
        [((rows, width), BF16, False)],
        2 * rows * width * (w_qkv.shape[1] - LANES),
    )[0]


class Norm:
    def __init__(self, weight, column, sums=None, second=None):
        self.weight, self.column, self.sums, self.second = weight, column, sums, second


def rows_gradient(grid, me, lefts, rights, masks, chunk, norm=None):
    lefts = [left if isinstance(left, tuple) else (left,) for left in lefts]
    rows, width = lefts[0][0].shape[0], sum(part.shape[1] for part in lefts[0])
    columns = sum(r.shape[1] for _, r in rights)
    last = len(lefts) - 1
    emit = norm is not None and norm.second is not None
    if not grid.in_pieces(width >> grid.bits):
        parts = []
        if norm:
            column = norm.column
            gain, shift = (norm.weight[:, n - LANES : n - LANES + 1].astype(F32) for n in (0, 1))
            sums = norm.sums if norm.sums is not None else jnp.zeros((width, LANES), F32)
        for n, r in rights:
            product = contract_rows(jnp.concatenate(lefts[n], 1), r)
            if norm and n == last:
                total = jnp.sum(r.astype(F32), 0, keepdims=True)
                own = norm.weight[:, column : column + r.shape[1]].astype(F32)
                column += r.shape[1]
                both = [jnp.sum(own * t, 1, keepdims=True) for t in (product, total)]
                sums = sums + jnp.pad(jnp.concatenate(both, 1), ((0, 0), (0, LANES - 2)))
                product = gain * product + shift * total
            parts.append(product)
        if emit:
            parts.append(sums + jnp.pad(norm.second[:2].T, ((0, 0), (2, LANES - 4))))
        pieces = (jnp.concatenate(parts, 1).astype(BF16),)
        return (pieces, sums) if norm and not emit else pieces
    masks = [m for m in masks if m]
    flat = [part for left in lefts for part in left]
    steps_of = [r.shape[1] // chunk for _, r in rights]
    starts = [sum(steps_of[:n]) for n in range(len(rights))]
    steps = sum(steps_of)
    pairs = grid.dp // 2
    piece = width // grid.dp
    total = columns + (LANES if emit else 0)
    extras, extra_specs = [], []
    if norm:
        first = min(starts[n] for n, (of, _) in enumerate(rights) if of == last)
        extras = [norm.weight]
        extra_specs = [
            whole_spec(norm.weight.shape),
        ]
        for some in (norm.sums, norm.second):
            if some is not None:
                extras.append(some)
                extra_specs.append(whole_spec(some.shape))

    def kernel(me_ref, *refs):
        left_refs, refs = refs[: len(flat)], refs[len(flat) :]
        right_refs, refs = refs[: len(rights)], refs[len(rights) :]
        extra_refs, refs = refs[: len(extras)], refs[len(extras) :]
        keep_ref, away_ref, *refs = refs
        if norm:
            sums_ref, *refs = refs
            weight_ref = extra_refs[0]
        turned_refs = refs
        step = pl.program_id(0)
        device = me_ref[0]
        core = device & 1

        def put(product, at):
            for index in range(pairs):
                place = piece_of(index, device, masks)
                even = product[2 * index * piece : (2 * index + 1) * piece, :]
                odd = product[(2 * index + 1) * piece : (2 * index + 2) * piece, :]
                keep_ref[place, :, at] = jnp.where(core == 0, even, odd).astype(BF16)
                away_ref[place, :, at] = jnp.where(core == 0, odd, even).astype(BF16)

        @pl.when(step == 0)
        def _():
            n = 0
            for left, turned_ref in zip(lefts, turned_refs, strict=True):
                at = 0
                for part in left:
                    turned_ref[at : at + part.shape[1], :] = left_refs[n][...].T
                    at, n = at + part.shape[1], n + 1
            if norm:
                if norm.sums is not None:
                    sums_ref[...] = extra_refs[1][...]
                else:
                    sums_ref[...] = jnp.zeros_like(sums_ref)

        for n, ref in enumerate(right_refs):
            @pl.when((step >= starts[n]) & (step < starts[n] + steps_of[n]))
            def _(n=n, ref=ref):
                product = times(turned_refs[rights[n][0]][...], ref[...])
                if norm and rights[n][0] == last:
                    total = jnp.sum(ref[...].astype(F32), 0, keepdims=True)
                    at = pl.multiple_of(norm.column + (step - first) * chunk, LANES)
                    own = weight_ref[:, pl.ds(at, chunk)].astype(F32)
                    lane = lax.broadcasted_iota(jnp.int32, (1, LANES), 1)
                    sums_ref[...] += jnp.where(
                        lane == 0, jnp.sum(own * product, 1, keepdims=True), 0.0
                    ) + jnp.where(lane == 1, jnp.sum(own * total, 1, keepdims=True), 0.0)
                    param = weight_ref[:, -LANES:].astype(F32)
                    product = param[:, 0:1] * product + param[:, 1:2] * total
                put(product, pl.ds(pl.multiple_of(step * chunk, LANES), chunk))

        if emit:
            @pl.when(step == steps - 1)
            def _():
                second = extra_refs[-1][0:2, :]
                below = jnp.zeros((2, width), F32)
                tail = jnp.zeros((LANES - 4, width), F32)
                put(
                    sums_ref[...] + jnp.concatenate([below, second, tail], 0).T,
                    pl.ds(columns, LANES),
                )

    def right_spec(n):
        return pl.BlockSpec(
            (rows, chunk), lambda i, me: (0, jnp.clip(i - starts[n], 0, steps_of[n] - 1))
        )

    shape = (pairs, piece, total)
    sums_shape = (width, LANES)
    outs = pl.pallas_call(
        kernel,
        grid_spec=pltpu.PrefetchScalarGridSpec(
            num_scalar_prefetch=1,
            grid=(steps,),
            in_specs=[whole_spec(left.shape) for left in flat]
            + [right_spec(n) for n in range(len(rights))]
            + extra_specs,
            out_specs=[whole_spec(shape)] * 2 + [whole_spec(sums_shape)] * bool(norm),
            scratch_shapes=[pltpu.VMEM((width, rows), BF16)] * len(lefts),
        ),
        out_shape=[jax.ShapeDtypeStruct(shape, BF16)] * 2
        + [jax.ShapeDtypeStruct(sums_shape, F32)] * bool(norm),
        compiler_params=pltpu.CompilerParams(vmem_limit_bytes=VMEM_BYTES),
        cost_estimate=cost(2 * rows * width * columns, 2 * (rows * (width + columns) + width * columns)),
        name="rows_gradient",
    )(me, *flat, *[r for _, r in rights], *extras)
    if norm and not emit:
        return outs[:2], outs[2]
    return outs[:2]


def columns_gradient(grid, me, left, right, masks):
    masks = [m for m in masks if m]
    rows, wide = left.shape
    width = right.shape[1]
    piece = wide // grid.dp
    if not grid.in_pieces(wide >> grid.bits) or (2 * piece) % LANES:
        return (contract_rows(left, right).astype(BF16),)
    pairs = grid.dp // 2

    def kernel(me_ref, left_ref, right_ref, keep_ref, away_ref):
        product = contract_rows(left_ref[...], right_ref[...])
        even, odd = product[:piece, :], product[piece:, :]
        core = me_ref[0] & 1
        keep_ref[...] = jnp.where(core == 0, even, odd).astype(BF16)
        away_ref[...] = jnp.where(core == 0, odd, even).astype(BF16)

    out = pl.BlockSpec((None, piece, width), lambda i, me: (piece_of(i, me[0], masks), 0, 0))
    shape = (pairs, piece, width)
    return pl.pallas_call(
        kernel,
        grid_spec=pltpu.PrefetchScalarGridSpec(
            num_scalar_prefetch=1,
            grid=(pairs,),
            in_specs=[
                pl.BlockSpec((rows, 2 * piece), lambda i, me: (0, i)),
                whole_spec(right.shape),
            ],
            out_specs=[out] * 2,
        ),
        out_shape=[jax.ShapeDtypeStruct(shape, BF16)] * 2,
        compiler_params=pltpu.CompilerParams(vmem_limit_bytes=VMEM_BYTES),
        cost_estimate=cost(2 * rows * width * wide, 2 * (rows * (width + wide) + width * wide)),
        name="columns_gradient",
    )(me, left, right)


def body(
    grid,
    tokens,
    first_values,
    cotangent,
    lengths,
    qkv_master,
    qkv_moment,
    qkv_average,
    out_master,
    out_moment,
    out_average,
    up_master,
    up_moment,
    up_average,
    down_master,
    down_moment,
    down_average,
    norm_master,
    norm_moment,
    norm_average,
):
    count, half, width = tokens.shape
    length = 2 * half
    part = width // 2
    norm_columns = norm_master.shape[1]
    assert count == 2
    me = jnp.stack([lax.axis_index("dp"), lax.axis_index("seq")]).astype(jnp.int32)
    far, near = grid.masks[:-2], grid.masks[-2]
    back = far[::-1]
    go, end = grid.go, grid.end
    pairs = width // LANES
    half_pairs = pairs // 2

    fresh_blocks = [n * pairs + p for p in range(half_pairs) for n in range(3)]
    reused_blocks = [n * pairs + p for p in range(half_pairs, pairs) for n in range(2)]

    def blocks(array, which):
        return jnp.concatenate([array[:, n * LANES : (n + 1) * LANES] for n in which], 1)

    fresh_shard = blocks(qkv_master, fresh_blocks).astype(BF16)
    reused_shard = jnp.concatenate(
        [blocks(qkv_master, reused_blocks), jnp.pad(norm_master, ((0, 0), (0, LANES - norm_columns)))], 1
    ).astype(BF16)
    out_up_shard = jnp.concatenate([out_master, up_master], 1).astype(BF16)
    order_fresh, order_reused = [0, *far, near, 1], [0, near, *far, 1]
    order_plane = [*far, near, 1]
    fresh = Chain(grid.gather(fresh_shard, order_fresh))
    reused = Chain(grid.gather(reused_shard, order_reused))
    out_up = Chain(grid.gather_plane(out_up_shard, near))
    down = Chain(grid.gather_plane(down_master.astype(BF16), near))
    tokens_whole = Chain(grid.to_other(tokens))
    values_whole = Chain(grid.to_whole(first_values))
    cotangent_whole = Chain(grid.to_whole(cotangent))
    go(fresh, reused)
    go(tokens_whole)
    go(fresh, reused)
    go(fresh, reused)
    go(out_up)
    go(fresh, reused)
    go(values_whole)
    go(fresh, reused, now=tokens_whole.came[0])
    go(out_up)
    go(cotangent_whole, now=values_whole.came[0])
    fresh_pieces, reused_pieces, (rows_own, rows_other) = end(fresh, reused, tokens_whole)
    w_qkv = Weight(grid, width, (fresh_pieces, order_fresh), (reused_pieces, order_reused))

    projected, rows_in, unit_one, w_qkv, norm = project(me, rows_own, rows_other, w_qkv)
    now = projected
    base = 3 * half_pairs
    one = ((0, 3), (1, 3), (2, 3))
    two = ((base, 2), (base + 1, 2), (0, 1))
    projected, = go(out_up, down, now=now, inputs=(projected,))
    attended_one, totals_one = attend_forward(projected, projected, projected, one, length, half_pairs)
    now = attended_one
    (values_in,) = end(values_whole, now=now)
    values_in, = go(down, now=now, inputs=(values_in,))
    attended_two, totals_two = attend_forward(projected, projected, values_in, two, length, half_pairs)
    now = attended_two
    attended = (attended_one, attended_two)
    go(out_up, now=after(now, *down.came))
    go(out_up)
    attended_two, = go(down, now=now, inputs=(attended_two,))
    (out_up_pieces,) = end(out_up)
    w_out_up = Weight(grid, width, (out_up_pieces, order_plane))
    mid_rows, normed_two, hidden, slope = to_hidden(
        me, (attended_one, attended_two), rows_in, norm, w_out_up
    )
    now = normed_two
    hidden, = go(down, now=now, inputs=(hidden,))
    (whole_cotangent,) = end(cotangent_whole, now=now)
    own_lengths = lax.dynamic_index_in_dim(
        lengths.reshape(2, count // 2), lax.axis_index("seq"), 0, keepdims=False
    )
    position = lax.iota(jnp.int32, length)
    keep_mask = (position[None, :] < own_lengths[:, None]).reshape(-1)
    grad_mixed = jnp.where(keep_mask[:, None], whole_cotangent, jnp.zeros((), BF16))

    back_down, back_up, back_fresh = [near, *back, 0], [0, near, *back], [0, near, *back]
    back_reused = back_down
    grad_down = columns_gradient(grid, me, hidden, grad_mixed, back_down)
    sum_down = Chain(grid.scatter_sum(grad_down, back_down))
    now = grad_down[0]
    slope, = go(down, sum_down, now=now, inputs=(slope,))
    (down_pieces,) = end(down, now=now)
    w_down = Weight(grid, hidden.shape[1], (down_pieces, order_plane))
    grad_hidden = hidden_gradient(me, slope, grad_mixed, w_down)
    now = grad_hidden
    grad_hidden, = go(sum_down, now=now, inputs=(grad_hidden,))
    grad_up = rows_gradient(grid, me, [normed_two], [(0, grad_hidden)], back_up, 768)
    now = grad_up[0]
    sum_up = Chain(grid.scatter_sum(grad_up, back_up))
    hidden, = go(sum_up, now=now, inputs=(hidden,))
    mixed = from_hidden(me, hidden, mid_rows, w_down)
    now = mixed
    mixed_halves = Chain(grid.to_halves(mixed, half))
    grad_hidden, = go(sum_up, now=now, inputs=(grad_hidden,))
    grad_mid, grad_mid_low, grad_attended, sums_two = to_middle(
        me, grad_hidden, mid_rows, grad_mixed, norm, w_out_up
    )
    now = grad_attended

    def attend_back(which, at, many):
        values = values_in if which else projected
        return attend_backward(
            projected, projected, values, attended[which], grad_attended,
            totals_two if which else totals_one,
            (*(two if which else one), (0, 1), (which * half_pairs, 1)),
            length, at, many, not which,
        )

    grad_attended, = go(sum_down, mixed_halves, now=now, inputs=(grad_attended,))
    (grad_one,) = attend_back(0, 0, 1)
    now = grad_one
    grad_attended, = go(sum_up, now=now, inputs=(grad_attended,))
    (grad_two,) = attend_back(0, 1, 2)
    now = grad_two
    grad_two, = go(sum_down, sum_up, now=now, inputs=(grad_two,))
    grad_fresh, sums_one = rows_gradient(
        grid, me, [attended, unit_one], [(0, grad_mid_low), (1, grad_one), (1, grad_two)],
        back_fresh, 384, Norm(w_qkv, 0),
    )
    now = grad_fresh[0]
    sum_fresh = Chain(grid.scatter_sum(grad_fresh, back_fresh))
    grad_attended, = go(sum_fresh, sum_down, sum_up, now=now, inputs=(grad_attended,))
    grad_three, value_three = attend_back(1, 0, 1)
    now = grad_three
    grad_attended, = go(sum_fresh, now=now, inputs=(grad_attended,))
    grad_four, value_four = attend_back(1, 1, 2)
    now = grad_four
    grad_four, = go(sum_fresh, now=now, inputs=(grad_four,))
    grad_reused = rows_gradient(
        grid, me, [unit_one], [(0, grad_three), (0, grad_four)], back_reused, 256,
        Norm(w_qkv, 3 * part, sums_one, sums_two),
    )
    now = grad_reused[0]
    pieces = len(grad_reused) > 1
    sum_reused = Chain(grid.scatter_sum(grad_reused, back_reused, pieces, pieces))
    first_halves = Chain(grid.to_halves(jnp.concatenate([value_three, value_four], 1), half))
    go(sum_reused, now=now)
    grad_four, = go(sum_reused, inputs=(grad_four,))
    grad_four, = go(first_halves, sum_fresh, inputs=(grad_four,))
    tokens_grad = to_tokens(
        me, [grad_one, grad_two, grad_three, grad_four], rows_in, grad_mid, norm, w_qkv
    )
    now = tokens_grad
    tokens_halves = Chain(grid.to_halves(tokens_grad, half))
    go(sum_reused, now=now)
    go(tokens_halves, sum_fresh, now=now)
    sum_up, sum_down, mixed = end(sum_up, sum_down, mixed_halves, now=now)
    sum_reused, sum_fresh, tokens_grad, first_grad = end(
        sum_reused, sum_fresh, tokens_halves, first_halves
    )
    sum_out, sum_fresh = sum_fresh[:, :width], sum_fresh[:, width:]
    qkv = (qkv_moment, qkv_master, qkv_average)
    norms = (norm_moment, norm_master, norm_average)
    layout = [(place, True, n) for n, place in enumerate(fresh_blocks)]
    layout += [(place, False, n) for n, place in enumerate(reused_blocks)]
    if pieces:
        *qkv_new, one, two, three = finish(
            *sum_reused, sum_fresh, qkv, tuple(n.T for n in norms), layout
        )
        norm_new = (one.T, two.T, three.T)
    else:
        both = {
            place: (sum_fresh if is_fresh else sum_reused)[:, n * LANES : (n + 1) * LANES]
            for place, is_fresh, n in layout
        }
        qkv_new = update(jnp.concatenate([both[n] for n in range(len(both))], 1), *qkv)
        norm_new = update(sum_reused[:, 2 * part : 2 * part + norm_columns], *norms)
    return (
        mixed,
        tokens_grad,
        first_grad,
        *qkv_new,
        *update(sum_out, out_moment, out_master, out_average),
        *update(sum_up, up_moment, up_master, up_average),
        *update(sum_down, down_moment, down_master, down_average),
        *norm_new,
    )


def solution(mesh):
    activation = P("dp", "seq", None)
    parameter = P(("dp", "seq"), None)
    return jax.shard_map(
        functools.partial(body, Grid(mesh)),
        mesh=mesh,
        in_specs=(activation,) * 3 + (P("dp"),) + (parameter,) * 15,
        out_specs=(activation,) * 3 + (parameter,) * 15,
        check_vma=False,
    )
```

```python
import functools

import jax
import jax.numpy as jnp
from jax import lax
from jax.experimental import pallas as pl
from jax.experimental.pallas import tpu as pltpu
from jax.sharding import PartitionSpec as P

HEAD_DIM = 64
LANES = 128
EPSILON = 1e-05
MOMENTUM = 0.5
AVERAGING = 0.5
RATE = 0.0006
SCALE = HEAD_DIM ** (-0.5)
VMEM_BYTES = 24 << 20

BF16 = jnp.bfloat16
F32 = jnp.float32


def cost(flops, moved):
    return pl.CostEstimate(
        flops=int(flops) // 8, bytes_accessed=int(moved) // 8, transcendentals=0
    )


def times_transposed(left, right):
    return lax.dot_general(left, right, (((1,), (1,)), ((), ())), preferred_element_type=F32)


def times(left, right):
    return lax.dot_general(left, right, (((1,), (0,)), ((), ())), preferred_element_type=F32)


def contract_rows(left, right):
    return lax.dot_general(left, right, (((0,), (0,)), ((), ())), preferred_element_type=F32)


def attend_forward_kernel(tile, q_ref, k_ref, v_ref, out_ref, totals_ref):
    length = q_ref.shape[0]
    first = lax.broadcasted_iota(jnp.int32, (1, LANES), 1) < HEAD_DIM
    row = lax.broadcasted_iota(jnp.int32, (tile, tile), 0)
    column = lax.broadcasted_iota(jnp.int32, (tile, tile), 1)
    for block in range(length // tile):
        start, stop = block * tile, (block + 1) * tile
        queries = q_ref[start:stop, :] * jnp.asarray(SCALE, BF16)
        outputs, totals = [], []
        for own in (first, ~first):
            scores = times_transposed(
                jnp.where(own, queries, jnp.zeros((), BF16)), k_ref[:stop, :]
            )
            diagonal = jnp.where(row >= column, scores[:, start:], -1e30)
            scores = (
                diagonal if block == 0 else jnp.concatenate([scores[:, :start], diagonal], 1)
            )
            maximum = jnp.max(scores, 1, keepdims=True)
            weights = jnp.exp(scores - maximum)
            summed = jnp.sum(weights, 1, keepdims=True)
            outputs.append(times(weights.astype(BF16), v_ref[:stop, :]) * (1.0 / summed))
            totals.append(maximum + jnp.log(summed))
        out_ref[start:stop, :] = jnp.where(first, outputs[0], outputs[1]).astype(BF16)
        turned = jnp.where(first, totals[0], totals[1]).T
        totals_ref[0:1, start:stop] = turned[0:1, :]
        totals_ref[1:2, start:stop] = turned[HEAD_DIM : HEAD_DIM + 1, :]


def attend_backward_kernel(
    tile, q_ref, k_ref, v_ref, out_ref, grad_ref, totals_ref, grad_refs, sum_q_ref
):
    grad_q_ref, grad_k_ref, grad_v_ref = grad_refs
    length = q_ref.shape[0]
    first = lax.broadcasted_iota(jnp.int32, (1, LANES), 1) < HEAD_DIM
    head_of_lane = lax.broadcasted_iota(jnp.int32, (8, LANES), 1) // HEAD_DIM
    pick = jnp.where(
        head_of_lane == lax.broadcasted_iota(jnp.int32, (8, LANES), 0), 1.0, 0.0
    ).astype(BF16)
    product = out_ref[...].astype(F32) * grad_ref[...].astype(F32)
    coarse = product.astype(BF16)
    fine = (product - coarse.astype(F32)).astype(BF16)
    inner = times_transposed(pick, coarse) + times_transposed(pick, fine)
    row = lax.broadcasted_iota(jnp.int32, (tile, tile), 0)
    column = lax.broadcasted_iota(jnp.int32, (tile, tile), 1)
    for start in range(0, length, tile):
        stop = start + tile
        keys = k_ref[start:stop, :] * jnp.asarray(SCALE, BF16)
        own_values = v_ref[start:stop, :]
        queries, grads = q_ref[start:, :], grad_ref[start:, :]
        grad_keys, grad_values = [], []
        for head, own in enumerate((first, ~first)):
            own_keys = jnp.where(own, keys, jnp.zeros((), BF16))
            scores = times_transposed(own_keys, queries)
            probs = jnp.exp(scores - totals_ref[head : head + 1, start:])
            diagonal = jnp.where(column >= row, probs[:, :tile], 0.0)
            probs = (
                diagonal if stop == length else jnp.concatenate([diagonal, probs[:, tile:]], 1)
            )
            grad_probs = times_transposed(
                jnp.where(own, own_values, jnp.zeros((), BF16)), grads
            )
            grad_scores = (probs * (grad_probs - inner[head : head + 1, start:])).astype(BF16)
            grad_values.append(times(probs.astype(BF16), grads))
            grad_keys.append(times(grad_scores, queries))
            part = contract_rows(grad_scores, own_keys)
            if start == 0 and head == 0:
                sum_q_ref[...] = part
            else:
                sum_q_ref[start:, :] += part
        grad_k_ref[start:stop, :] = (
            jnp.where(first, grad_keys[0], grad_keys[1]) * SCALE
        ).astype(BF16)
        grad_v_ref[start:stop, :] = jnp.where(first, grad_values[0], grad_values[1]).astype(BF16)
    grad_q_ref[...] = sum_q_ref[...].astype(BF16)


def column_spec(length, base, step=1, width=LANES):
    return pl.BlockSpec((length, width), lambda s, p: (s, base + step * p))


def attend_forward(queries, keys, values, places, length, pairs):
    rows = queries.shape[0]
    seqs = rows // length
    return pl.pallas_call(
        functools.partial(attend_forward_kernel, min(512, length)),
        grid=(seqs, pairs),
        in_specs=[column_spec(length, *place) for place in places],
        out_specs=[
            column_spec(length, 0),
            pl.BlockSpec((None, None, 2, length), lambda s, p: (s, p, 0, 0)),
        ],
        out_shape=[
            jax.ShapeDtypeStruct((rows, pairs * LANES), BF16),
            jax.ShapeDtypeStruct((seqs, pairs, 2, length), F32),
        ],
        compiler_params=pltpu.CompilerParams(vmem_limit_bytes=VMEM_BYTES),
        cost_estimate=cost(12 * rows * length * pairs * LANES, 8 * rows * pairs * LANES),
        name="attend_forward",
    )(queries, keys, values)


def attend_backward(queries, keys, values, attended, grads, totals, places, length, at, pairs, together):
    seqs = totals.shape[0]
    rows = seqs * length
    places = [(base + step * at, step) for base, step in places]
    widths = (3 * LANES,) if together else (2 * LANES, LANES)

    def kernel(*refs):
        ins, outs, sum_q_ref = refs[:6], refs[6:-1], refs[-1]
        parts = [outs[0].at[:, :LANES], outs[0].at[:, LANES : 2 * LANES]]
        parts.append(outs[0].at[:, 2 * LANES :] if together else outs[1])
        attend_backward_kernel(min(256, length), *ins, parts, sum_q_ref)

    return pl.pallas_call(
        kernel,
        grid=(seqs, pairs),
        in_specs=[column_spec(length, *place) for place in places]
        + [pl.BlockSpec((None, None, 2, length), lambda s, p: (s, at + p, 0, 0))],
        out_specs=[column_spec(length, 0, 1, w) for w in widths],
        out_shape=[jax.ShapeDtypeStruct((rows, pairs * w), BF16) for w in widths],
        scratch_shapes=[pltpu.VMEM((length, LANES), F32)],
        compiler_params=pltpu.CompilerParams(vmem_limit_bytes=VMEM_BYTES),
        cost_estimate=cost(24 * rows * length * pairs * LANES, 16 * rows * pairs * LANES),
        name="attend_backward",
    )(queries, keys, values, attended, grads, totals)


def after(array, *others):
    others = [o for o in others if o is not None]
    return lax.optimization_barrier((array, *others))[0] if others else array


class Chain:
    def __init__(self, steps):
        self.steps, self.came, self.value, self.left = steps, None, None, True

    def step(self, now):
        try:
            if self.came is None:
                return next(self.steps)
            return self.steps.send([after(c, now) for c in self.came])
        except StopIteration as stop:
            self.value, self.left = stop.value, False
            return []


class Grid:
    def __init__(self, mesh):
        self.dp, halves = mesh.shape["dp"], mesh.shape["seq"]
        assert halves == 2 and self.dp & (self.dp - 1) == 0
        self.bits = self.dp.bit_length()
        self.masks = [1 << b for b in reversed(range(self.bits - 1))]

    def go(self, *chains, now=None, inputs=()):
        moves = [(chain, chain.step(now)) for chain in chains]
        arrays = [after(array, now) for _, some in moves for array, _ in some]
        if inputs and arrays:
            tied = lax.optimization_barrier((*inputs, *arrays))
            inputs, arrays = tied[: len(inputs)], tied[len(inputs) :]
        for chain, some in moves:
            chain.came = [self.swap(arrays[n], mask) for n, (_, mask) in enumerate(some)]
            arrays = arrays[len(some) :]
        return inputs

    def swap(self, array, mask):
        if mask == 0:
            return lax.ppermute(array, "seq", [(0, 1), (1, 0)])
        return lax.ppermute(array, "dp", [(i, i ^ mask) for i in range(self.dp)])

    def end(self, *chains, now=None):
        while any(chain.left for chain in chains):
            self.go(*[chain for chain in chains if chain.left], now=now)
        return [chain.value for chain in chains]

    def bit(self, mask):
        if mask == 0:
            return lax.axis_index("seq")
        return jnp.where(lax.axis_index("dp") & mask, 1, 0)

    def in_pieces(self, rows):
        return (2 * rows) % 16 == 0

    def pair(self, held, came):
        low = self.bit(0) == 0
        return jnp.concatenate([jnp.where(low, held, came), jnp.where(low, came, held)], 1)

    def gather(self, shard, masks):
        if not self.in_pieces(shard.shape[0]):
            return (yield from self.gather_in_order(shard))
        held = shard[None]
        for mask in masks[:-1]:
            (came,) = yield [(held, mask)]
            held = jnp.concatenate([held, came], 0) if mask else self.pair(held, came)
        (came,) = yield [(held, masks[-1])]
        return held, came

    def gather_plane(self, shard, near):
        if not self.in_pieces(shard.shape[0]):
            return (yield from self.gather_in_order(shard))
        held = shard[None]
        for mask in self.masks[:-2]:
            (came,) = yield [(held, mask)]
            held = jnp.concatenate([held, came], 0)
        aside, across = yield [(held, near), (held, 0)]
        cut = held.shape[2] // 2 // LANES * LANES
        left, right = yield [(across[:, :, :cut], near), (aside[:, :, cut:], 0)]
        corner = jnp.concatenate([left, right], 2)
        held = jnp.concatenate([self.pair(held, across), self.pair(aside, corner)], 0)
        (came,) = yield [(held, 1)]
        return held, came

    def flips(self, masks):
        masks = [m for m in masks if m]
        return [
            sum(m for b, m in enumerate(masks) if j >> b & 1) for j in range(1 << len(masks))
        ]

    def gather_in_order(self, shard):
        whole = shard
        for step, mask in enumerate(self.masks + [0]):
            (came,) = yield [(whole, mask)]
            low = self.bit(mask) == 0
            whole = jnp.stack([jnp.where(low, whole, came), jnp.where(low, came, whole)], step)
        return (whole.reshape(-1, shard.shape[-1]),)

    def scatter_sum(self, pieces, masks, direct=False, unsummed=False):
        if len(pieces) == 1:
            return (yield from self.scatter_sum_in_order(pieces[0]))
        keep, away = pieces
        (came,) = yield [(away, 1)]
        for step, mask in enumerate(masks):
            count, rows, columns = keep.shape
            if direct and mask in self.masks[:-2]:
                if mask == self.masks[-3]:
                    far = [m for m in masks if m in self.masks[:-2]][::-1]
                    flips = self.flips(far)
                    moves = [(self.add(keep[j : j + 1], came[j : j + 1]), flips[j]) for j in range(1, count)]
                    keep = self.add(keep[:1], came[:1])
                    several = yield moves
                    came = sum(c.astype(F32) for c in several)
                continue
            if mask:
                parts = [(t[: count // 2], t[count // 2 :]) for t in (keep, came)]
            else:
                parts = [self.part(t) for t in (keep, came)]
            away = self.add(parts[0][1], parts[1][1])
            keep = self.add(parts[0][0], parts[1][0])
            (came,) = yield [(away, mask)]
        return (keep[0], came[0]) if unsummed else keep[0].astype(F32) + came[0].astype(F32)

    def part(self, array):
        count, rows, columns = array.shape
        split = array.reshape(count, 2, rows // 2, columns)
        seq = self.bit(0)
        return [lax.dynamic_index_in_dim(split, w, 1, keepdims=False) for w in (seq, 1 - seq)]

    def scatter_sum_plane(self, pieces, near):
        if len(pieces) == 1:
            return (yield from self.scatter_sum_in_order(pieces[0]))
        keep, away = pieces
        (came,) = yield [(away, 1)]
        half = keep.shape[0] // 2
        cut = keep.shape[2] // 2 // LANES * LANES
        (own, across), (aside, corner) = (
            [
                self.add(k, c)
                for k, c in zip(self.part(keep[at]), self.part(came[at]), strict=True)
            ]
            for at in (slice(0, half), slice(half, None))
        )
        left, right = yield [(corner[:, :, :cut], near), (corner[:, :, cut:], 0)]
        across = jnp.concatenate([self.add(across[:, :, :cut], left), across[:, :, cut:]], 2)
        aside = jnp.concatenate([aside[:, :, :cut], self.add(aside[:, :, cut:], right)], 2)
        left, right = yield [(aside, near), (across, 0)]
        total = own.astype(F32) + left.astype(F32) + right.astype(F32)
        for mask in self.masks[:-2][::-1]:
            total = total.astype(BF16)
            half = total.shape[0] // 2
            (came,) = yield [(total[half:], mask)]
            total = total[:half].astype(F32) + came.astype(F32)
        return total[0]

    def add(self, left, right):
        return (left.astype(F32) + right.astype(F32)).astype(BF16)

    def scatter_sum_in_order(self, partial):
        rows, columns = partial.shape
        order = self.masks + [0]
        whole = partial.reshape((2,) * self.bits + (rows >> self.bits, columns))
        for step in reversed(range(self.bits)):
            bit = self.bit(order[step])
            away = lax.dynamic_index_in_dim(whole, 1 - bit, step, keepdims=False)
            keep = lax.dynamic_index_in_dim(whole, bit, step, keepdims=False)
            (came,) = yield [(away, order[step])]
            whole = keep.astype(F32) + came.astype(F32)
            if step:
                whole = whole.astype(BF16)
        return whole

    def to_other(self, array):
        count, half, width = array.shape
        seq = self.bit(0)
        split = array.reshape(2, count // 2, half, width)
        keep = lax.dynamic_index_in_dim(split, seq, 0, keepdims=False)
        (came,) = yield [(lax.dynamic_index_in_dim(split, 1 - seq, 0, keepdims=False), 0)]
        return keep.reshape(-1, width), came.reshape(-1, width)

    def to_whole(self, array):
        count, half, width = array.shape
        seq = self.bit(0)
        split = array.reshape(2, count // 2, half, width)
        keep = lax.dynamic_index_in_dim(split, seq, 0, keepdims=False)
        (came,) = yield [(lax.dynamic_index_in_dim(split, 1 - seq, 0, keepdims=False), 0)]
        low = seq == 0
        return jnp.stack(
            [jnp.where(low, keep, came), jnp.where(low, came, keep)], 1
        ).reshape(count * half, width)

    def to_halves(self, array, half):
        width = array.shape[-1]
        seq = self.bit(0)
        split = array.reshape(-1, 2, half, width)
        keep = lax.dynamic_index_in_dim(split, seq, 1, keepdims=False)
        (came,) = yield [(lax.dynamic_index_in_dim(split, 1 - seq, 1, keepdims=False), 0)]
        low = seq == 0
        return jnp.concatenate([jnp.where(low, keep, came), jnp.where(low, came, keep)], 0)


class Weight:
    def __init__(self, grid, rows, *gathered):
        self.arrays, self.groups, self.columns, self.rows = [], [], 0, rows
        for arrays, order in gathered:
            flips = grid.flips(order) if len(arrays) == 2 else None
            self.arrays += arrays
            self.groups.append((flips, self.columns, arrays[0].shape[-1]))
            self.columns += arrays[0].shape[-1]

    @property
    def copies(self):
        return sum(len(flips) if flips else 1 for flips, _, _ in self.groups)

    def specs(self):
        return [pl.BlockSpec(memory_space=pl.ANY)] * len(self.arrays)

    def scratch(self):
        return [
            pltpu.VMEM((self.rows, self.columns), BF16),
            pltpu.SemaphoreType.DMA((self.copies,)),
        ]

    def loads(self, me, refs, whole, sems):
        found, at = [], 0
        for flips, start, columns in self.groups:
            if flips is None:
                found.append((refs[at], whole.at[:, start : start + columns]))
                at += 1
                continue
            half = len(flips) // 2
            rows = self.rows // len(flips)
            for j, flip in enumerate(flips):
                to = pl.multiple_of((me ^ flip) * rows, 16)
                found.append(
                    (
                        refs[at + j // half].at[j % half],
                        whole.at[pl.ds(to, rows), start : start + columns],
                    )
                )
            at += 2
        return [
            pltpu.make_async_copy(source, target, sems.at[n])
            for n, (source, target) in enumerate(found)
        ]


def piece_of(index, me, masks):
    apart = index ^ (me >> 1)
    place = 0
    for mask in masks:
        place = 2 * place + jnp.where(apart & (mask >> 1), 1, 0)
    return place


def normalize(values):
    center = values - jnp.mean(values, -1, keepdims=True)
    spread = jnp.mean(center * center, -1, keepdims=True)
    inverse = lax.rsqrt(spread + EPSILON)
    return center * inverse, inverse


def normalize_back(grad, unit, inverse, gain):
    scaled = grad * gain
    along = jnp.mean(scaled * unit, -1, keepdims=True)
    level = jnp.mean(scaled, -1, keepdims=True)
    return inverse * (scaled - level - unit * along)


GELU_A = (2.0 / 3.141592653589793) ** 0.5
GELU_B = 0.044715


def gelu_both(u):
    square = u * u
    turned = jnp.tanh(u * (GELU_A + (GELU_A * GELU_B) * square))
    half = 0.5 + 0.5 * turned
    slope = half + (0.5 * u) * (1.0 - turned * turned) * (GELU_A + (3 * GELU_A * GELU_B) * square)
    return u * half, slope


def update(gradient, moment, master, average):
    moment_new = MOMENTUM * moment + gradient
    master_new = master - RATE * (gradient + MOMENTUM * moment_new)
    average_new = AVERAGING * average + (1.0 - AVERAGING) * master_new
    return (moment_new, master_new, average_new)


def finish(keep, came, fresh, parameters, norms, layout):
    rows, columns = parameters[0].shape
    many = norms[0].shape[0]

    def kernel(keep_ref, came_ref, fresh_ref, *refs):
        ins, outs = refs[:6], refs[6:]
        for place, is_fresh, block in layout:
            at, to = slice(block * LANES, (block + 1) * LANES), slice(place * LANES, (place + 1) * LANES)
            if is_fresh:
                total = fresh_ref[:, at]
            else:
                total = keep_ref[:, at].astype(F32) + came_ref[:, at].astype(F32)
            for ref, new in zip(outs, update(total, *(r[:, to] for r in ins[:3]))):
                ref[:, to] = new
        last = slice(keep_ref.shape[1] - LANES, keep_ref.shape[1])
        total = (keep_ref[:, last].astype(F32) + came_ref[:, last].astype(F32)).T[:many, :]
        for ref, new in zip(outs[3:], update(total, *(r[...] for r in ins[3:]))):
            ref[...] = new

    return pl.pallas_call(
        kernel,
        out_shape=[jax.ShapeDtypeStruct(a.shape, F32) for a in (*parameters, *norms)],
        name="finish",
    )(keep, came, fresh, *parameters, *norms)


def row_spec(tile, width, again=0):
    return pl.BlockSpec((tile, width), lambda i, me: (i % again if again else i, 0))


def whole_spec(shape):
    return pl.BlockSpec(shape, lambda i, me: (0,) * len(shape))


def row_call(kernel, name, me, tile, rows, ins, weights, outs, flops, scratch=(), give_me=False):
    n_in, n_out = len(ins), len(outs)

    def run(me_ref, *refs):
        at = n_in
        in_refs = refs[:n_in]
        weight_refs = []
        for weight in weights:
            weight_refs.append(refs[at : at + len(weight.arrays)])
            at += len(weight.arrays)
        out_refs = refs[at : at + n_out]
        at += n_out
        held, loads = [], []
        for weight, its in zip(weights, weight_refs, strict=True):
            held.append(refs[at])
            loads.append(weight.loads(me_ref[0], its, refs[at], refs[at + 1]))
            at += 2
        step = pl.program_id(0)

        @pl.when(step == 0)
        def _():
            for some in loads:
                for load in some:
                    load.start()

        def ready(which):
            @pl.when(step == 0)
            def _():
                for load in loads[which]:
                    load.wait()

            return held[which]

        kernel(step, ready, *in_refs, *out_refs, *refs[at:], *([me_ref] if give_me else []))

    moved = sum(a.size * a.dtype.itemsize for a, _ in ins)
    moved += sum(w.rows * w.columns * 2 for w in weights)
    moved += sum(s[0] * s[1] * jnp.dtype(d).itemsize for s, d, _ in outs)
    return pl.pallas_call(
        run,
        grid_spec=pltpu.PrefetchScalarGridSpec(
            num_scalar_prefetch=1,
            grid=(rows // tile,),
            in_specs=[
                whole_spec(a.shape) if whole is True else row_spec(tile, a.shape[1], whole)
                for a, whole in ins
            ]
            + [s for w in weights for s in w.specs()],
            out_specs=[
                whole_spec(shape) if whole else row_spec(tile, shape[1])
                for shape, _, whole in outs
            ],
            scratch_shapes=[s for w in weights for s in w.scratch()] + list(scratch),
        ),
        out_shape=[jax.ShapeDtypeStruct(shape, dtype) for shape, dtype, _ in outs],
        compiler_params=pltpu.CompilerParams(vmem_limit_bytes=VMEM_BYTES),
        cost_estimate=cost(flops, moved),
        name=name,
    )(me, *[a for a, _ in ins], *[x for w in weights for x in w.arrays])


def project(me, own, other, weight):
    rows, width = 2 * own.shape[0], own.shape[1]
    columns = weight.columns - LANES
    tile = 256
    per_half = own.shape[0] // tile

    def kernel(step, ready, own_ref, other_ref, projected_ref, rows_ref, unit_ref, weight_ref, norm_ref, me_ref):
        mine = (step // per_half == me_ref[1]).astype(jnp.int32)
        now = jnp.where(mine == 1, own_ref[...], other_ref[...])
        rows_ref[...] = now
        unit, _ = normalize(now.astype(F32))
        unit_ref[...] = unit.astype(BF16)
        held = ready(0)

        @pl.when(step == 0)
        def _():
            norm_ref[...] = held[:, columns:].astype(F32).T[: norm_ref.shape[0], :]
            weight_ref[...] = held[...]

        normed = (unit * norm_ref[0:1, :] + norm_ref[1:2, :]).astype(BF16)
        projected_ref[...] = times(normed, held[:, :columns]).astype(BF16)

    return row_call(
        kernel,
        "project",
        me,
        tile,
        rows,
        [(own, per_half), (other, per_half)],
        [weight],
        [
            ((rows, columns), BF16, False),
            ((rows, width), BF16, False),
            ((rows, width), BF16, False),
            ((width, weight.columns), BF16, True),
            ((8, width), F32, True),
        ],
        2 * rows * width * columns,
        give_me=True,
    )


def to_hidden(me, attended, rows_in, norm, w_out_up):
    rows, width = rows_in.shape
    hidden = w_out_up.columns - width
    chunk = 768

    part = width // 2

    def kernel(step, ready, one_ref, two_ref, rows_ref, norm_ref, mid_ref, normed_ref, hidden_ref, slope_ref):
        held = ready(0)
        mid = rows_ref[...].astype(F32) + times(one_ref[...], held[:part, :width])
        mid = mid + times(two_ref[...], held[part:, :width])
        mid_ref[...] = mid
        unit, _ = normalize(mid)
        normed = (unit * norm_ref[2:3, :] + norm_ref[3:4, :]).astype(BF16)
        normed_ref[...] = normed
        for at in range(0, hidden, chunk):
            act, slope = gelu_both(times(normed, held[:, width + at : width + at + chunk]))
            hidden_ref[:, at : at + chunk] = act.astype(BF16)
            slope_ref[:, at : at + chunk] = slope.astype(BF16)

    return row_call(
        kernel,
        "to_hidden",
        me,
        256,
        rows,
        [(attended[0], False), (attended[1], False), (rows_in, False), (norm, True)],
        [w_out_up],
        [
            ((rows, width), F32, False),
            ((rows, width), BF16, False),
            ((rows, hidden), BF16, False),
            ((rows, hidden), BF16, False),
        ],
        2 * rows * width * (width + hidden),
    )


def from_hidden(me, hidden, mid_rows, w_down):
    rows, width = mid_rows.shape
    wide = hidden.shape[1]

    def kernel(step, ready, hidden_ref, mid_ref, mixed_ref):
        down = ready(0)
        mixed_ref[...] = (mid_ref[...] + times(hidden_ref[...], down[...])).astype(BF16)

    return row_call(
        kernel,
        "from_hidden",
        me,
        256,
        rows,
        [(hidden, False), (mid_rows, False)],
        [w_down],
        [((rows, width), BF16, False)],
        2 * rows * width * wide,
    )[0]


def hidden_gradient(me, slope, grad_mixed, w_down):
    rows, wide = slope.shape
    width = grad_mixed.shape[1]
    chunk = 768

    def kernel(step, ready, slope_ref, grad_ref, back_ref):
        down = ready(0)
        grad = grad_ref[...]
        for at in range(0, wide, chunk):
            part = times_transposed(grad, down[at : at + chunk, :])
            back_ref[:, at : at + chunk] = (
                part * slope_ref[:, at : at + chunk].astype(F32)
            ).astype(BF16)

    return row_call(
        kernel,
        "hidden_gradient",
        me,
        256,
        rows,
        [(slope, False), (grad_mixed, False)],
        [w_down],
        [((rows, wide), BF16, False)],
        2 * rows * width * wide,
    )[0]


def to_middle(me, grad_hidden, mid_rows, grad_mixed, norm, w_out_up):
    rows, width = mid_rows.shape

    def kernel(step, ready, hidden_ref, mid_ref, grad_ref, norm_ref, dmid_ref, low_ref, do_ref, sums_ref):
        unit, inverse = normalize(mid_ref[...])
        held = ready(0)
        back = times_transposed(hidden_ref[...], held[:, width:])

        @pl.when(step == 0)
        def _():
            sums_ref[...] = jnp.zeros_like(sums_ref)

        sums_ref[0:1, :] += jnp.sum(back * unit, 0, keepdims=True)
        sums_ref[1:2, :] += jnp.sum(back, 0, keepdims=True)
        dmid = grad_ref[...].astype(F32) + normalize_back(back, unit, inverse, norm_ref[2:3, :])
        dmid_ref[...] = dmid
        low = dmid.astype(BF16)
        low_ref[...] = low
        do_ref[...] = times_transposed(low, held[:, :width]).astype(BF16)

    return row_call(
        kernel,
        "to_middle",
        me,
        256,
        rows,
        [(grad_hidden, False), (mid_rows, False), (grad_mixed, False), (norm, True)],
        [w_out_up],
        [
            ((rows, width), F32, False),
            ((rows, width), BF16, False),
            ((rows, width), BF16, False),
            ((8, width), F32, True),
        ],
        2 * rows * width * (width + grad_hidden.shape[1]),
    )


def to_tokens(me, grads, rows_in, grad_mid, norm, w_qkv):
    rows, width = rows_in.shape

    def kernel(step, ready, *refs):
        grad_refs, (rows_ref, dmid_ref, norm_ref, weight_ref, out_ref) = (
            refs[: len(grads)],
            refs[len(grads) :],
        )
        unit, inverse = normalize(rows_ref[...].astype(F32))
        back, at = None, 0
        for ref in grad_refs:
            part = times_transposed(ref[...], weight_ref[:, at : at + ref.shape[1]])
            back = part if back is None else back + part
            at += ref.shape[1]
        out_ref[...] = (
            dmid_ref[...] + normalize_back(back, unit, inverse, norm_ref[0:1, :])
        ).astype(BF16)

    return row_call(
        kernel,
        "to_tokens",
        me,
        256,
        rows,
        [(g, False) for g in grads]
        + [(rows_in, False), (grad_mid, False), (norm, True), (w_qkv, True)],
        [],
        [((rows, width), BF16, False)],
        2 * rows * width * (w_qkv.shape[1] - LANES),
    )[0]


class Norm:
    def __init__(self, weight, column, sums=None, second=None):
        self.weight, self.column, self.sums, self.second = weight, column, sums, second


def rows_gradient(grid, me, lefts, rights, masks, chunk, norm=None):
    lefts = [left if isinstance(left, tuple) else (left,) for left in lefts]
    rows, width = lefts[0][0].shape[0], sum(part.shape[1] for part in lefts[0])
    columns = sum(r.shape[1] for _, r in rights)
    last = len(lefts) - 1
    emit = norm is not None and norm.second is not None
    if not grid.in_pieces(width >> grid.bits):
        parts = []
        if norm:
            column = norm.column
            gain, shift = (norm.weight[:, n - LANES : n - LANES + 1].astype(F32) for n in (0, 1))
            sums = norm.sums if norm.sums is not None else jnp.zeros((width, LANES), F32)
        for n, r in rights:
            product = contract_rows(jnp.concatenate(lefts[n], 1), r)
            if norm and n == last:
                total = jnp.sum(r.astype(F32), 0, keepdims=True)
                own = norm.weight[:, column : column + r.shape[1]].astype(F32)
                column += r.shape[1]
                both = [jnp.sum(own * t, 1, keepdims=True) for t in (product, total)]
                sums = sums + jnp.pad(jnp.concatenate(both, 1), ((0, 0), (0, LANES - 2)))
                product = gain * product + shift * total
            parts.append(product)
        if emit:
            parts.append(sums + jnp.pad(norm.second[:2].T, ((0, 0), (2, LANES - 4))))
        pieces = (jnp.concatenate(parts, 1).astype(BF16),)
        return (pieces, sums) if norm and not emit else pieces
    masks = [m for m in masks if m]
    flat = [part for left in lefts for part in left]
    steps_of = [r.shape[1] // chunk for _, r in rights]
    starts = [sum(steps_of[:n]) for n in range(len(rights))]
    steps = sum(steps_of)
    pairs = grid.dp // 2
    piece = width // grid.dp
    total = columns + (LANES if emit else 0)
    extras, extra_specs = [], []
    if norm:
        first = min(starts[n] for n, (of, _) in enumerate(rights) if of == last)
        extras = [norm.weight]
        extra_specs = [
            whole_spec(norm.weight.shape),
        ]
        for some in (norm.sums, norm.second):
            if some is not None:
                extras.append(some)
                extra_specs.append(whole_spec(some.shape))

    def kernel(me_ref, *refs):
        left_refs, refs = refs[: len(flat)], refs[len(flat) :]
        right_refs, refs = refs[: len(rights)], refs[len(rights) :]
        extra_refs, refs = refs[: len(extras)], refs[len(extras) :]
        keep_ref, away_ref, *refs = refs
        if norm:
            sums_ref, *refs = refs
            weight_ref = extra_refs[0]
        turned_refs = refs
        step = pl.program_id(0)
        device = me_ref[0]
        core = device & 1

        def put(product, at):
            for index in range(pairs):
                place = piece_of(index, device, masks)
                even = product[2 * index * piece : (2 * index + 1) * piece, :]
                odd = product[(2 * index + 1) * piece : (2 * index + 2) * piece, :]
                keep_ref[place, :, at] = jnp.where(core == 0, even, odd).astype(BF16)
                away_ref[place, :, at] = jnp.where(core == 0, odd, even).astype(BF16)

        @pl.when(step == 0)
        def _():
            n = 0
            for left, turned_ref in zip(lefts, turned_refs, strict=True):
                at = 0
                for part in left:
                    turned_ref[at : at + part.shape[1], :] = left_refs[n][...].T
                    at, n = at + part.shape[1], n + 1
            if norm:
                if norm.sums is not None:
                    sums_ref[...] = extra_refs[1][...]
                else:
                    sums_ref[...] = jnp.zeros_like(sums_ref)

        for n, ref in enumerate(right_refs):
            @pl.when((step >= starts[n]) & (step < starts[n] + steps_of[n]))
            def _(n=n, ref=ref):
                product = times(turned_refs[rights[n][0]][...], ref[...])
                if norm and rights[n][0] == last:
                    total = jnp.sum(ref[...].astype(F32), 0, keepdims=True)
                    at = pl.multiple_of(norm.column + (step - first) * chunk, LANES)
                    own = weight_ref[:, pl.ds(at, chunk)].astype(F32)
                    lane = lax.broadcasted_iota(jnp.int32, (1, LANES), 1)
                    sums_ref[...] += jnp.where(
                        lane == 0, jnp.sum(own * product, 1, keepdims=True), 0.0
                    ) + jnp.where(lane == 1, jnp.sum(own * total, 1, keepdims=True), 0.0)
                    param = weight_ref[:, -LANES:].astype(F32)
                    product = param[:, 0:1] * product + param[:, 1:2] * total
                put(product, pl.ds(pl.multiple_of(step * chunk, LANES), chunk))

        if emit:
            @pl.when(step == steps - 1)
            def _():
                second = extra_refs[-1][0:2, :]
                below = jnp.zeros((2, width), F32)
                tail = jnp.zeros((LANES - 4, width), F32)
                put(
                    sums_ref[...] + jnp.concatenate([below, second, tail], 0).T,
                    pl.ds(columns, LANES),
                )

    def right_spec(n):
        return pl.BlockSpec(
            (rows, chunk), lambda i, me: (0, jnp.clip(i - starts[n], 0, steps_of[n] - 1))
        )

    shape = (pairs, piece, total)
    sums_shape = (width, LANES)
    outs = pl.pallas_call(
        kernel,
        grid_spec=pltpu.PrefetchScalarGridSpec(
            num_scalar_prefetch=1,
            grid=(steps,),
            in_specs=[whole_spec(left.shape) for left in flat]
            + [right_spec(n) for n in range(len(rights))]
            + extra_specs,
            out_specs=[whole_spec(shape)] * 2 + [whole_spec(sums_shape)] * bool(norm),
            scratch_shapes=[pltpu.VMEM((width, rows), BF16)] * len(lefts),
        ),
        out_shape=[jax.ShapeDtypeStruct(shape, BF16)] * 2
        + [jax.ShapeDtypeStruct(sums_shape, F32)] * bool(norm),
        compiler_params=pltpu.CompilerParams(vmem_limit_bytes=VMEM_BYTES),
        cost_estimate=cost(2 * rows * width * columns, 2 * (rows * (width + columns) + width * columns)),
        name="rows_gradient",
    )(me, *flat, *[r for _, r in rights], *extras)
    if norm and not emit:
        return outs[:2], outs[2]
    return outs[:2]


def columns_gradient(grid, me, left, right, masks):
    masks = [m for m in masks if m]
    rows, wide = left.shape
    width = right.shape[1]
    piece = wide // grid.dp
    if not grid.in_pieces(wide >> grid.bits) or (2 * piece) % LANES:
        return (contract_rows(left, right).astype(BF16),)
    pairs = grid.dp // 2

    def kernel(me_ref, left_ref, right_ref, keep_ref, away_ref):
        product = contract_rows(left_ref[...], right_ref[...])
        even, odd = product[:piece, :], product[piece:, :]
        core = me_ref[0] & 1
        keep_ref[...] = jnp.where(core == 0, even, odd).astype(BF16)
        away_ref[...] = jnp.where(core == 0, odd, even).astype(BF16)

    out = pl.BlockSpec((None, piece, width), lambda i, me: (piece_of(i, me[0], masks), 0, 0))
    shape = (pairs, piece, width)
    return pl.pallas_call(
        kernel,
        grid_spec=pltpu.PrefetchScalarGridSpec(
            num_scalar_prefetch=1,
            grid=(pairs,),
            in_specs=[
                pl.BlockSpec((rows, 2 * piece), lambda i, me: (0, i)),
                whole_spec(right.shape),
            ],
            out_specs=[out] * 2,
        ),
        out_shape=[jax.ShapeDtypeStruct(shape, BF16)] * 2,
        compiler_params=pltpu.CompilerParams(vmem_limit_bytes=VMEM_BYTES),
        cost_estimate=cost(2 * rows * width * wide, 2 * (rows * (width + wide) + width * wide)),
        name="columns_gradient",
    )(me, left, right)


def body(
    grid,
    tokens,
    first_values,
    cotangent,
    lengths,
    qkv_master,
    qkv_moment,
    qkv_average,
    out_master,
    out_moment,
    out_average,
    up_master,
    up_moment,
    up_average,
    down_master,
    down_moment,
    down_average,
    norm_master,
    norm_moment,
    norm_average,
):
    count, half, width = tokens.shape
    length = 2 * half
    part = width // 2
    norm_columns = norm_master.shape[1]
    assert count == 2
    me = jnp.stack([lax.axis_index("dp"), lax.axis_index("seq")]).astype(jnp.int32)
    far, near = grid.masks[:-2], grid.masks[-2]
    back = far[::-1]
    go, end = grid.go, grid.end
    pairs = width // LANES
    half_pairs = pairs // 2

    fresh_blocks = [n * pairs + p for p in range(half_pairs) for n in range(3)]
    reused_blocks = [n * pairs + p for p in range(half_pairs, pairs) for n in range(2)]

    def blocks(array, which):
        return jnp.concatenate([array[:, n * LANES : (n + 1) * LANES] for n in which], 1)

    fresh_shard = blocks(qkv_master, fresh_blocks).astype(BF16)
    reused_shard = jnp.concatenate(
        [blocks(qkv_master, reused_blocks), jnp.pad(norm_master, ((0, 0), (0, LANES - norm_columns)))], 1
    ).astype(BF16)
    out_up_shard = jnp.concatenate([out_master, up_master], 1).astype(BF16)
    order_fresh, order_reused = [0, *far, near, 1], [0, near, *far, 1]
    order_plane = [*far, near, 1]
    fresh = Chain(grid.gather(fresh_shard, order_fresh))
    reused = Chain(grid.gather(reused_shard, order_reused))
    out_up = Chain(grid.gather_plane(out_up_shard, near))
    down = Chain(grid.gather_plane(down_master.astype(BF16), near))
    tokens_whole = Chain(grid.to_other(tokens))
    values_whole = Chain(grid.to_whole(first_values))
    cotangent_whole = Chain(grid.to_whole(cotangent))
    go(fresh, reused)
    go(tokens_whole)
    go(fresh, reused)
    go(fresh, reused)
    go(out_up)
    go(fresh, reused)
    go(values_whole)
    go(fresh, reused, now=tokens_whole.came[0])
    go(out_up)
    go(cotangent_whole, now=values_whole.came[0])
    fresh_pieces, reused_pieces, (rows_own, rows_other) = end(fresh, reused, tokens_whole)
    w_qkv = Weight(grid, width, (fresh_pieces, order_fresh), (reused_pieces, order_reused))

    projected, rows_in, unit_one, w_qkv, norm = project(me, rows_own, rows_other, w_qkv)
    now = projected
    base = 3 * half_pairs
    one = ((0, 3), (1, 3), (2, 3))
    two = ((base, 2), (base + 1, 2), (0, 1))
    projected, = go(out_up, down, now=now, inputs=(projected,))
    attended_one, totals_one = attend_forward(projected, projected, projected, one, length, half_pairs)
    now = attended_one
    (values_in,) = end(values_whole, now=now)
    values_in, = go(down, now=now, inputs=(values_in,))
    attended_two, totals_two = attend_forward(projected, projected, values_in, two, length, half_pairs)
    now = attended_two
    attended = (attended_one, attended_two)
    go(out_up, now=after(now, *down.came))
    go(out_up)
    attended_two, = go(down, now=now, inputs=(attended_two,))
    (out_up_pieces,) = end(out_up)
    w_out_up = Weight(grid, width, (out_up_pieces, order_plane))
    mid_rows, normed_two, hidden, slope = to_hidden(
        me, (attended_one, attended_two), rows_in, norm, w_out_up
    )
    now = normed_two
    hidden, = go(down, now=now, inputs=(hidden,))
    (whole_cotangent,) = end(cotangent_whole, now=now)
    own_lengths = lax.dynamic_index_in_dim(
        lengths.reshape(2, count // 2), lax.axis_index("seq"), 0, keepdims=False
    )
    position = lax.iota(jnp.int32, length)
    keep_mask = (position[None, :] < own_lengths[:, None]).reshape(-1)
    grad_mixed = jnp.where(keep_mask[:, None], whole_cotangent, jnp.zeros((), BF16))

    back_down, back_up, back_fresh = [near, *back, 0], [0, near, *back], [near, *back]
    back_reused = back_down
    grad_down = columns_gradient(grid, me, hidden, grad_mixed, back_down)
    sum_down = Chain(grid.scatter_sum(grad_down, back_down))
    now = grad_down[0]
    slope, = go(down, sum_down, now=now, inputs=(slope,))
    (down_pieces,) = end(down, now=now)
    w_down = Weight(grid, hidden.shape[1], (down_pieces, order_plane))
    grad_hidden = hidden_gradient(me, slope, grad_mixed, w_down)
    now = grad_hidden
    grad_hidden, = go(sum_down, now=now, inputs=(grad_hidden,))
    grad_up = rows_gradient(grid, me, [normed_two], [(0, grad_hidden)], back_up, 768)
    now = grad_up[0]
    sum_up = Chain(grid.scatter_sum(grad_up, back_up))
    hidden, = go(sum_up, now=now, inputs=(hidden,))
    mixed = from_hidden(me, hidden, mid_rows, w_down)
    now = mixed
    mixed_halves = Chain(grid.to_halves(mixed, half))
    grad_hidden, = go(sum_up, now=now, inputs=(grad_hidden,))
    grad_mid, grad_mid_low, grad_attended, sums_two = to_middle(
        me, grad_hidden, mid_rows, grad_mixed, norm, w_out_up
    )
    now = grad_attended

    def attend_back(which, at, many):
        values = values_in if which else projected
        return attend_backward(
            projected, projected, values, attended[which], grad_attended,
            totals_two if which else totals_one,
            (*(two if which else one), (0, 1), (which * half_pairs, 1)),
            length, at, many, not which,
        )

    grad_attended, = go(sum_down, mixed_halves, now=now, inputs=(grad_attended,))
    (grad_one,) = attend_back(0, 0, 1)
    now = grad_one
    grad_attended, = go(sum_up, now=now, inputs=(grad_attended,))
    (grad_two,) = attend_back(0, 1, 2)
    now = grad_two
    now = after(now, *mixed_halves.came)
    grad_two, = go(sum_down, sum_up, now=now, inputs=(grad_two,))
    grad_fresh, sums_one = rows_gradient(
        grid, me, [attended, unit_one], [(0, grad_mid_low), (1, grad_one), (1, grad_two)],
        back_fresh, 384, Norm(w_qkv, 0),
    )
    now = grad_fresh[0]
    sum_fresh = Chain(grid.scatter_sum_plane(grad_fresh, near))
    grad_attended, = go(sum_fresh, sum_down, sum_up, now=now, inputs=(grad_attended,))
    grad_three, value_three = attend_back(1, 0, 1)
    now = grad_three
    grad_attended, = go(sum_fresh, now=now, inputs=(grad_attended,))
    grad_four, value_four = attend_back(1, 1, 2)
    now = grad_four
    grad_four, = go(sum_fresh, now=now, inputs=(grad_four,))
    grad_reused = rows_gradient(
        grid, me, [unit_one], [(0, grad_three), (0, grad_four)], back_reused, 256,
        Norm(w_qkv, 3 * part, sums_one, sums_two),
    )
    now = grad_reused[0]
    pieces = len(grad_reused) > 1
    sum_reused = Chain(grid.scatter_sum(grad_reused, back_reused, pieces, pieces))
    first_halves = Chain(grid.to_halves(jnp.concatenate([value_three, value_four], 1), half))
    go(first_halves, now=now)
    go(sum_reused, now=now)
    grad_four, = go(sum_reused, inputs=(grad_four,))
    grad_four, = go(sum_fresh, inputs=(grad_four,))
    tokens_grad = to_tokens(
        me, [grad_one, grad_two, grad_three, grad_four], rows_in, grad_mid, norm, w_qkv
    )
    now = tokens_grad
    tokens_halves = Chain(grid.to_halves(tokens_grad, half))
    go(sum_reused, now=now)
    go(tokens_halves, sum_fresh, now=now)
    sum_up, sum_down, mixed, first_grad = end(sum_up, sum_down, mixed_halves, first_halves, now=now)
    sum_reused, sum_fresh, tokens_grad = end(sum_reused, sum_fresh, tokens_halves)
    sum_out, sum_fresh = sum_fresh[:, :width], sum_fresh[:, width:]
    qkv = (qkv_moment, qkv_master, qkv_average)
    norms = (norm_moment, norm_master, norm_average)
    layout = [(place, True, n) for n, place in enumerate(fresh_blocks)]
    layout += [(place, False, n) for n, place in enumerate(reused_blocks)]
    if pieces:
        *qkv_new, one, two, three = finish(
            *sum_reused, after(sum_fresh, tokens_grad, first_grad, mixed), qkv,
            tuple(n.T for n in norms), layout
        )
        norm_new = (one.T, two.T, three.T)
    else:
        both = {
            place: (sum_fresh if is_fresh else sum_reused)[:, n * LANES : (n + 1) * LANES]
            for place, is_fresh, n in layout
        }
        qkv_new = update(jnp.concatenate([both[n] for n in range(len(both))], 1), *qkv)
        norm_new = update(sum_reused[:, 2 * part : 2 * part + norm_columns], *norms)
    return (
        mixed,
        tokens_grad,
        first_grad,
        *qkv_new,
        *update(sum_out, out_moment, out_master, out_average),
        *update(sum_up, up_moment, up_master, up_average),
        *update(sum_down, down_moment, down_master, down_average),
        *norm_new,
    )


def solution(mesh):
    activation = P("dp", "seq", None)
    parameter = P(("dp", "seq"), None)
    return jax.shard_map(
        functools.partial(body, Grid(mesh)),
        mesh=mesh,
        in_specs=(activation,) * 3 + (P("dp"),) + (parameter,) * 15,
        out_specs=(activation,) * 3 + (parameter,) * 15,
        check_vma=False,
    )
```

```python
import functools

import jax
import jax.numpy as jnp
from jax import lax
from jax.experimental import pallas as pl
from jax.experimental.pallas import tpu as pltpu
from jax.sharding import PartitionSpec as P

HEAD_DIM = 64
LANES = 128
EPSILON = 1e-05
MOMENTUM = 0.5
AVERAGING = 0.5
RATE = 0.0006
SCALE = HEAD_DIM ** (-0.5)
VMEM_BYTES = 24 << 20

BF16 = jnp.bfloat16
F32 = jnp.float32


def cost(flops, moved):
    return pl.CostEstimate(
        flops=int(flops) // 8, bytes_accessed=int(moved) // 8, transcendentals=0
    )


def times_transposed(left, right):
    return lax.dot_general(left, right, (((1,), (1,)), ((), ())), preferred_element_type=F32)


def times(left, right):
    return lax.dot_general(left, right, (((1,), (0,)), ((), ())), preferred_element_type=F32)


def contract_rows(left, right):
    return lax.dot_general(left, right, (((0,), (0,)), ((), ())), preferred_element_type=F32)


def attend_forward_kernel(tile, q_ref, k_ref, v_ref, out_ref, totals_ref):
    length = q_ref.shape[0]
    first = lax.broadcasted_iota(jnp.int32, (1, LANES), 1) < HEAD_DIM
    row = lax.broadcasted_iota(jnp.int32, (tile, tile), 0)
    column = lax.broadcasted_iota(jnp.int32, (tile, tile), 1)
    for block in range(length // tile):
        start, stop = block * tile, (block + 1) * tile
        queries = q_ref[start:stop, :] * jnp.asarray(SCALE, BF16)
        outputs, totals = [], []
        for own in (first, ~first):
            scores = times_transposed(
                jnp.where(own, queries, jnp.zeros((), BF16)), k_ref[:stop, :]
            )
            diagonal = jnp.where(row >= column, scores[:, start:], -1e30)
            scores = (
                diagonal if block == 0 else jnp.concatenate([scores[:, :start], diagonal], 1)
            )
            maximum = jnp.max(scores, 1, keepdims=True)
            weights = jnp.exp(scores - maximum)
            summed = jnp.sum(weights, 1, keepdims=True)
            outputs.append(times(weights.astype(BF16), v_ref[:stop, :]) * (1.0 / summed))
            totals.append(maximum + jnp.log(summed))
        out_ref[start:stop, :] = jnp.where(first, outputs[0], outputs[1]).astype(BF16)
        turned = jnp.where(first, totals[0], totals[1]).T
        totals_ref[0:1, start:stop] = turned[0:1, :]
        totals_ref[1:2, start:stop] = turned[HEAD_DIM : HEAD_DIM + 1, :]


def attend_backward_kernel(
    tile, q_ref, k_ref, v_ref, out_ref, grad_ref, totals_ref, grad_refs, sum_q_ref
):
    grad_q_ref, grad_k_ref, grad_v_ref = grad_refs
    length = q_ref.shape[0]
    first = lax.broadcasted_iota(jnp.int32, (1, LANES), 1) < HEAD_DIM
    head_of_lane = lax.broadcasted_iota(jnp.int32, (8, LANES), 1) // HEAD_DIM
    pick = jnp.where(
        head_of_lane == lax.broadcasted_iota(jnp.int32, (8, LANES), 0), 1.0, 0.0
    ).astype(BF16)
    product = out_ref[...].astype(F32) * grad_ref[...].astype(F32)
    coarse = product.astype(BF16)
    fine = (product - coarse.astype(F32)).astype(BF16)
    inner = times_transposed(pick, coarse) + times_transposed(pick, fine)
    row = lax.broadcasted_iota(jnp.int32, (tile, tile), 0)
    column = lax.broadcasted_iota(jnp.int32, (tile, tile), 1)
    for start in range(0, length, tile):
        stop = start + tile
        keys = k_ref[start:stop, :] * jnp.asarray(SCALE, BF16)
        own_values = v_ref[start:stop, :]
        queries, grads = q_ref[start:, :], grad_ref[start:, :]
        grad_keys, grad_values = [], []
        for head, own in enumerate((first, ~first)):
            own_keys = jnp.where(own, keys, jnp.zeros((), BF16))
            scores = times_transposed(own_keys, queries)
            probs = jnp.exp(scores - totals_ref[head : head + 1, start:])
            diagonal = jnp.where(column >= row, probs[:, :tile], 0.0)
            probs = (
                diagonal if stop == length else jnp.concatenate([diagonal, probs[:, tile:]], 1)
            )
            grad_probs = times_transposed(
                jnp.where(own, own_values, jnp.zeros((), BF16)), grads
            )
            grad_scores = (probs * (grad_probs - inner[head : head + 1, start:])).astype(BF16)
            grad_values.append(times(probs.astype(BF16), grads))
            grad_keys.append(times(grad_scores, queries))
            part = contract_rows(grad_scores, own_keys)
            if start == 0 and head == 0:
                sum_q_ref[...] = part
            else:
                sum_q_ref[start:, :] += part
        grad_k_ref[start:stop, :] = (
            jnp.where(first, grad_keys[0], grad_keys[1]) * SCALE
        ).astype(BF16)
        grad_v_ref[start:stop, :] = jnp.where(first, grad_values[0], grad_values[1]).astype(BF16)
    grad_q_ref[...] = sum_q_ref[...].astype(BF16)


def column_spec(length, base, step=1, width=LANES):
    return pl.BlockSpec((length, width), lambda s, p: (s, base + step * p))


def attend_forward(queries, keys, values, places, length, pairs):
    rows = queries.shape[0]
    seqs = rows // length
    return pl.pallas_call(
        functools.partial(attend_forward_kernel, min(512, length)),
        grid=(seqs, pairs),
        in_specs=[column_spec(length, *place) for place in places],
        out_specs=[
            column_spec(length, 0),
            pl.BlockSpec((None, None, 2, length), lambda s, p: (s, p, 0, 0)),
        ],
        out_shape=[
            jax.ShapeDtypeStruct((rows, pairs * LANES), BF16),
            jax.ShapeDtypeStruct((seqs, pairs, 2, length), F32),
        ],
        compiler_params=pltpu.CompilerParams(vmem_limit_bytes=VMEM_BYTES),
        cost_estimate=cost(12 * rows * length * pairs * LANES, 8 * rows * pairs * LANES),
        name="attend_forward",
    )(queries, keys, values)


def attend_backward(queries, keys, values, attended, grads, totals, places, length, at, pairs, together):
    seqs = totals.shape[0]
    rows = seqs * length
    places = [(base + step * at, step) for base, step in places]
    widths = (3 * LANES,) if together else (2 * LANES, LANES)

    def kernel(*refs):
        ins, outs, sum_q_ref = refs[:6], refs[6:-1], refs[-1]
        parts = [outs[0].at[:, :LANES], outs[0].at[:, LANES : 2 * LANES]]
        parts.append(outs[0].at[:, 2 * LANES :] if together else outs[1])
        attend_backward_kernel(min(256, length), *ins, parts, sum_q_ref)

    return pl.pallas_call(
        kernel,
        grid=(seqs, pairs),
        in_specs=[column_spec(length, *place) for place in places]
        + [pl.BlockSpec((None, None, 2, length), lambda s, p: (s, at + p, 0, 0))],
        out_specs=[column_spec(length, 0, 1, w) for w in widths],
        out_shape=[jax.ShapeDtypeStruct((rows, pairs * w), BF16) for w in widths],
        scratch_shapes=[pltpu.VMEM((length, LANES), F32)],
        compiler_params=pltpu.CompilerParams(vmem_limit_bytes=VMEM_BYTES),
        cost_estimate=cost(24 * rows * length * pairs * LANES, 16 * rows * pairs * LANES),
        name="attend_backward",
    )(queries, keys, values, attended, grads, totals)


def after(array, *others):
    others = [o for o in others if o is not None]
    return lax.optimization_barrier((array, *others))[0] if others else array


class Chain:
    def __init__(self, steps):
        self.steps, self.came, self.value, self.left = steps, None, None, True

    def step(self, now):
        try:
            if self.came is None:
                return next(self.steps)
            return self.steps.send([after(c, now) for c in self.came])
        except StopIteration as stop:
            self.value, self.left = stop.value, False
            return []


class Grid:
    def __init__(self, mesh):
        self.dp, halves = mesh.shape["dp"], mesh.shape["seq"]
        assert halves == 2 and self.dp & (self.dp - 1) == 0
        self.bits = self.dp.bit_length()
        self.masks = [1 << b for b in reversed(range(self.bits - 1))]

    def go(self, *chains, now=None, inputs=()):
        moves = [(chain, chain.step(now)) for chain in chains]
        arrays = [after(array, now) for _, some in moves for array, _ in some]
        if inputs and arrays:
            tied = lax.optimization_barrier((*inputs, *arrays))
            inputs, arrays = tied[: len(inputs)], tied[len(inputs) :]
        for chain, some in moves:
            chain.came = [self.swap(arrays[n], mask) for n, (_, mask) in enumerate(some)]
            arrays = arrays[len(some) :]
        return inputs

    def swap(self, array, mask):
        if mask == 0:
            return lax.ppermute(array, "seq", [(0, 1), (1, 0)])
        return lax.ppermute(array, "dp", [(i, i ^ mask) for i in range(self.dp)])

    def end(self, *chains, now=None):
        while any(chain.left for chain in chains):
            self.go(*[chain for chain in chains if chain.left], now=now)
        return [chain.value for chain in chains]

    def bit(self, mask):
        if mask == 0:
            return lax.axis_index("seq")
        return jnp.where(lax.axis_index("dp") & mask, 1, 0)

    def in_pieces(self, rows):
        return (2 * rows) % 16 == 0

    def pair(self, held, came):
        low = self.bit(0) == 0
        return jnp.concatenate([jnp.where(low, held, came), jnp.where(low, came, held)], 1)

    def gather(self, shard, masks):
        if not self.in_pieces(shard.shape[0]):
            return (yield from self.gather_in_order(shard))
        held = shard[None]
        for mask in masks[:-1]:
            (came,) = yield [(held, mask)]
            held = jnp.concatenate([held, came], 0) if mask else self.pair(held, came)
        (came,) = yield [(held, masks[-1])]
        return held, came

    def gather_plane(self, shard, near):
        if not self.in_pieces(shard.shape[0]):
            return (yield from self.gather_in_order(shard))
        held = shard[None]
        for mask in self.masks[:-2]:
            (came,) = yield [(held, mask)]
            held = jnp.concatenate([held, came], 0)
        aside, across = yield [(held, near), (held, 0)]
        cut = held.shape[2] // 2 // LANES * LANES
        left, right = yield [(across[:, :, :cut], near), (aside[:, :, cut:], 0)]
        corner = jnp.concatenate([left, right], 2)
        held = jnp.concatenate([self.pair(held, across), self.pair(aside, corner)], 0)
        (came,) = yield [(held, 1)]
        return held, came

    def flips(self, masks):
        masks = [m for m in masks if m]
        return [
            sum(m for b, m in enumerate(masks) if j >> b & 1) for j in range(1 << len(masks))
        ]

    def gather_in_order(self, shard):
        whole = shard
        for step, mask in enumerate(self.masks + [0]):
            (came,) = yield [(whole, mask)]
            low = self.bit(mask) == 0
            whole = jnp.stack([jnp.where(low, whole, came), jnp.where(low, came, whole)], step)
        return (whole.reshape(-1, shard.shape[-1]),)

    def scatter_sum(self, pieces, masks, direct=False, unsummed=False):
        if len(pieces) == 1:
            return (yield from self.scatter_sum_in_order(pieces[0]))
        keep, away = pieces
        (came,) = yield [(away, 1)]
        for step, mask in enumerate(masks):
            count, rows, columns = keep.shape
            if direct and mask in self.masks[:-2]:
                if mask == self.masks[-3]:
                    far = [m for m in masks if m in self.masks[:-2]][::-1]
                    flips = self.flips(far)
                    moves = [(self.add(keep[j : j + 1], came[j : j + 1]), flips[j]) for j in range(1, count)]
                    keep = self.add(keep[:1], came[:1])
                    several = yield moves
                    came = sum(c.astype(F32) for c in several)
                continue
            if mask:
                parts = [(t[: count // 2], t[count // 2 :]) for t in (keep, came)]
            else:
                parts = [self.part(t) for t in (keep, came)]
            away = self.add(parts[0][1], parts[1][1])
            keep = self.add(parts[0][0], parts[1][0])
            (came,) = yield [(away, mask)]
        return (keep[0], came[0]) if unsummed else keep[0].astype(F32) + came[0].astype(F32)

    def part(self, array):
        count, rows, columns = array.shape
        split = array.reshape(count, 2, rows // 2, columns)
        seq = self.bit(0)
        return [lax.dynamic_index_in_dim(split, w, 1, keepdims=False) for w in (seq, 1 - seq)]

    def scatter_sum_plane(self, pieces, near):
        if len(pieces) == 1:
            return (yield from self.scatter_sum_in_order(pieces[0]))
        keep, away = pieces
        (came,) = yield [(away, 1)]
        half = keep.shape[0] // 2
        cut = keep.shape[2] // 2 // LANES * LANES
        (own, across), (aside, corner) = (
            [
                self.add(k, c)
                for k, c in zip(self.part(keep[at]), self.part(came[at]), strict=True)
            ]
            for at in (slice(0, half), slice(half, None))
        )
        left, right = yield [(corner[:, :, :cut], near), (corner[:, :, cut:], 0)]
        across = jnp.concatenate([self.add(across[:, :, :cut], left), across[:, :, cut:]], 2)
        aside = jnp.concatenate([aside[:, :, :cut], self.add(aside[:, :, cut:], right)], 2)
        left, right = yield [(aside, near), (across, 0)]
        total = own.astype(F32) + left.astype(F32) + right.astype(F32)
        for mask in self.masks[:-2][::-1]:
            total = total.astype(BF16)
            half = total.shape[0] // 2
            (came,) = yield [(total[half:], mask)]
            total = total[:half].astype(F32) + came.astype(F32)
        return total[0]

    def add(self, left, right):
        return (left.astype(F32) + right.astype(F32)).astype(BF16)

    def scatter_sum_in_order(self, partial):
        rows, columns = partial.shape
        order = self.masks + [0]
        whole = partial.reshape((2,) * self.bits + (rows >> self.bits, columns))
        for step in reversed(range(self.bits)):
            bit = self.bit(order[step])
            away = lax.dynamic_index_in_dim(whole, 1 - bit, step, keepdims=False)
            keep = lax.dynamic_index_in_dim(whole, bit, step, keepdims=False)
            (came,) = yield [(away, order[step])]
            whole = keep.astype(F32) + came.astype(F32)
            if step:
                whole = whole.astype(BF16)
        return whole

    def to_other(self, array):
        count, half, width = array.shape
        seq = self.bit(0)
        split = array.reshape(2, count // 2, half, width)
        keep = lax.dynamic_index_in_dim(split, seq, 0, keepdims=False)
        (came,) = yield [(lax.dynamic_index_in_dim(split, 1 - seq, 0, keepdims=False), 0)]
        return keep.reshape(-1, width), came.reshape(-1, width)

    def to_whole(self, array):
        count, half, width = array.shape
        seq = self.bit(0)
        split = array.reshape(2, count // 2, half, width)
        keep = lax.dynamic_index_in_dim(split, seq, 0, keepdims=False)
        (came,) = yield [(lax.dynamic_index_in_dim(split, 1 - seq, 0, keepdims=False), 0)]
        low = seq == 0
        return jnp.stack(
            [jnp.where(low, keep, came), jnp.where(low, came, keep)], 1
        ).reshape(count * half, width)

    def to_halves(self, array, half):
        width = array.shape[-1]
        seq = self.bit(0)
        split = array.reshape(-1, 2, half, width)
        keep = lax.dynamic_index_in_dim(split, seq, 1, keepdims=False)
        (came,) = yield [(lax.dynamic_index_in_dim(split, 1 - seq, 1, keepdims=False), 0)]
        low = seq == 0
        return jnp.concatenate([jnp.where(low, keep, came), jnp.where(low, came, keep)], 0)


class Weight:
    def __init__(self, grid, rows, *gathered):
        self.arrays, self.groups, self.columns, self.rows = [], [], 0, rows
        for arrays, order in gathered:
            flips = grid.flips(order) if len(arrays) == 2 else None
            self.arrays += arrays
            self.groups.append((flips, self.columns, arrays[0].shape[-1]))
            self.columns += arrays[0].shape[-1]

    @property
    def copies(self):
        return sum(len(flips) if flips else 1 for flips, _, _ in self.groups)

    def specs(self):
        return [pl.BlockSpec(memory_space=pl.ANY)] * len(self.arrays)

    def scratch(self):
        return [
            pltpu.VMEM((self.rows, self.columns), BF16),
            pltpu.SemaphoreType.DMA((self.copies,)),
        ]

    def loads(self, me, refs, whole, sems):
        found, at = [], 0
        for flips, start, columns in self.groups:
            if flips is None:
                found.append((refs[at], whole.at[:, start : start + columns]))
                at += 1
                continue
            half = len(flips) // 2
            rows = self.rows // len(flips)
            for j, flip in enumerate(flips):
                to = pl.multiple_of((me ^ flip) * rows, 16)
                found.append(
                    (
                        refs[at + j // half].at[j % half],
                        whole.at[pl.ds(to, rows), start : start + columns],
                    )
                )
            at += 2
        return [
            pltpu.make_async_copy(source, target, sems.at[n])
            for n, (source, target) in enumerate(found)
        ]


def piece_of(index, me, masks):
    apart = index ^ (me >> 1)
    place = 0
    for mask in masks:
        place = 2 * place + jnp.where(apart & (mask >> 1), 1, 0)
    return place


def normalize(values):
    center = values - jnp.mean(values, -1, keepdims=True)
    spread = jnp.mean(center * center, -1, keepdims=True)
    inverse = lax.rsqrt(spread + EPSILON)
    return center * inverse, inverse


def normalize_back(grad, unit, inverse, gain):
    scaled = grad * gain
    along = jnp.mean(scaled * unit, -1, keepdims=True)
    level = jnp.mean(scaled, -1, keepdims=True)
    return inverse * (scaled - level - unit * along)


GELU_A = (2.0 / 3.141592653589793) ** 0.5
GELU_B = 0.044715


def gelu_both(u):
    square = u * u
    turned = jnp.tanh(u * (GELU_A + (GELU_A * GELU_B) * square))
    half = 0.5 + 0.5 * turned
    slope = half + (0.5 * u) * (1.0 - turned * turned) * (GELU_A + (3 * GELU_A * GELU_B) * square)
    return u * half, slope


def update(gradient, moment, master, average):
    moment_new = MOMENTUM * moment + gradient
    master_new = master - RATE * (gradient + MOMENTUM * moment_new)
    average_new = AVERAGING * average + (1.0 - AVERAGING) * master_new
    return (moment_new, master_new, average_new)


def finish(keep, came, fresh, parameters, norms, layout):
    rows, columns = parameters[0].shape
    many = norms[0].shape[0]

    def kernel(keep_ref, came_ref, fresh_ref, *refs):
        ins, outs = refs[:6], refs[6:]
        for place, is_fresh, block in layout:
            at, to = slice(block * LANES, (block + 1) * LANES), slice(place * LANES, (place + 1) * LANES)
            if is_fresh:
                total = fresh_ref[:, at]
            else:
                total = keep_ref[:, at].astype(F32) + came_ref[:, at].astype(F32)
            for ref, new in zip(outs, update(total, *(r[:, to] for r in ins[:3]))):
                ref[:, to] = new
        last = slice(keep_ref.shape[1] - LANES, keep_ref.shape[1])
        total = (keep_ref[:, last].astype(F32) + came_ref[:, last].astype(F32)).T[:many, :]
        for ref, new in zip(outs[3:], update(total, *(r[...] for r in ins[3:]))):
            ref[...] = new

    return pl.pallas_call(
        kernel,
        out_shape=[jax.ShapeDtypeStruct(a.shape, F32) for a in (*parameters, *norms)],
        name="finish",
    )(keep, came, fresh, *parameters, *norms)


def row_spec(tile, width, again=0):
    return pl.BlockSpec((tile, width), lambda i, me: (i % again if again else i, 0))


def whole_spec(shape):
    return pl.BlockSpec(shape, lambda i, me: (0,) * len(shape))


def row_call(kernel, name, me, tile, rows, ins, weights, outs, flops, scratch=(), give_me=False):
    n_in, n_out = len(ins), len(outs)

    def run(me_ref, *refs):
        at = n_in
        in_refs = refs[:n_in]
        weight_refs = []
        for weight in weights:
            weight_refs.append(refs[at : at + len(weight.arrays)])
            at += len(weight.arrays)
        out_refs = refs[at : at + n_out]
        at += n_out
        held, loads = [], []
        for weight, its in zip(weights, weight_refs, strict=True):
            held.append(refs[at])
            loads.append(weight.loads(me_ref[0], its, refs[at], refs[at + 1]))
            at += 2
        step = pl.program_id(0)

        @pl.when(step == 0)
        def _():
            for some in loads:
                for load in some:
                    load.start()

        def ready(which):
            @pl.when(step == 0)
            def _():
                for load in loads[which]:
                    load.wait()

            return held[which]

        kernel(step, ready, *in_refs, *out_refs, *refs[at:], *([me_ref] if give_me else []))

    moved = sum(a.size * a.dtype.itemsize for a, _ in ins)
    moved += sum(w.rows * w.columns * 2 for w in weights)
    moved += sum(s[0] * s[1] * jnp.dtype(d).itemsize for s, d, _ in outs)
    return pl.pallas_call(
        run,
        grid_spec=pltpu.PrefetchScalarGridSpec(
            num_scalar_prefetch=1,
            grid=(rows // tile,),
            in_specs=[
                whole_spec(a.shape) if whole is True else row_spec(tile, a.shape[1], whole)
                for a, whole in ins
            ]
            + [s for w in weights for s in w.specs()],
            out_specs=[
                whole_spec(shape) if whole else row_spec(tile, shape[1])
                for shape, _, whole in outs
            ],
            scratch_shapes=[s for w in weights for s in w.scratch()] + list(scratch),
        ),
        out_shape=[jax.ShapeDtypeStruct(shape, dtype) for shape, dtype, _ in outs],
        compiler_params=pltpu.CompilerParams(vmem_limit_bytes=VMEM_BYTES),
        cost_estimate=cost(flops, moved),
        name=name,
    )(me, *[a for a, _ in ins], *[x for w in weights for x in w.arrays])


def project(me, own, other, weight):
    rows, width = 2 * own.shape[0], own.shape[1]
    columns = weight.columns - LANES
    tile = 256
    per_half = own.shape[0] // tile

    def kernel(step, ready, own_ref, other_ref, projected_ref, rows_ref, unit_ref, weight_ref, norm_ref, me_ref):
        mine = (step // per_half == me_ref[1]).astype(jnp.int32)
        now = jnp.where(mine == 1, own_ref[...], other_ref[...])
        rows_ref[...] = now
        unit, _ = normalize(now.astype(F32))
        unit_ref[...] = unit.astype(BF16)
        held = ready(0)

        @pl.when(step == 0)
        def _():
            norm_ref[...] = held[:, columns:].astype(F32).T[: norm_ref.shape[0], :]
            weight_ref[...] = held[...]

        normed = (unit * norm_ref[0:1, :] + norm_ref[1:2, :]).astype(BF16)
        projected_ref[...] = times(normed, held[:, :columns]).astype(BF16)

    return row_call(
        kernel,
        "project",
        me,
        tile,
        rows,
        [(own, per_half), (other, per_half)],
        [weight],
        [
            ((rows, columns), BF16, False),
            ((rows, width), BF16, False),
            ((rows, width), BF16, False),
            ((width, weight.columns), BF16, True),
            ((8, width), F32, True),
        ],
        2 * rows * width * columns,
        give_me=True,
    )


def to_hidden(me, attended, rows_in, norm, w_out_up):
    rows, width = rows_in.shape
    hidden = w_out_up.columns - width
    chunk = 768

    part = width // 2

    def kernel(step, ready, one_ref, two_ref, rows_ref, norm_ref, mid_ref, normed_ref, hidden_ref, slope_ref):
        held = ready(0)
        mid = rows_ref[...].astype(F32) + times(one_ref[...], held[:part, :width])
        mid = mid + times(two_ref[...], held[part:, :width])
        mid_ref[...] = mid
        unit, _ = normalize(mid)
        normed = (unit * norm_ref[2:3, :] + norm_ref[3:4, :]).astype(BF16)
        normed_ref[...] = normed
        for at in range(0, hidden, chunk):
            act, slope = gelu_both(times(normed, held[:, width + at : width + at + chunk]))
            hidden_ref[:, at : at + chunk] = act.astype(BF16)
            slope_ref[:, at : at + chunk] = slope.astype(BF16)

    return row_call(
        kernel,
        "to_hidden",
        me,
        256,
        rows,
        [(attended[0], False), (attended[1], False), (rows_in, False), (norm, True)],
        [w_out_up],
        [
            ((rows, width), F32, False),
            ((rows, width), BF16, False),
            ((rows, hidden), BF16, False),
            ((rows, hidden), BF16, False),
        ],
        2 * rows * width * (width + hidden),
    )


def from_hidden(me, hidden, mid_rows, w_down):
    rows, width = mid_rows.shape
    wide = hidden.shape[1]

    def kernel(step, ready, hidden_ref, mid_ref, mixed_ref):
        down = ready(0)
        mixed_ref[...] = (mid_ref[...] + times(hidden_ref[...], down[...])).astype(BF16)

    return row_call(
        kernel,
        "from_hidden",
        me,
        256,
        rows,
        [(hidden, False), (mid_rows, False)],
        [w_down],
        [((rows, width), BF16, False)],
        2 * rows * width * wide,
    )[0]


def hidden_gradient(me, slope, grad_mixed, w_down):
    rows, wide = slope.shape
    width = grad_mixed.shape[1]
    chunk = 768

    def kernel(step, ready, slope_ref, grad_ref, back_ref):
        down = ready(0)
        grad = grad_ref[...]
        for at in range(0, wide, chunk):
            part = times_transposed(grad, down[at : at + chunk, :])
            back_ref[:, at : at + chunk] = (
                part * slope_ref[:, at : at + chunk].astype(F32)
            ).astype(BF16)

    return row_call(
        kernel,
        "hidden_gradient",
        me,
        256,
        rows,
        [(slope, False), (grad_mixed, False)],
        [w_down],
        [((rows, wide), BF16, False)],
        2 * rows * width * wide,
    )[0]


def to_middle(me, grad_hidden, mid_rows, grad_mixed, norm, w_out_up):
    rows, width = mid_rows.shape

    def kernel(step, ready, hidden_ref, mid_ref, grad_ref, norm_ref, dmid_ref, low_ref, do_ref, sums_ref):
        unit, inverse = normalize(mid_ref[...])
        held = ready(0)
        back = times_transposed(hidden_ref[...], held[:, width:])

        @pl.when(step == 0)
        def _():
            sums_ref[...] = jnp.zeros_like(sums_ref)

        sums_ref[0:1, :] += jnp.sum(back * unit, 0, keepdims=True)
        sums_ref[1:2, :] += jnp.sum(back, 0, keepdims=True)
        dmid = grad_ref[...].astype(F32) + normalize_back(back, unit, inverse, norm_ref[2:3, :])
        dmid_ref[...] = dmid
        low = dmid.astype(BF16)
        low_ref[...] = low
        do_ref[...] = times_transposed(low, held[:, :width]).astype(BF16)

    return row_call(
        kernel,
        "to_middle",
        me,
        256,
        rows,
        [(grad_hidden, False), (mid_rows, False), (grad_mixed, False), (norm, True)],
        [w_out_up],
        [
            ((rows, width), F32, False),
            ((rows, width), BF16, False),
            ((rows, width), BF16, False),
            ((8, width), F32, True),
        ],
        2 * rows * width * (width + grad_hidden.shape[1]),
    )


def to_tokens(me, grads, rows_in, grad_mid, norm, w_qkv):
    rows, width = rows_in.shape

    def kernel(step, ready, *refs):
        grad_refs, (rows_ref, dmid_ref, norm_ref, weight_ref, out_ref) = (
            refs[: len(grads)],
            refs[len(grads) :],
        )
        unit, inverse = normalize(rows_ref[...].astype(F32))
        back, at = None, 0
        for ref in grad_refs:
            part = times_transposed(ref[...], weight_ref[:, at : at + ref.shape[1]])
            back = part if back is None else back + part
            at += ref.shape[1]
        out_ref[...] = (
            dmid_ref[...] + normalize_back(back, unit, inverse, norm_ref[0:1, :])
        ).astype(BF16)

    return row_call(
        kernel,
        "to_tokens",
        me,
        256,
        rows,
        [(g, False) for g in grads]
        + [(rows_in, False), (grad_mid, False), (norm, True), (w_qkv, True)],
        [],
        [((rows, width), BF16, False)],
        2 * rows * width * (w_qkv.shape[1] - LANES),
    )[0]


class Norm:
    def __init__(self, weight, column, sums=None, second=None):
        self.weight, self.column, self.sums, self.second = weight, column, sums, second


def rows_gradient(grid, me, lefts, rights, masks, chunk, norm=None):
    lefts = [left if isinstance(left, tuple) else (left,) for left in lefts]
    rows, width = lefts[0][0].shape[0], sum(part.shape[1] for part in lefts[0])
    columns = sum(r.shape[1] for _, r in rights)
    last = len(lefts) - 1
    emit = norm is not None and norm.second is not None
    if not grid.in_pieces(width >> grid.bits):
        parts = []
        if norm:
            column = norm.column
            gain, shift = (norm.weight[:, n - LANES : n - LANES + 1].astype(F32) for n in (0, 1))
            sums = norm.sums if norm.sums is not None else jnp.zeros((width, LANES), F32)
        for n, r in rights:
            product = contract_rows(jnp.concatenate(lefts[n], 1), r)
            if norm and n == last:
                total = jnp.sum(r.astype(F32), 0, keepdims=True)
                own = norm.weight[:, column : column + r.shape[1]].astype(F32)
                column += r.shape[1]
                both = [jnp.sum(own * t, 1, keepdims=True) for t in (product, total)]
                sums = sums + jnp.pad(jnp.concatenate(both, 1), ((0, 0), (0, LANES - 2)))
                product = gain * product + shift * total
            parts.append(product)
        if emit:
            parts.append(sums + jnp.pad(norm.second[:2].T, ((0, 0), (2, LANES - 4))))
        pieces = (jnp.concatenate(parts, 1).astype(BF16),)
        return (pieces, sums) if norm and not emit else pieces
    masks = [m for m in masks if m]
    flat = [part for left in lefts for part in left]
    steps_of = [r.shape[1] // chunk for _, r in rights]
    starts = [sum(steps_of[:n]) for n in range(len(rights))]
    steps = sum(steps_of)
    pairs = grid.dp // 2
    piece = width // grid.dp
    total = columns + (LANES if emit else 0)
    extras, extra_specs = [], []
    if norm:
        first = min(starts[n] for n, (of, _) in enumerate(rights) if of == last)
        extras = [norm.weight]
        extra_specs = [
            whole_spec(norm.weight.shape),
        ]
        for some in (norm.sums, norm.second):
            if some is not None:
                extras.append(some)
                extra_specs.append(whole_spec(some.shape))

    def kernel(me_ref, *refs):
        left_refs, refs = refs[: len(flat)], refs[len(flat) :]
        right_refs, refs = refs[: len(rights)], refs[len(rights) :]
        extra_refs, refs = refs[: len(extras)], refs[len(extras) :]
        keep_ref, away_ref, *refs = refs
        if norm:
            sums_ref, *refs = refs
            weight_ref = extra_refs[0]
        turned_refs = refs
        step = pl.program_id(0)
        device = me_ref[0]
        core = device & 1

        def put(product, at):
            for index in range(pairs):
                place = piece_of(index, device, masks)
                even = product[2 * index * piece : (2 * index + 1) * piece, :]
                odd = product[(2 * index + 1) * piece : (2 * index + 2) * piece, :]
                keep_ref[place, :, at] = jnp.where(core == 0, even, odd).astype(BF16)
                away_ref[place, :, at] = jnp.where(core == 0, odd, even).astype(BF16)

        @pl.when(step == 0)
        def _():
            n = 0
            for left, turned_ref in zip(lefts, turned_refs, strict=True):
                at = 0
                for part in left:
                    turned_ref[at : at + part.shape[1], :] = left_refs[n][...].T
                    at, n = at + part.shape[1], n + 1
            if norm:
                if norm.sums is not None:
                    sums_ref[...] = extra_refs[1][...]
                else:
                    sums_ref[...] = jnp.zeros_like(sums_ref)

        for n, ref in enumerate(right_refs):
            @pl.when((step >= starts[n]) & (step < starts[n] + steps_of[n]))
            def _(n=n, ref=ref):
                product = times(turned_refs[rights[n][0]][...], ref[...])
                if norm and rights[n][0] == last:
                    total = jnp.sum(ref[...].astype(F32), 0, keepdims=True)
                    at = pl.multiple_of(norm.column + (step - first) * chunk, LANES)
                    own = weight_ref[:, pl.ds(at, chunk)].astype(F32)
                    lane = lax.broadcasted_iota(jnp.int32, (1, LANES), 1)
                    sums_ref[...] += jnp.where(
                        lane == 0, jnp.sum(own * product, 1, keepdims=True), 0.0
                    ) + jnp.where(lane == 1, jnp.sum(own * total, 1, keepdims=True), 0.0)
                    param = weight_ref[:, -LANES:].astype(F32)
                    product = param[:, 0:1] * product + param[:, 1:2] * total
                put(product, pl.ds(pl.multiple_of(step * chunk, LANES), chunk))

        if emit:
            @pl.when(step == steps - 1)
            def _():
                second = extra_refs[-1][0:2, :]
                below = jnp.zeros((2, width), F32)
                tail = jnp.zeros((LANES - 4, width), F32)
                put(
                    sums_ref[...] + jnp.concatenate([below, second, tail], 0).T,
                    pl.ds(columns, LANES),
                )

    def right_spec(n):
        return pl.BlockSpec(
            (rows, chunk), lambda i, me: (0, jnp.clip(i - starts[n], 0, steps_of[n] - 1))
        )

    shape = (pairs, piece, total)
    sums_shape = (width, LANES)
    outs = pl.pallas_call(
        kernel,
        grid_spec=pltpu.PrefetchScalarGridSpec(
            num_scalar_prefetch=1,
            grid=(steps,),
            in_specs=[whole_spec(left.shape) for left in flat]
            + [right_spec(n) for n in range(len(rights))]
            + extra_specs,
            out_specs=[whole_spec(shape)] * 2 + [whole_spec(sums_shape)] * bool(norm),
            scratch_shapes=[pltpu.VMEM((width, rows), BF16)] * len(lefts),
        ),
        out_shape=[jax.ShapeDtypeStruct(shape, BF16)] * 2
        + [jax.ShapeDtypeStruct(sums_shape, F32)] * bool(norm),
        compiler_params=pltpu.CompilerParams(vmem_limit_bytes=VMEM_BYTES),
        cost_estimate=cost(2 * rows * width * columns, 2 * (rows * (width + columns) + width * columns)),
        name="rows_gradient",
    )(me, *flat, *[r for _, r in rights], *extras)
    if norm and not emit:
        return outs[:2], outs[2]
    return outs[:2]


def columns_gradient(grid, me, left, right, masks):
    masks = [m for m in masks if m]
    rows, wide = left.shape
    width = right.shape[1]
    piece = wide // grid.dp
    if not grid.in_pieces(wide >> grid.bits) or (2 * piece) % LANES:
        return (contract_rows(left, right).astype(BF16),)
    pairs = grid.dp // 2

    def kernel(me_ref, left_ref, right_ref, keep_ref, away_ref):
        product = contract_rows(left_ref[...], right_ref[...])
        even, odd = product[:piece, :], product[piece:, :]
        core = me_ref[0] & 1
        keep_ref[...] = jnp.where(core == 0, even, odd).astype(BF16)
        away_ref[...] = jnp.where(core == 0, odd, even).astype(BF16)

    out = pl.BlockSpec((None, piece, width), lambda i, me: (piece_of(i, me[0], masks), 0, 0))
    shape = (pairs, piece, width)
    return pl.pallas_call(
        kernel,
        grid_spec=pltpu.PrefetchScalarGridSpec(
            num_scalar_prefetch=1,
            grid=(pairs,),
            in_specs=[
                pl.BlockSpec((rows, 2 * piece), lambda i, me: (0, i)),
                whole_spec(right.shape),
            ],
            out_specs=[out] * 2,
        ),
        out_shape=[jax.ShapeDtypeStruct(shape, BF16)] * 2,
        compiler_params=pltpu.CompilerParams(vmem_limit_bytes=VMEM_BYTES),
        cost_estimate=cost(2 * rows * width * wide, 2 * (rows * (width + wide) + width * wide)),
        name="columns_gradient",
    )(me, left, right)


def body(
    grid,
    tokens,
    first_values,
    cotangent,
    lengths,
    qkv_master,
    qkv_moment,
    qkv_average,
    out_master,
    out_moment,
    out_average,
    up_master,
    up_moment,
    up_average,
    down_master,
    down_moment,
    down_average,
    norm_master,
    norm_moment,
    norm_average,
):
    count, half, width = tokens.shape
    length = 2 * half
    part = width // 2
    norm_columns = norm_master.shape[1]
    assert count == 2
    me = jnp.stack([lax.axis_index("dp"), lax.axis_index("seq")]).astype(jnp.int32)
    far, near = grid.masks[:-2], grid.masks[-2]
    back = far[::-1]
    go, end = grid.go, grid.end
    pairs = width // LANES
    half_pairs = pairs // 2

    fresh_blocks = [n * pairs + p for p in range(half_pairs) for n in range(3)]
    reused_blocks = [n * pairs + p for p in range(half_pairs, pairs) for n in range(2)]

    def blocks(array, which):
        return jnp.concatenate([array[:, n * LANES : (n + 1) * LANES] for n in which], 1)

    fresh_shard = blocks(qkv_master, fresh_blocks).astype(BF16)
    reused_shard = jnp.concatenate(
        [blocks(qkv_master, reused_blocks), jnp.pad(norm_master, ((0, 0), (0, LANES - norm_columns)))], 1
    ).astype(BF16)
    out_up_shard = jnp.concatenate([out_master, up_master], 1).astype(BF16)
    order_fresh, order_reused = [0, *far, near, 1], [0, near, *far, 1]
    order_plane = [*far, near, 1]
    fresh = Chain(grid.gather(fresh_shard, order_fresh))
    reused = Chain(grid.gather(reused_shard, order_reused))
    out_up = Chain(grid.gather_plane(out_up_shard, near))
    down = Chain(grid.gather_plane(down_master.astype(BF16), near))
    tokens_whole = Chain(grid.to_other(tokens))
    values_whole = Chain(grid.to_whole(first_values))
    cotangent_whole = Chain(grid.to_whole(cotangent))
    go(fresh, reused)
    go(tokens_whole)
    go(fresh, reused)
    go(fresh, reused)
    go(out_up)
    go(fresh, reused)
    go(values_whole)
    go(fresh, reused, now=tokens_whole.came[0])
    go(out_up)
    go(cotangent_whole, now=values_whole.came[0])
    fresh_pieces, reused_pieces, (rows_own, rows_other) = end(fresh, reused, tokens_whole)
    w_qkv = Weight(grid, width, (fresh_pieces, order_fresh), (reused_pieces, order_reused))

    projected, rows_in, unit_one, w_qkv, norm = project(me, rows_own, rows_other, w_qkv)
    now = projected
    base = 3 * half_pairs
    one = ((0, 3), (1, 3), (2, 3))
    two = ((base, 2), (base + 1, 2), (0, 1))
    projected, = go(out_up, down, now=now, inputs=(projected,))
    attended_one, totals_one = attend_forward(projected, projected, projected, one, length, half_pairs)
    now = attended_one
    (values_in,) = end(values_whole, now=now)
    values_in, = go(down, now=now, inputs=(values_in,))
    attended_two, totals_two = attend_forward(projected, projected, values_in, two, length, half_pairs)
    now = attended_two
    attended = (attended_one, attended_two)
    go(out_up, now=after(now, *down.came))
    go(out_up)
    attended_two, = go(down, now=now, inputs=(attended_two,))
    (out_up_pieces,) = end(out_up)
    w_out_up = Weight(grid, width, (out_up_pieces, order_plane))
    mid_rows, normed_two, hidden, slope = to_hidden(
        me, (attended_one, attended_two), rows_in, norm, w_out_up
    )
    now = normed_two
    hidden, = go(down, now=now, inputs=(hidden,))
    (whole_cotangent,) = end(cotangent_whole, now=now)
    own_lengths = lax.dynamic_index_in_dim(
        lengths.reshape(2, count // 2), lax.axis_index("seq"), 0, keepdims=False
    )
    position = lax.iota(jnp.int32, length)
    keep_mask = (position[None, :] < own_lengths[:, None]).reshape(-1)
    grad_mixed = jnp.where(keep_mask[:, None], whole_cotangent, jnp.zeros((), BF16))

    back_down, back_up, back_fresh = [near, *back, 0], [0, near, *back], [near, *back]
    back_reused = back_down
    grad_down = columns_gradient(grid, me, hidden, grad_mixed, back_down)
    sum_down = Chain(grid.scatter_sum(grad_down, back_down))
    now = grad_down[0]
    slope, = go(down, sum_down, now=now, inputs=(slope,))
    (down_pieces,) = end(down, now=now)
    w_down = Weight(grid, hidden.shape[1], (down_pieces, order_plane))
    grad_hidden = hidden_gradient(me, slope, grad_mixed, w_down)
    now = grad_hidden
    grad_hidden, = go(sum_down, now=now, inputs=(grad_hidden,))
    grad_up = rows_gradient(grid, me, [normed_two], [(0, grad_hidden)], back_up, 768)
    now = grad_up[0]
    sum_up = Chain(grid.scatter_sum(grad_up, back_up))
    hidden, = go(sum_up, now=now, inputs=(hidden,))
    mixed = from_hidden(me, hidden, mid_rows, w_down)
    now = mixed
    mixed_halves = Chain(grid.to_halves(mixed, half))
    grad_hidden, = go(sum_up, now=now, inputs=(grad_hidden,))
    grad_mid, grad_mid_low, grad_attended, sums_two = to_middle(
        me, grad_hidden, mid_rows, grad_mixed, norm, w_out_up
    )
    now = grad_attended

    def attend_back(which, at, many):
        values = values_in if which else projected
        return attend_backward(
            projected, projected, values, attended[which], grad_attended,
            totals_two if which else totals_one,
            (*(two if which else one), (0, 1), (which * half_pairs, 1)),
            length, at, many, not which,
        )

    grad_attended, = go(sum_down, mixed_halves, now=now, inputs=(grad_attended,))
    (grad_one,) = attend_back(0, 0, 1)
    now = grad_one
    grad_attended, = go(sum_up, now=now, inputs=(grad_attended,))
    (grad_two,) = attend_back(0, 1, 2)
    now = grad_two
    now = after(now, *mixed_halves.came)
    grad_two, = go(sum_down, sum_up, now=now, inputs=(grad_two,))
    grad_fresh, sums_one = rows_gradient(
        grid, me, [attended, unit_one], [(0, grad_mid_low), (1, grad_one), (1, grad_two)],
        back_fresh, 384, Norm(w_qkv, 0),
    )
    now = grad_fresh[0]
    sum_fresh = Chain(grid.scatter_sum_plane(grad_fresh, near))
    grad_attended, = go(sum_fresh, sum_down, sum_up, now=now, inputs=(grad_attended,))
    grad_three, value_three = attend_back(1, 0, 1)
    now = grad_three
    grad_attended, = go(sum_fresh, now=now, inputs=(grad_attended,))
    grad_four, value_four = attend_back(1, 1, 2)
    now = grad_four
    grad_four, = go(sum_fresh, now=now, inputs=(grad_four,))
    grad_reused = rows_gradient(
        grid, me, [unit_one], [(0, grad_three), (0, grad_four)], back_reused, 256,
        Norm(w_qkv, 3 * part, sums_one, sums_two),
    )
    now = grad_reused[0]
    pieces = len(grad_reused) > 1
    sum_reused = Chain(grid.scatter_sum(grad_reused, back_reused, pieces, pieces))
    first_halves = Chain(grid.to_halves(jnp.concatenate([value_three, value_four], 1), half))
    go(first_halves, now=now)
    go(sum_reused, now=now)
    grad_four, = go(sum_reused, inputs=(grad_four,))
    grad_four, = go(sum_fresh, inputs=(grad_four,))
    tokens_grad = to_tokens(
        me, [grad_one, grad_two, grad_three, grad_four], rows_in, grad_mid, norm, w_qkv
    )
    now = tokens_grad
    tokens_halves = Chain(grid.to_halves(tokens_grad, half))
    late, = go(sum_reused, now=now, inputs=(norm,))
    go(tokens_halves, sum_fresh, now=now)
    sum_up, sum_down, mixed = end(sum_up, sum_down, mixed_halves, now=now)
    (first_grad,) = end(first_halves, now=late)
    sum_reused, sum_fresh, tokens_grad = end(sum_reused, sum_fresh, tokens_halves)
    sum_out, sum_fresh = sum_fresh[:, :width], sum_fresh[:, width:]
    qkv = (qkv_moment, qkv_master, qkv_average)
    norms = (norm_moment, norm_master, norm_average)
    layout = [(place, True, n) for n, place in enumerate(fresh_blocks)]
    layout += [(place, False, n) for n, place in enumerate(reused_blocks)]
    if pieces:
        *qkv_new, one, two, three = finish(
            *sum_reused, after(sum_fresh, tokens_grad, first_grad, mixed), qkv,
            tuple(n.T for n in norms), layout
        )
        norm_new = (one.T, two.T, three.T)
    else:
        both = {
            place: (sum_fresh if is_fresh else sum_reused)[:, n * LANES : (n + 1) * LANES]
            for place, is_fresh, n in layout
        }
        qkv_new = update(jnp.concatenate([both[n] for n in range(len(both))], 1), *qkv)
        norm_new = update(sum_reused[:, 2 * part : 2 * part + norm_columns], *norms)
    return (
        mixed,
        tokens_grad,
        first_grad,
        *qkv_new,
        *update(sum_out, out_moment, out_master, out_average),
        *update(sum_up, up_moment, up_master, up_average),
        *update(sum_down, down_moment, down_master, down_average),
        *norm_new,
    )


def solution(mesh):
    activation = P("dp", "seq", None)
    parameter = P(("dp", "seq"), None)
    return jax.shard_map(
        functools.partial(body, Grid(mesh)),
        mesh=mesh,
        in_specs=(activation,) * 3 + (P("dp"),) + (parameter,) * 15,
        out_specs=(activation,) * 3 + (parameter,) * 15,
        check_vma=False,
    )
```
